32 devices in a mesh: mem: 4 (over x, core), grid: 8 (over z, y).
Axes of the slice: x: 2, y: 2, z: 4, core: 2. Of those that a mesh axis runs over, the one named last changes fastest.
Arguments:
- hidden: bfloat16 [8, 1024, 16384], P('mem', None, 'grid'), may hold values from -6 to 6
- target: float32 [100, 16384], P(None, 'grid'), may hold values from -5 to 5
- area: float32 [16384], P('grid'), may hold values from 0.2 to 2
- var_weight: float32 [100], replicated, may hold values from 0.2 to 2
- w_inner: bfloat16 [1024, 1024], replicated, may hold values from -0.1875 to 0.1875
- b_inner: float32 [1024], replicated, may hold values from -3 to 3
- w_out: bfloat16 [100, 1024], replicated, may hold values from -0.1875 to 0.1875
- b_out: float32 [100], replicated, may hold values from -3 to 3
Outputs:
- loss: float32 [], replicated
- grad_hidden: bfloat16 [8, 1024, 16384], P('mem', None, 'grid')
- grad_inner: float32 [1024, 1024], P('grid')
- grad_out: float32 [100, 1024], replicated
The draws below stay inside these ranges and needn't reach their ends.
All inputs are finite; a program needn't handle non-finite values.
Results may differ from the reference program's by a relative error of at most 0.0025.
The reference program's roundings to bfloat16 on the way (of `act`, `grad_fields` and `grad_pre`) count: a program that leaves them out, or rounds other values in their place, can miss the bound.
Values sent between devices are 32-bit elements; how exact they have to be, the bound alone decides.
No kernel may reach another device: no remote copies, remote signals or barrier semaphores. Data moves between devices by JAX's collectives and lax.ppermute only.
A program may use at most 128 MiB of HBM per device.

```python
import math
import jax
import jax.numpy as jnp

H = 1024
V = 100
MEMBERS = 8
NPOINTS = 16384


def levels(own_key, dims, split, smallest, largest):
    gain, own = 1.0, jax.random.fold_in(own_key, 6)
    for dim, parts in split:
        heights = jnp.exp(jax.random.uniform(jax.random.fold_in(own, dim), (parts,), jnp.float32, smallest / len(split), largest / len(split)))
        gain = gain * jnp.repeat(heights, dims[dim] // parts).reshape([-1 if axis == dim else 1 for axis in range(len(dims))])
    return gain


def normal_values(own_key, dims, spread, bound, cuts=(), held_as=jnp.bfloat16):
    loudness = levels(own_key, dims, cuts, -0.22, 0.18) if cuts else 1.0
    result = jax.random.normal(own_key, dims, jnp.float32) * spread * loudness
    return jnp.minimum(jnp.maximum(result, -bound), bound).astype(held_as)


def setup_inputs(seed: int = 0) -> dict:
    key_list = jax.random.split(jax.random.key(seed), 9)
    return {
        "hidden": normal_values(key_list[0], (MEMBERS, H, NPOINTS), 1.0, 6.0, ((0, 4), (2, 8))),
        "target": normal_values(key_list[1], (V, NPOINTS), 0.7, 5.0, ((1, 8),), jnp.float32),
        "area": jnp.clip(jnp.exp(math.log(2.0) - 2.3025851 * jax.random.uniform(key_list[2], (NPOINTS,), jnp.float32) ** levels(key_list[2], (NPOINTS,), ((0, 8),), -0.2, 0.2)), 0.2, 2.0),
        "var_weight": jnp.clip(jnp.exp(jax.random.uniform(key_list[3], (V,), jnp.float32, math.log(0.2), math.log(2.0))), 0.2, 2.0),
        "w_inner": normal_values(key_list[4], (H, H), H ** -0.5, 0.1875),
        "b_inner": normal_values(key_list[5], (H,), 0.5, 3.0, (), jnp.float32),
        "w_out": normal_values(key_list[6], (V, H), H ** -0.5, 0.1875),
        "b_out": normal_values(key_list[7], (V,), 0.5, 3.0, (), jnp.float32),
    }


def smooth(d):
    return jnp.sqrt(d * d + 0.0004) - 0.02

def slope(d):
    return d / jnp.sqrt(d * d + 0.0004)

def reference(hidden, target, area, var_weight, w_inner, b_inner, w_out, b_out):
    members = hidden.shape[0]
    npoints = hidden.shape[2]
    weight = var_weight[:, None] * area[None, :]
    fields = []
    for m in range(members):
        pre = jnp.dot(w_inner, hidden[m], preferred_element_type=jnp.float32) + b_inner[:, None]
        act = jax.nn.gelu(pre).astype(jnp.bfloat16)
        fields.append(jnp.dot(w_out, act, preferred_element_type=jnp.float32) + b_out[:, None])
    denom = members * (members - 1)
    obs_sum = jnp.zeros_like(target)
    pair_sum = jnp.zeros_like(target)
    dsum = [jnp.zeros_like(target) for m in range(members)]
    for i in range(members):
        obs_sum = obs_sum + smooth(fields[i] - target)
        for j in range(i + 1, members):
            diff = fields[i] - fields[j]
            pair_sum = pair_sum + smooth(diff)
            sl = slope(diff)
            dsum[i] = dsum[i] + sl
            dsum[j] = dsum[j] - sl
    total = jnp.sum(weight * (obs_sum / members - pair_sum / denom))
    loss = total / npoints
    scale = 1.0 / jnp.sqrt(jnp.float32(members * npoints))
    grad_inner = jnp.zeros((w_inner.shape[0], w_inner.shape[1]), jnp.float32)
    grad_out = jnp.zeros((w_out.shape[0], w_out.shape[1]), jnp.float32)
    grads = []
    for m in range(members):
        pre = jnp.dot(w_inner, hidden[m], preferred_element_type=jnp.float32) + b_inner[:, None]
        act = jax.nn.gelu(pre).astype(jnp.bfloat16)
        grad_fields = (weight * (slope(fields[m] - target) / members - dsum[m] / denom)).astype(jnp.bfloat16)
        grad_act = jnp.dot(w_out.T, grad_fields, preferred_element_type=jnp.float32)
        back_fn = jax.vjp(jax.nn.gelu, pre)[1]
        grad_pre = back_fn(grad_act)[0].astype(jnp.bfloat16)
        grads.append(jnp.dot(w_inner.T, grad_pre, preferred_element_type=jnp.float32).astype(jnp.bfloat16))
        grad_inner = grad_inner + jnp.dot(grad_pre, hidden[m].T, preferred_element_type=jnp.float32)
        grad_out = grad_out + jnp.dot(grad_fields, act.T, preferred_element_type=jnp.float32)
    return (loss, jnp.stack(grads), grad_inner * scale, grad_out * scale)
```

```python
import functools
import math

import jax
import jax.numpy as jnp
from jax import lax
from jax.experimental import pallas as pl
from jax.experimental.pallas import tpu as pltpu
from jax.sharding import PartitionSpec as P

PARTS = 4
FWD_TILE = 256
BWD_TILE = 256
EPS = 0.0004
K0 = math.sqrt(2.0 / math.pi)
K1 = K0 * 0.044715
VMEM = 56 * 1024 * 1024
NT = (((1,), (1,)), ((), ()))


def column(row, size):
    r = lax.broadcasted_iota(jnp.int32, (size, size), 0)
    c = lax.broadcasted_iota(jnp.int32, (size, size), 1)
    return jnp.sum(jnp.where(r == c, row, 0.0), axis=1, keepdims=True)


def forward_kernel(hid_ref, w_ref, b_ref, wo_ref, bo_ref, act_ref, slope_ref, f_ref, bias):
    @pl.when(pl.program_id(0) == 0)
    def _():
        for k in range(bias.shape[0] // 128):
            bias[pl.ds(k * 128, 128), :] = jnp.broadcast_to(
                column(b_ref[:, pl.ds(k * 128, 128)], 128), (128, 128)
            )

    out_bias = column(bo_ref[...], bo_ref.shape[1])
    for s in range(hid_ref.shape[2] // FWD_TILE):
        cols = pl.ds(s * FWD_TILE, FWD_TILE)
        b = jnp.concatenate([bias[...]] * (FWD_TILE // 128), axis=1)
        x = jnp.dot(w_ref[...], hid_ref[0, :, cols], preferred_element_type=jnp.float32) + b
        x2 = x * x
        u = 0.5 + 0.5 * jnp.tanh(x * (K0 + K1 * x2))
        act = (x * u).astype(jnp.bfloat16)
        act_ref[0, :, cols] = act
        slope_ref[0, :, cols] = u + (u - u * u) * (x * (2.0 * K0 + 6.0 * K1 * x2))
        f_ref[0, :, cols] = (
            jnp.dot(wo_ref[...], act, preferred_element_type=jnp.float32) + out_bias
        )


def forward(part, hidden, w_inner, b_inner, w_out, b_out):
    mloc, h, n = hidden.shape
    v = w_out.shape[0]
    p = n // PARTS
    whole = lambda m: (0, 0)
    once = pl.Buffered(1)
    return pl.pallas_call(
        forward_kernel,
        grid=(mloc,),
        in_specs=[
            pl.BlockSpec((1, h, p), lambda m: (m, 0, part)),
            pl.BlockSpec((h, h), whole, pipeline_mode=once),
            pl.BlockSpec((1, h), whole, pipeline_mode=once),
            pl.BlockSpec((v, h), whole, pipeline_mode=once),
            pl.BlockSpec((1, v), whole, pipeline_mode=once),
        ],
        out_specs=[
            pl.BlockSpec((1, h, p), lambda m: (m, 0, 0)),
            pl.BlockSpec((1, h, p), lambda m: (m, 0, 0)),
            pl.BlockSpec((1, v, p), lambda m: (m, 0, 0)),
        ],
        out_shape=[
            jax.ShapeDtypeStruct((mloc, h, p), jnp.bfloat16),
            jax.ShapeDtypeStruct((mloc, h, p), jnp.float32),
            jax.ShapeDtypeStruct((mloc, v, p), jnp.float32),
        ],
        scratch_shapes=[pltpu.VMEM((h, 128), jnp.float32)],
        compiler_params=pltpu.CompilerParams(vmem_limit_bytes=VMEM),
        cost_estimate=pl.CostEstimate(
            flops=2 * mloc * p * h * (h + v), bytes_accessed=mloc * p * h * 8 + 2 * h * h,
            transcendentals=mloc * p * h,
        ),
        name="forward_part",
    )(hidden, w_inner, b_inner, w_out, b_out)


def backward_kernel(
    first, last, dims, members,
    f_ref, fc_ref, fx_ref, fxc_ref, target_ref, area_ref, vw_ref, act_ref, slope_ref, hid_ref,
    wot_ref, wt_ref, acc_in, extra_in, gh_in, gh_ref, extra_ref, *refs,
):
    if last:
        keep_a, send_a, keep_x, send_x, acc, gf = refs
    else:
        acc, gf = refs
    step = pl.program_id(0)
    mloc, v, t = f_ref.shape
    h = wt_ref.shape[0]
    denom = members * (members - 1)
    vw = column(vw_ref[...], v)
    area = area_ref[...]
    loss = jnp.zeros((1, t), jnp.float32)
    for r0 in range(0, v, 16):
        rows = pl.ds(r0, min(16, v - r0))
        own = [f_ref[m, rows, :] for m in range(mloc)]
        others = [ref[m, rows, :] for ref in (fc_ref, fx_ref, fxc_ref) for m in range(mloc)]
        target = target_ref[rows, :]
        dsum = [None] * mloc
        obs = []
        cross = jnp.zeros_like(target)
        inner = jnp.zeros_like(target)
        near = jnp.zeros_like(target)
        n_cross = n_inner = 0

        def pair(a, b):
            d = a - b
            s = d * d + EPS
            r = lax.rsqrt(s)
            return d * r, s * r

        def add(m, value):
            dsum[m] = value if dsum[m] is None else dsum[m] + value

        for i in range(mloc):
            sl, ph = pair(own[i], target)
            obs.append(sl)
            near = near + ph
            for b in others:
                sl, ph = pair(own[i], b)
                add(i, sl)
                cross = cross + ph
                n_cross += 1
            for j in range(i + 1, mloc):
                sl, ph = pair(own[i], own[j])
                add(i, sl)
                add(j, -sl)
                inner = inner + ph
                n_inner += 1
        weight = vw[r0 : r0 + 16] * area
        for m in range(mloc):
            gf[m, rows, :] = weight * (obs[m] * (1.0 / members) - dsum[m] * (1.0 / denom))
        near = (near - 0.02 * mloc) * (1.0 / members)
        pairs = (inner - 0.02 * n_inner) + 0.5 * (cross - 0.02 * n_cross)
        loss = loss + jnp.sum(weight * (near - pairs * (1.0 / denom)), axis=0, keepdims=True)
    for m in range(mloc):
        gf[m, pl.ds(v, gf.shape[1] - v), :] = jnp.zeros((gf.shape[1] - v, t), jnp.float32)

    gp = []
    extra = None
    for m in range(mloc):
        g = gf[m].astype(jnp.bfloat16)
        ga = jnp.dot(wot_ref[...], g, preferred_element_type=jnp.float32)
        gp.append((ga * slope_ref[m]).astype(jnp.bfloat16))
        out = lax.dot_general(g, act_ref[m], NT, preferred_element_type=jnp.float32)
        extra = out if extra is None else extra + out
    gpc = jnp.concatenate(gp, axis=1)
    hidc = jnp.concatenate([hid_ref[m] for m in range(mloc)], axis=1)
    prod = lax.dot_general(gpc, hidc, NT, preferred_element_type=jnp.float32)

    @pl.when(step == 0)
    def _():
        if first:
            acc[...] = prod
            extra_ref[...] = extra
        else:
            acc[...] = acc_in[...] + prod
            extra_ref[...] = extra_in[...] + extra

    @pl.when(step > 0)
    def _():
        acc[...] += prod
        extra_ref[...] += extra

    extra_ref[pl.ds(v, 1), pl.ds(0, t)] += loss
    for m in range(mloc):
        gh_ref[m] = jnp.dot(wt_ref[...], gp[m], preferred_element_type=jnp.float32).astype(
            jnp.bfloat16
        )
    if last:
        n_hi, n_lo = dims

        @pl.when(step == pl.num_programs(0) - 1)
        def _():
            mem = lax.axis_index("mem")
            grid = lax.axis_index("grid")
            x, core = mem // 2, mem % 2
            hi, lo = grid // n_lo, grid % n_lo
            r = h // (2 * n_hi * n_lo)
            ca = keep_a.shape[3]
            cx = keep_x.shape[4]
            for dlo in range(n_lo):
                for dhi in range(n_hi):
                    g = lax.rem(hi + dhi, n_hi) * n_lo + lax.rem(lo + dlo, n_lo)
                    for c, part_a, part_x in ((core, keep_a, keep_x), (1 - core, send_a, send_x)):
                        r0 = pl.multiple_of((g * 2 + c) * r, r)
                        part_a[dlo, dhi] = acc[pl.ds(r0, r), pl.ds(0, ca)]
                        left = acc[pl.ds(r0, r), pl.ds(ca, cx)]
                        right = acc[pl.ds(r0, r), pl.ds(ca + cx, cx)]
                        part_x[0, dlo, dhi] = jnp.where(x == 0, left, right)
                        part_x[1, dlo, dhi] = jnp.where(x == 0, right, left)


def backward(part, dims, members, fields, rest, acc, extra, gh):
    target, area, vw, act, slope, hidden, wot, wt = rest
    mloc, h, n = hidden.shape
    v = target.shape[0]
    vp = wot.shape[1]
    p = n // PARTS
    t = BWD_TILE
    steps = p // t
    first, last = part == 0, part == PARTS - 1
    off = part * steps
    once = pl.Buffered(1)
    f_spec = pl.BlockSpec((mloc, v, t), lambda s: (0, 0, s))
    big = pl.BlockSpec((mloc, h, t), lambda s: (0, 0, s))
    whole = lambda s: (0, 0)
    const = lambda a: pl.BlockSpec(a.shape, whole, pipeline_mode=once)
    anyspec = pl.BlockSpec(memory_space=pl.ANY)
    placed = pl.BlockSpec((mloc, h, t), lambda s: (0, 0, off + s))
    in_specs = [f_spec] * 4 + [
        pl.BlockSpec((v, t), lambda s: (0, off + s)),
        pl.BlockSpec((1, t), lambda s: (0, off + s)),
        const(vw), big, big, placed, const(wot), const(wt),
    ]
    args = [*fields, target, area, vw, act, slope, hidden, wot, wt]
    kernel = functools.partial(backward_kernel, first, last, dims, members)
    if first:
        kernel_fn = lambda *refs: kernel(*refs[:12], None, None, None, *refs[12:])
        aliases = {}
    else:
        kernel_fn = kernel
        in_specs += [const(acc), const(extra), anyspec]
        args += [acc, extra, gh]
        aliases = {14: 0}
    out_specs = [placed, pl.BlockSpec((vp, h), whole)]
    out_shape = [
        jax.ShapeDtypeStruct(hidden.shape, jnp.bfloat16),
        jax.ShapeDtypeStruct((vp, h), jnp.float32),
    ]
    scratch = [pltpu.VMEM((mloc, vp, t), jnp.float32)]
    if last:
        n_hi, n_lo = dims
        r = h // (2 * n_hi * n_lo)
        ca = h // 2
        cx = (h - ca) // 2
        for shape in ((n_lo, n_hi, r, ca), (n_lo, n_hi, r, ca), (2, n_lo, n_hi, r, cx), (2, n_lo, n_hi, r, cx)):
            out_specs.append(pl.BlockSpec(shape, lambda s, k=len(shape): (0,) * k))
            out_shape.append(jax.ShapeDtypeStruct(shape, jnp.float32))
        scratch = [pltpu.VMEM((h, h), jnp.float32)] + scratch
    else:
        out_specs.append(pl.BlockSpec((h, h), whole))
        out_shape.append(jax.ShapeDtypeStruct((h, h), jnp.float32))
    return pl.pallas_call(
        kernel_fn,
        grid=(steps,),
        in_specs=in_specs,
        out_specs=out_specs,
        out_shape=out_shape,
        scratch_shapes=scratch,
        input_output_aliases=aliases,
        compiler_params=pltpu.CompilerParams(vmem_limit_bytes=VMEM),
        cost_estimate=pl.CostEstimate(
            flops=4 * mloc * p * h * (h + v), bytes_accessed=mloc * p * h * 10 + 10 * h * h,
            transcendentals=mloc * p * v * 8,
        ),
        name="backward_part",
    )(*args)


def shards(hidden, target, area, var_weight, w_inner, b_inner, w_out, b_out):
    mloc, h, n = hidden.shape
    n_mem = lax.axis_size("mem")
    n_grid = lax.axis_size("grid")
    members = mloc * n_mem
    npoints = n * n_grid
    v = w_out.shape[0]
    vp = 128
    n_lo = 2
    while n_lo * n_lo * 4 <= n_grid:
        n_lo *= 2
    n_hi = n_grid // n_lo

    swap_x = [(i, (i + n_mem // 2) % n_mem) for i in range(n_mem)]
    swap_core = [(i, i ^ 1) for i in range(n_mem)]

    def shift_lo(k):
        return [(a * n_lo + b, a * n_lo + (b + k) % n_lo) for a in range(n_hi) for b in range(n_lo)]

    def shift_hi(k):
        return [(a * n_lo + b, (a + k) % n_hi * n_lo + b) for a in range(n_hi) for b in range(n_lo)]

    to_x = lambda a: lax.ppermute(a, "mem", swap_x)
    to_core = lambda a: lax.ppermute(a, "mem", swap_core)
    to_lo = lambda a, k: lax.ppermute(a, "grid", shift_lo(k))
    to_hi = lambda a, k: lax.ppermute(a, "grid", shift_hi(k))

    parts = []
    for part in range(PARTS):
        parts.append(
            forward(part, hidden, w_inner, b_inner.reshape(1, h), w_out, b_out.reshape(1, v))
        )
    exchanged = []
    for act, slope, fields in parts:
        far = to_x(fields)
        exchanged.append((fields, to_core(fields), far, to_core(far)))

    w_inner, w_out, _ = lax.optimization_barrier((w_inner, w_out, parts[1][2]))
    wt = w_inner.T
    wot = jnp.pad(w_out, ((0, vp - v), (0, 0))).T
    vw, area = var_weight.reshape(1, v), area.reshape(1, n)
    acc = extra = gh = None
    for part in range(PARTS):
        act, slope, _ = parts[part]
        rest = (target, area, vw, act, slope, hidden, wot, wt)
        gh, extra, *accs = backward(
            part, (n_hi, n_lo), members, exchanged[part], rest, acc, extra, gh
        )
        acc = accs[0]
    keep_a, send_a, keep_x, send_x = accs

    core = lax.axis_index("mem") % 2
    x = lax.axis_index("mem") // 2

    def along_lo(blocks):
        total = blocks(0)
        for k in range(1, n_lo):
            total = total + to_lo(blocks(k), k)
        return total

    def along_hi(blocks):
        total = blocks[0]
        for k in range(1, n_hi):
            total = total + to_hi(blocks[k], k)
        return total

    got_a = to_core(send_a)
    got_x = to_core(send_x)
    sum_a = along_lo(lambda k: keep_a[k] + got_a[k])
    own_x = keep_x[0] + got_x[0] + to_x(keep_x[1] + got_x[1])
    sum_x = along_lo(lambda k: own_x[k])
    end_a = along_hi(sum_a)
    end_x = along_hi(sum_x)
    end_a = end_a + to_x(end_a)
    far_x = to_x(end_x)
    end_x = jnp.where(
        x == 0, jnp.concatenate([end_x, far_x], 1), jnp.concatenate([far_x, end_x], 1)
    )
    scale = 1.0 / math.sqrt(members * npoints)
    mine = jnp.concatenate([end_a, end_x], 1) * scale
    other = to_core(mine)
    grad_inner = jnp.where(
        core == 0, jnp.concatenate([mine, other], 0), jnp.concatenate([other, mine], 0)
    )
    extra = lax.psum(extra, ("mem", "grid"))
    loss = jnp.sum(extra[v]) / npoints
    return (loss, gh, grad_inner, extra[:v] * scale)


def solution(mesh):
    in_specs = (P("mem", None, "grid"), P(None, "grid"), P("grid"), P(), P(), P(), P(), P())
    out_specs = (P(), P("mem", None, "grid"), P("grid", None), P())
    return jax.shard_map(shards, mesh=mesh, in_specs=in_specs, out_specs=out_specs, check_vma=False)
```

```python
import functools
import math

import jax
import jax.numpy as jnp
from jax import lax
from jax.experimental import pallas as pl
from jax.experimental.pallas import tpu as pltpu
from jax.sharding import PartitionSpec as P

PARTS = 4
FWD_TILE = 256
BWD_TILE = 256
EPS = 0.0004
K0 = math.sqrt(2.0 / math.pi)
K1 = K0 * 0.044715
SLAB = 256
FWD_VMEM = 20 * 1024 * 1024
BWD_VMEM = 34 * 1024 * 1024
NT = (((1,), (1,)), ((), ()))


def column(row, size):
    r = lax.broadcasted_iota(jnp.int32, (size, size), 0)
    c = lax.broadcasted_iota(jnp.int32, (size, size), 1)
    return jnp.sum(jnp.where(r == c, row, 0.0), axis=1, keepdims=True)


def forward_kernel(tiles, hid_ref, w_ref, b_ref, wo_ref, bo_ref, act_ref, slope_ref, f_ref, bias, even, odd):
    step = pl.program_id(0)

    @pl.when(step == 0)
    def _():
        for k in range(bias.shape[0] // 128):
            bias[pl.ds(k * 128, 128), :] = jnp.broadcast_to(
                column(b_ref[:, pl.ds(k * 128, 128)], 128), (128, 128)
            )

    def both(fill, drain):
        h, t = fill.shape
        fill[...] = jnp.dot(w_ref[...], hid_ref[0], preferred_element_type=jnp.float32)
        out = jnp.broadcast_to(column(bo_ref[...], bo_ref.shape[1]), f_ref.shape[1:])
        for k in range(0, h, SLAB):
            for r in range(k, k + SLAB, 16):
                rows = pl.ds(r, 16)
                b = jnp.concatenate([bias[rows, :]] * (t // 128), axis=1)
                x = drain[rows, :] + b
                q = x * x * K1
                th = jnp.tanh(x * (K0 + q))
                up = 1.0 + th
                act_ref[0, rows, :] = (x * up).astype(jnp.bfloat16)
                slope_ref[0, rows, :] = up * (1.0 + (1.0 - th) * (x * (K0 + 3.0 * q)))
            slab = pl.ds(k, SLAB)
            out = out + jnp.dot(
                wo_ref[:, slab], act_ref[0, slab, :], preferred_element_type=jnp.float32
            )
        f_ref[0] = out

    @pl.when(step % 2 == 0)
    def _():
        both(even, odd)

    @pl.when(step % 2 == 1)
    def _():
        both(odd, even)


def forward(part, hidden, w_inner, b_inner, w_out, b_out):
    mloc, h, n = hidden.shape
    v = w_out.shape[0]
    p = n // PARTS
    t = FWD_TILE
    per = p // t
    tiles = mloc * per
    whole = lambda s: (0, 0)
    once = pl.Buffered(1)

    def ahead(s):
        s = jnp.minimum(s, tiles - 1)
        return (s // per, 0, part * per + s % per)

    def behind(s):
        s = jnp.maximum(s - 1, 0)
        return (s // per, 0, s % per)

    return pl.pallas_call(
        functools.partial(forward_kernel, tiles),
        grid=(tiles + 1,),
        in_specs=[
            pl.BlockSpec((1, h, t), ahead),
            pl.BlockSpec((h, h), whole, pipeline_mode=once),
            pl.BlockSpec((1, h), whole, pipeline_mode=once),
            pl.BlockSpec((v, h), whole, pipeline_mode=once),
            pl.BlockSpec((1, v), whole, pipeline_mode=once),
        ],
        out_specs=[
            pl.BlockSpec((1, h, t), behind),
            pl.BlockSpec((1, h, t), behind),
            pl.BlockSpec((1, v, t), behind),
        ],
        out_shape=[
            jax.ShapeDtypeStruct((mloc, h, p), jnp.bfloat16),
            jax.ShapeDtypeStruct((mloc, h, p), jnp.float32),
            jax.ShapeDtypeStruct((mloc, v, p), jnp.float32),
        ],
        scratch_shapes=[
            pltpu.VMEM((h, 128), jnp.float32),
            pltpu.VMEM((h, t), jnp.float32),
            pltpu.VMEM((h, t), jnp.float32),
        ],
        compiler_params=pltpu.CompilerParams(vmem_limit_bytes=FWD_VMEM),
        cost_estimate=pl.CostEstimate(
            flops=2 * mloc * p * h * (h + v), bytes_accessed=mloc * p * h * 8 + 2 * h * h,
            transcendentals=mloc * p * h,
        ),
        name="forward_part",
    )(hidden, w_inner, b_inner, w_out, b_out)


def backward_kernel(
    first, last, dims, members,
    f_ref, fc_ref, fx_ref, fxc_ref, target_ref, area_ref, vw_ref, act_ref, slope_ref, hid_ref,
    wot_ref, wt_ref, acc_in, extra_in, gh_in, gh_ref, extra_ref, *refs,
):
    if last:
        keep_a, send_a, keep_x, send_x, acc, gf, gp = refs
    else:
        acc, gf, gp = refs
    step = pl.program_id(0)
    mloc, v, t = f_ref.shape
    h = wt_ref.shape[0]
    denom = members * (members - 1)
    vw = column(vw_ref[...], v)
    area = area_ref[...]
    loss = jnp.zeros((1, t), jnp.float32)
    for r0 in range(0, v, 16):
        rows = pl.ds(r0, min(16, v - r0))
        own = [f_ref[m, rows, :] for m in range(mloc)]
        others = [ref[m, rows, :] for ref in (fc_ref, fx_ref, fxc_ref) for m in range(mloc)]
        target = target_ref[rows, :]
        dsum = [None] * mloc
        obs = []
        cross = jnp.zeros_like(target)
        inner = jnp.zeros_like(target)
        near = jnp.zeros_like(target)
        n_cross = n_inner = 0

        def pair(a, b):
            d = a - b
            s = d * d + EPS
            r = lax.rsqrt(s)
            return d * r, s * r

        def add(m, value):
            dsum[m] = value if dsum[m] is None else dsum[m] + value

        for i in range(mloc):
            sl, ph = pair(own[i], target)
            obs.append(sl)
            near = near + ph
            for b in others:
                sl, ph = pair(own[i], b)
                add(i, sl)
                cross = cross + ph
                n_cross += 1
            for j in range(i + 1, mloc):
                sl, ph = pair(own[i], own[j])
                add(i, sl)
                add(j, -sl)
                inner = inner + ph
                n_inner += 1
        weight = vw[r0 : r0 + 16] * area
        for m in range(mloc):
            gf[m, rows, :] = weight * (obs[m] * (1.0 / members) - dsum[m] * (1.0 / denom))
        near = (near - 0.02 * mloc) * (1.0 / members)
        pairs = (inner - 0.02 * n_inner) + 0.5 * (cross - 0.02 * n_cross)
        loss = loss + jnp.sum(weight * (near - pairs * (1.0 / denom)), axis=0, keepdims=True)
    for m in range(mloc):
        gf[m, pl.ds(v, gf.shape[1] - v), :] = jnp.zeros((gf.shape[1] - v, t), jnp.float32)

    g = jnp.concatenate([gf[m] for m in range(mloc)], axis=1).astype(jnp.bfloat16)
    for k in range(0, h, SLAB):
        rows = pl.ds(k, SLAB)
        ga = jnp.dot(wot_ref[rows, :], g, preferred_element_type=jnp.float32)
        slope = jnp.concatenate([slope_ref[m, rows, :] for m in range(mloc)], axis=1)
        gp[rows, :] = (ga * slope).astype(jnp.bfloat16)
    hid = jnp.concatenate([hid_ref[m] for m in range(mloc)], axis=1)
    act = jnp.concatenate([act_ref[m] for m in range(mloc)], axis=1)
    extra = lax.dot_general(g, act, NT, preferred_element_type=jnp.float32)

    def accumulate(base, extra_base):
        extra_ref[...] = extra if extra_base is None else extra_base[...] + extra
        for k in range(0, h, SLAB):
            rows = pl.ds(k, SLAB)
            prod = lax.dot_general(gp[rows, :], hid, NT, preferred_element_type=jnp.float32)
            acc[rows, :] = prod if base is None else base[rows, :] + prod

    @pl.when(step == 0)
    def _():
        accumulate(acc_in, extra_in)

    @pl.when(step > 0)
    def _():
        accumulate(acc, extra_ref)

    extra_ref[pl.ds(v, 1), pl.ds(0, t)] += loss
    for k in range(0, h, SLAB):
        rows = pl.ds(k, SLAB)
        out = jnp.dot(wt_ref[rows, :], gp[...], preferred_element_type=jnp.float32)
        for m in range(mloc):
            gh_ref[m, rows, :] = out[:, m * t : (m + 1) * t].astype(jnp.bfloat16)
    if last:
        n_hi, n_lo = dims

        @pl.when(step == pl.num_programs(0) - 1)
        def _():
            mem = lax.axis_index("mem")
            grid = lax.axis_index("grid")
            x, core = mem // 2, mem % 2
            hi, lo = grid // n_lo, grid % n_lo
            r = h // (2 * n_hi * n_lo)
            ca = keep_a.shape[3]
            cx = keep_x.shape[4]
            for dlo in range(n_lo):
                for dhi in range(n_hi):
                    g = lax.rem(hi + dhi, n_hi) * n_lo + lax.rem(lo + dlo, n_lo)
                    for c, part_a, part_x in ((core, keep_a, keep_x), (1 - core, send_a, send_x)):
                        r0 = pl.multiple_of((g * 2 + c) * r, r)
                        part_a[dlo, dhi] = acc[pl.ds(r0, r), pl.ds(0, ca)]
                        left = acc[pl.ds(r0, r), pl.ds(ca, cx)]
                        right = acc[pl.ds(r0, r), pl.ds(ca + cx, cx)]
                        part_x[0, dlo, dhi] = jnp.where(x == 0, left, right)
                        part_x[1, dlo, dhi] = jnp.where(x == 0, right, left)


def backward(part, dims, members, fields, rest, acc, extra, gh):
    target, area, vw, act, slope, hidden, wot, wt = rest
    mloc, h, n = hidden.shape
    v = target.shape[0]
    vp = wot.shape[1]
    p = n // PARTS
    t = BWD_TILE
    steps = p // t
    first, last = part == 0, part == PARTS - 1
    off = part * steps
    once = pl.Buffered(1)
    f_spec = pl.BlockSpec((mloc, v, t), lambda s: (0, 0, s))
    big = pl.BlockSpec((mloc, h, t), lambda s: (0, 0, s))
    whole = lambda s: (0, 0)
    const = lambda a: pl.BlockSpec(a.shape, whole, pipeline_mode=once)
    anyspec = pl.BlockSpec(memory_space=pl.ANY)
    placed = pl.BlockSpec((mloc, h, t), lambda s: (0, 0, off + s))
    in_specs = [f_spec] * 4 + [
        pl.BlockSpec((v, t), lambda s: (0, off + s)),
        pl.BlockSpec((1, t), lambda s: (0, off + s)),
        const(vw), big, big, placed, const(wot), const(wt),
    ]
    args = [*fields, target, area, vw, act, slope, hidden, wot, wt]
    kernel = functools.partial(backward_kernel, first, last, dims, members)
    if first:
        kernel_fn = lambda *refs: kernel(*refs[:12], None, None, None, *refs[12:])
        aliases = {}
    else:
        kernel_fn = kernel
        in_specs += [const(acc), const(extra), anyspec]
        args += [acc, extra, gh]
        aliases = {14: 0}
    out_specs = [placed, pl.BlockSpec((vp, h), whole, pipeline_mode=once)]
    out_shape = [
        jax.ShapeDtypeStruct(hidden.shape, jnp.bfloat16),
        jax.ShapeDtypeStruct((vp, h), jnp.float32),
    ]
    scratch = [
        pltpu.VMEM((mloc, vp, t), jnp.float32),
        pltpu.VMEM((h, mloc * t), jnp.bfloat16),
    ]
    if last:
        n_hi, n_lo = dims
        r = h // (2 * n_hi * n_lo)
        ca = h // 2
        cx = (h - ca) // 2
        for shape in ((n_lo, n_hi, r, ca), (n_lo, n_hi, r, ca), (2, n_lo, n_hi, r, cx), (2, n_lo, n_hi, r, cx)):
            out_specs.append(pl.BlockSpec(shape, lambda s, k=len(shape): (0,) * k, pipeline_mode=once))
            out_shape.append(jax.ShapeDtypeStruct(shape, jnp.float32))
        scratch = [pltpu.VMEM((h, h), jnp.float32)] + scratch
    else:
        out_specs.append(pl.BlockSpec((h, h), whole, pipeline_mode=once))
        out_shape.append(jax.ShapeDtypeStruct((h, h), jnp.float32))
    return pl.pallas_call(
        kernel_fn,
        grid=(steps,),
        in_specs=in_specs,
        out_specs=out_specs,
        out_shape=out_shape,
        scratch_shapes=scratch,
        input_output_aliases=aliases,
        compiler_params=pltpu.CompilerParams(vmem_limit_bytes=BWD_VMEM),
        cost_estimate=pl.CostEstimate(
            flops=4 * mloc * p * h * (h + v), bytes_accessed=mloc * p * h * 10 + 10 * h * h,
            transcendentals=mloc * p * v * 8,
        ),
        name="backward_part",
    )(*args)


def shards(hidden, target, area, var_weight, w_inner, b_inner, w_out, b_out):
    mloc, h, n = hidden.shape
    n_mem = lax.axis_size("mem")
    n_grid = lax.axis_size("grid")
    members = mloc * n_mem
    npoints = n * n_grid
    v = w_out.shape[0]
    vp = 128
    n_lo = 2
    while n_lo * n_lo * 4 <= n_grid:
        n_lo *= 2
    n_hi = n_grid // n_lo

    swap_x = [(i, (i + n_mem // 2) % n_mem) for i in range(n_mem)]
    swap_core = [(i, i ^ 1) for i in range(n_mem)]

    def shift_lo(k):
        return [(a * n_lo + b, a * n_lo + (b + k) % n_lo) for a in range(n_hi) for b in range(n_lo)]

    def shift_hi(k):
        return [(a * n_lo + b, (a + k) % n_hi * n_lo + b) for a in range(n_hi) for b in range(n_lo)]

    to_x = lambda a: lax.ppermute(a, "mem", swap_x)
    to_core = lambda a: lax.ppermute(a, "mem", swap_core)
    to_lo = lambda a, k: lax.ppermute(a, "grid", shift_lo(k))
    to_hi = lambda a, k: lax.ppermute(a, "grid", shift_hi(k))

    half_out = w_out * jnp.bfloat16(0.5)
    parts = []
    for part in range(PARTS):
        parts.append(
            forward(part, hidden, w_inner, b_inner.reshape(1, h), half_out, b_out.reshape(1, v))
        )
    exchanged = []
    for act, slope, fields in parts:
        far = to_x(fields)
        exchanged.append((fields, to_core(fields), far, to_core(far)))

    w_inner, half_out, _ = lax.optimization_barrier((w_inner, half_out, parts[1][2]))
    wt = w_inner.T
    wot = jnp.pad(half_out, ((0, vp - v), (0, 0))).T
    vw, area = var_weight.reshape(1, v), area.reshape(1, n)
    acc = extra = gh = None
    for part in range(PARTS):
        act, slope, _ = parts[part]
        rest = (target, area, vw, act, slope, hidden, wot, wt)
        gh, extra, *accs = backward(
            part, (n_hi, n_lo), members, exchanged[part], rest, acc, extra, gh
        )
        acc = accs[0]
    keep_a, send_a, keep_x, send_x = accs

    core = lax.axis_index("mem") % 2
    x = lax.axis_index("mem") // 2

    def flips(name):
        n, k = lax.axis_size(name), 1
        while k < n:
            yield [(i, i ^ k) for i in range(n)]
            k *= 2

    def along_lo(blocks):
        total = blocks(0)
        for k in range(1, n_lo):
            total = total + to_lo(blocks(k), k)
        return total

    def along_hi(blocks):
        total = blocks[0]
        for k in range(1, n_hi):
            total = total + to_hi(blocks[k], k)
        return total

    half = vp // 2
    keep_e = lax.dynamic_slice_in_dim(extra, core * half, half, 0)
    send_e = lax.dynamic_slice_in_dim(extra, (1 - core) * half, half, 0)
    got_a = to_core(send_a)
    got_e = to_core(send_e)
    got_x = to_core(send_x)
    sum_a = along_lo(lambda k: keep_a[k] + got_a[k])
    own_x = keep_x[0] + got_x[0] + to_x(keep_x[1] + got_x[1])
    sum_e = keep_e + got_e
    for perm in flips("grid"):
        sum_e = sum_e + lax.ppermute(sum_e, "grid", perm)
    sum_e = sum_e + to_x(sum_e)
    sum_x = along_lo(lambda k: own_x[k])
    end_a = along_hi(sum_a)
    end_x = along_hi(sum_x)
    end_a = end_a + to_x(end_a)
    far_x = to_x(end_x)
    end_x = jnp.where(
        x == 0, jnp.concatenate([end_x, far_x], 1), jnp.concatenate([far_x, end_x], 1)
    )
    scale = 1.0 / math.sqrt(members * npoints)
    mine = jnp.concatenate([end_a, end_x], 1) * scale
    other = to_core(mine)
    grad_inner = jnp.where(
        core == 0, jnp.concatenate([mine, other], 0), jnp.concatenate([other, mine], 0)
    )
    other_e = to_core(sum_e)
    extra = jnp.where(
        core == 0, jnp.concatenate([sum_e, other_e], 0), jnp.concatenate([other_e, sum_e], 0)
    )
    loss = jnp.sum(extra[v]) / npoints
    return (loss, gh, grad_inner, extra[:v] * (0.5 * scale))


def solution(mesh):
    in_specs = (P("mem", None, "grid"), P(None, "grid"), P("grid"), P(), P(), P(), P(), P())
    out_specs = (P(), P("mem", None, "grid"), P("grid", None), P())
    return jax.shard_map(shards, mesh=mesh, in_specs=in_specs, out_specs=out_specs, check_vma=False)
```

```python
import functools
import math

import jax
import jax.numpy as jnp
from jax import lax
from jax.experimental import pallas as pl
from jax.experimental.pallas import tpu as pltpu
from jax.sharding import PartitionSpec as P

PARTS = 4
FWD_TILE = 512
BWD_TILE = 256
EPS = 0.0004
K0 = math.sqrt(2.0 / math.pi)
K1 = K0 * 0.044715
SLAB = 256
EXTRA_ROWS = 8
VMEM = 58 * 1024 * 1024
NT = (((1,), (1,)), ((), ()))


def column(row, size):
    r = lax.broadcasted_iota(jnp.int32, (size, size), 0)
    c = lax.broadcasted_iota(jnp.int32, (size, size), 1)
    return jnp.sum(jnp.where(r == c, row, 0.0), axis=1, keepdims=True)


def forward_kernel(tiles, hid_ref, w_ref, b_ref, wo_ref, bo_ref, act_ref, slope_ref, f_ref, bias, half, even, odd):
    step = pl.program_id(0)

    @pl.when(step == 0)
    def _():
        for k in range(bias.shape[0] // 128):
            bias[pl.ds(k * 128, 128), :] = jnp.broadcast_to(
                column(b_ref[:, pl.ds(k * 128, 128)], 128), (128, 128)
            )

        half[...] = wo_ref[...] * jnp.bfloat16(0.5)

    def both(fill, drain):
        h, t = fill.shape
        fill[...] = jnp.dot(w_ref[...], hid_ref[0], preferred_element_type=jnp.float32)
        out = jnp.broadcast_to(column(bo_ref[...], bo_ref.shape[1]), f_ref.shape[1:])
        for k in range(0, h, SLAB):
            for r in range(k, k + SLAB, 16):
                rows = pl.ds(r, 16)
                b = jnp.concatenate([bias[rows, :]] * 2, axis=1)
                for c in range(0, t, 256):
                    cols = pl.ds(c, 256)
                    x = drain[rows, cols] + b
                    q = x * x * K1
                    th = jnp.tanh(x * (K0 + q))
                    up = 1.0 + th
                    act_ref[0, rows, cols] = (x * up).astype(jnp.bfloat16)
                    slope_ref[0, rows, cols] = up * (1.0 + (1.0 - th) * (x * (K0 + 3.0 * q)))
            slab = pl.ds(k, SLAB)
            out = out + jnp.dot(
                half[:, slab], act_ref[0, slab, :], preferred_element_type=jnp.float32
            )
        f_ref[0] = out

    @pl.when(step % 2 == 0)
    def _():
        both(even, odd)

    @pl.when(step % 2 == 1)
    def _():
        both(odd, even)


def forward(part, hidden, w_inner, b_inner, w_out, b_out):
    mloc, h, n = hidden.shape
    v = w_out.shape[0]
    p = n // PARTS
    t = FWD_TILE
    per = p // t
    tiles = mloc * per
    whole = lambda s: (0, 0)
    once = pl.Buffered(1)

    def ahead(s):
        s = jnp.minimum(s, tiles - 1)
        return (s // per, 0, part * per + s % per)

    def behind(s):
        s = jnp.maximum(s - 1, 0)
        return (s // per, 0, s % per)

    return pl.pallas_call(
        functools.partial(forward_kernel, tiles),
        grid=(tiles + 1,),
        in_specs=[
            pl.BlockSpec((1, h, t), ahead),
            pl.BlockSpec((h, h), whole, pipeline_mode=once),
            pl.BlockSpec((1, h), whole, pipeline_mode=once),
            pl.BlockSpec((v, h), whole, pipeline_mode=once),
            pl.BlockSpec((1, v), whole, pipeline_mode=once),
        ],
        out_specs=[
            pl.BlockSpec((1, h, t), behind),
            pl.BlockSpec((1, h, t), behind),
            pl.BlockSpec((1, v, t), behind),
        ],
        out_shape=[
            jax.ShapeDtypeStruct((mloc, h, p), jnp.bfloat16),
            jax.ShapeDtypeStruct((mloc, h, p), jnp.float32),
            jax.ShapeDtypeStruct((mloc, v, p), jnp.float32),
        ],
        scratch_shapes=[
            pltpu.VMEM((h, 128), jnp.float32),
            pltpu.VMEM((v, h), jnp.bfloat16),
            pltpu.VMEM((h, t), jnp.float32),
            pltpu.VMEM((h, t), jnp.float32),
        ],
        compiler_params=pltpu.CompilerParams(vmem_limit_bytes=VMEM),
        cost_estimate=pl.CostEstimate(
            flops=2 * mloc * p * h * (h + v), bytes_accessed=mloc * p * h * 8 + 2 * h * h,
            transcendentals=mloc * p * h,
        ),
        name="forward_part",
    )(hidden, w_inner, b_inner, w_out, b_out)


def backward_kernel(
    first, last, dims, members,
    f_ref, fc_ref, fx_ref, fxc_ref, target_ref, area_ref, vw_ref, act_ref, slope_ref, hid_ref,
    wot_ref, wt_ref, acc_in, extra_in, gh_in, gh_ref, extra_ref, *refs,
):
    if last:
        keep_a, send_a, keep_x, send_x, acc, gf, gp = refs
    else:
        acc, gf, gp = refs
    step = pl.program_id(0)
    mloc, v, t = f_ref.shape
    h = wt_ref.shape[0]
    denom = members * (members - 1)
    vw = column(vw_ref[...], v)
    area = area_ref[...]
    loss = jnp.zeros((1, t), jnp.float32)
    for r0 in range(0, v, 8):
        rows = pl.ds(r0, min(8, v - r0))
        own = [f_ref[m, rows, :] for m in range(mloc)]
        others = [ref[m, rows, :] for ref in (fc_ref, fx_ref, fxc_ref) for m in range(mloc)]
        target = target_ref[rows, :]
        dsum = [None] * mloc
        obs = []
        cross = jnp.zeros_like(target)
        inner = jnp.zeros_like(target)
        near = jnp.zeros_like(target)
        n_cross = n_inner = 0

        def pair(a, b):
            d = a - b
            s = d * d + EPS
            r = lax.rsqrt(s)
            return d * r, s * r

        def add(m, value):
            dsum[m] = value if dsum[m] is None else dsum[m] + value

        for i in range(mloc):
            sl, ph = pair(own[i], target)
            obs.append(sl)
            near = near + ph
            for b in others:
                sl, ph = pair(own[i], b)
                add(i, sl)
                cross = cross + ph
                n_cross += 1
            for j in range(i + 1, mloc):
                sl, ph = pair(own[i], own[j])
                add(i, sl)
                add(j, -sl)
                inner = inner + ph
                n_inner += 1
        weight = vw[r0 : r0 + 8] * area
        for m in range(mloc):
            gf[m, rows, :] = weight * (obs[m] * (1.0 / members) - dsum[m] * (1.0 / denom))
        near = (near - 0.02 * mloc) * (1.0 / members)
        pairs = (inner - 0.02 * n_inner) + 0.5 * (cross - 0.02 * n_cross)
        loss = loss + jnp.sum(weight * (near - pairs * (1.0 / denom)), axis=0, keepdims=True)
    for m in range(mloc):
        gf[m, pl.ds(v, gf.shape[1] - v), :] = jnp.zeros((gf.shape[1] - v, t), jnp.float32)

    g = jnp.concatenate([gf[m] for m in range(mloc)], axis=1).astype(jnp.bfloat16)
    for k in range(0, h, SLAB):
        rows = pl.ds(k, SLAB)
        ga = jnp.dot(wot_ref[rows, :], g, preferred_element_type=jnp.float32)
        slope = jnp.concatenate([slope_ref[m, rows, :] for m in range(mloc)], axis=1)
        gp[rows, :] = (ga * slope).astype(jnp.bfloat16)
    hid = jnp.concatenate([hid_ref[m] for m in range(mloc)], axis=1)
    act = jnp.concatenate([act_ref[m] for m in range(mloc)], axis=1)
    extra = lax.dot_general(g, act, NT, preferred_element_type=jnp.float32)

    def accumulate(base, extra_base):
        extra_ref[...] = extra if extra_base is None else extra_base[...] + extra
        for k in range(0, h, SLAB):
            rows = pl.ds(k, SLAB)
            prod = lax.dot_general(gp[rows, :], hid, NT, preferred_element_type=jnp.float32)
            acc[rows, :] = prod if base is None else base[rows, :] + prod

    @pl.when(step == 0)
    def _():
        accumulate(acc_in, extra_in)

    @pl.when(step > 0)
    def _():
        accumulate(acc, extra_ref)

    extra_ref[pl.ds(v, 1), pl.ds(0, t)] += loss
    for k in range(0, h, SLAB):
        rows = pl.ds(k, SLAB)
        out = jnp.dot(wt_ref[rows, :], gp[...], preferred_element_type=jnp.float32)
        for m in range(mloc):
            gh_ref[m, rows, :] = out[:, m * t : (m + 1) * t].astype(jnp.bfloat16)
    if last:
        n_hi, n_lo = dims

        @pl.when(step == pl.num_programs(0) - 1)
        def _():
            mem = lax.axis_index("mem")
            grid = lax.axis_index("grid")
            x, core = mem // 2, mem % 2
            hi, lo = grid // n_lo, grid % n_lo
            r = h // (2 * n_hi * n_lo)
            ca = keep_a.shape[3]
            cx = keep_x.shape[4]
            for dlo in range(n_lo):
                for dhi in range(n_hi):
                    g = lax.rem(hi + dhi, n_hi) * n_lo + lax.rem(lo + dlo, n_lo)
                    for c, part_a, part_x in ((core, keep_a, keep_x), (1 - core, send_a, send_x)):
                        r0 = pl.multiple_of((g * 2 + c) * r, r)
                        part_a[dlo, dhi, pl.ds(0, r), :] = acc[pl.ds(r0, r), pl.ds(0, ca)]
                        e0 = (c * (n_hi * n_lo) + g) * EXTRA_ROWS
                        at = pl.multiple_of(
                            jnp.minimum(e0, extra_ref.shape[0] - EXTRA_ROWS), EXTRA_ROWS
                        )
                        for k in range(h // ca):
                            e = extra_ref[pl.ds(at, EXTRA_ROWS), pl.ds(k * ca, ca)]
                            part_a[dlo, dhi, pl.ds(r + k * EXTRA_ROWS, EXTRA_ROWS), :] = jnp.where(
                                e0 < extra_ref.shape[0], e, 0.0
                            )
                        left = acc[pl.ds(r0, r), pl.ds(ca, cx)]
                        right = acc[pl.ds(r0, r), pl.ds(ca + cx, cx)]
                        part_x[0, dlo, dhi] = jnp.where(x == 0, left, right)
                        part_x[1, dlo, dhi] = jnp.where(x == 0, right, left)


def backward(part, dims, members, fields, rest, acc, extra, gh):
    target, area, vw, act, slope, hidden, wot, wt = rest
    mloc, h, n = hidden.shape
    v = target.shape[0]
    vp = wot.shape[1]
    p = n // PARTS
    t = BWD_TILE
    steps = p // t
    first, last = part == 0, part == PARTS - 1
    off = part * steps
    once = pl.Buffered(1)
    f_spec = pl.BlockSpec((mloc, v, t), lambda s: (0, 0, s))
    big = pl.BlockSpec((mloc, h, t), lambda s: (0, 0, s))
    whole = lambda s: (0, 0)
    const = lambda a: pl.BlockSpec(a.shape, whole, pipeline_mode=once)
    anyspec = pl.BlockSpec(memory_space=pl.ANY)
    placed = pl.BlockSpec((mloc, h, t), lambda s: (0, 0, off + s))
    in_specs = [f_spec] * 4 + [
        pl.BlockSpec((v, t), lambda s: (0, off + s)),
        pl.BlockSpec((1, t), lambda s: (0, off + s)),
        const(vw), big, big, placed, const(wot), const(wt),
    ]
    args = [*fields, target, area, vw, act, slope, hidden, wot, wt]
    kernel = functools.partial(backward_kernel, first, last, dims, members)
    if first:
        kernel_fn = lambda *refs: kernel(*refs[:12], None, None, None, *refs[12:])
        aliases = {}
    else:
        kernel_fn = kernel
        in_specs += [const(acc), const(extra), anyspec]
        args += [acc, extra, gh]
        aliases = {14: 0}
    out_specs = [placed, pl.BlockSpec((vp, h), whole, pipeline_mode=once)]
    out_shape = [
        jax.ShapeDtypeStruct(hidden.shape, jnp.bfloat16),
        jax.ShapeDtypeStruct((vp, h), jnp.float32),
    ]
    scratch = [
        pltpu.VMEM((mloc, vp, t), jnp.float32),
        pltpu.VMEM((h, mloc * t), jnp.bfloat16),
    ]
    if last:
        n_hi, n_lo = dims
        r = h // (2 * n_hi * n_lo)
        ca = h // 2
        cx = (h - ca) // 2
        ra = r + h // ca * EXTRA_ROWS
        for shape in ((n_lo, n_hi, ra, ca), (n_lo, n_hi, ra, ca), (2, n_lo, n_hi, r, cx), (2, n_lo, n_hi, r, cx)):
            out_specs.append(pl.BlockSpec(shape, lambda s, k=len(shape): (0,) * k, pipeline_mode=once))
            out_shape.append(jax.ShapeDtypeStruct(shape, jnp.float32))
        scratch = [pltpu.VMEM((h, h), jnp.float32)] + scratch
    else:
        out_specs.append(pl.BlockSpec((h, h), whole, pipeline_mode=once))
        out_shape.append(jax.ShapeDtypeStruct((h, h), jnp.float32))
    return pl.pallas_call(
        kernel_fn,
        grid=(steps,),
        in_specs=in_specs,
        out_specs=out_specs,
        out_shape=out_shape,
        scratch_shapes=scratch,
        input_output_aliases=aliases,
        compiler_params=pltpu.CompilerParams(vmem_limit_bytes=VMEM),
        cost_estimate=pl.CostEstimate(
            flops=4 * mloc * p * h * (h + v), bytes_accessed=mloc * p * h * 10 + 10 * h * h,
            transcendentals=mloc * p * v * 8,
        ),
        name="backward_part",
    )(*args)


def shards(hidden, target, area, var_weight, w_inner, b_inner, w_out, b_out):
    mloc, h, n = hidden.shape
    n_mem = lax.axis_size("mem")
    n_grid = lax.axis_size("grid")
    members = mloc * n_mem
    npoints = n * n_grid
    v = w_out.shape[0]
    vp = 128
    n_lo = 2
    while n_lo * n_lo * 4 <= n_grid:
        n_lo *= 2
    n_hi = n_grid // n_lo

    swap_x = [(i, (i + n_mem // 2) % n_mem) for i in range(n_mem)]
    swap_core = [(i, i ^ 1) for i in range(n_mem)]

    def shift_lo(k):
        return [(a * n_lo + b, a * n_lo + (b + k) % n_lo) for a in range(n_hi) for b in range(n_lo)]

    def shift_hi(k):
        return [(a * n_lo + b, (a + k) % n_hi * n_lo + b) for a in range(n_hi) for b in range(n_lo)]

    to_x = lambda a: lax.ppermute(a, "mem", swap_x)
    to_core = lambda a: lax.ppermute(a, "mem", swap_core)
    to_lo = lambda a, k: lax.ppermute(a, "grid", shift_lo(k))
    to_hi = lambda a, k: lax.ppermute(a, "grid", shift_hi(k))

    parts = []
    for part in range(PARTS):
        parts.append(
            forward(part, hidden, w_inner, b_inner.reshape(1, h), w_out, b_out.reshape(1, v))
        )
    exchanged = []
    for act, slope, fields in parts:
        far = to_x(fields)
        exchanged.append((fields, to_core(fields), far, to_core(far)))

    w_inner, w_out, _ = lax.optimization_barrier((w_inner, w_out, parts[1][2]))
    wt = w_inner.T
    wot = jnp.pad(w_out * jnp.bfloat16(0.5), ((0, vp - v), (0, 0))).T
    vw, area = var_weight.reshape(1, v), area.reshape(1, n)
    acc = extra = gh = None
    for part in range(PARTS):
        act, slope, _ = parts[part]
        rest = (target, area, vw, act, slope, hidden, wot, wt)
        gh, extra, *accs = backward(
            part, (n_hi, n_lo), members, exchanged[part], rest, acc, extra, gh
        )
        acc = accs[0]
    keep_a, send_a, keep_x, send_x = accs


    def gathered(block, axis, name, bit):
        n = lax.axis_size(name)
        other = lax.ppermute(block, name, [(i, i ^ bit) for i in range(n)])
        return jnp.where(
            lax.axis_index(name) & bit == 0,
            jnp.concatenate([block, other], axis),
            jnp.concatenate([other, block], axis),
        )

    def along_lo(blocks):
        total = blocks(0)
        for k in range(1, n_lo):
            total = total + to_lo(blocks(k), k)
        return total

    def along_hi(blocks):
        total = blocks[0]
        for k in range(1, n_hi):
            total = total + to_hi(blocks[k], k)
        return total

    got_a = to_core(send_a)
    got_x = to_core(send_x)
    sum_a = along_lo(lambda k: keep_a[k] + got_a[k])
    own_x = keep_x[0] + got_x[0] + to_x(keep_x[1] + got_x[1])
    sum_x = along_lo(lambda k: own_x[k])
    end_a = along_hi(sum_a)
    end_x = along_hi(sum_x)
    end_a = end_a + to_x(end_a)
    r = h // (2 * n_grid)
    ca = end_a.shape[1]
    extra = jnp.concatenate(
        [end_a[r + k : r + k + EXTRA_ROWS] for k in range(0, end_a.shape[0] - r, EXTRA_ROWS)], 1
    )
    bit = 1
    while bit < n_grid:
        extra = gathered(extra, 0, "grid", bit)
        bit *= 2
    extra = gathered(extra, 0, "mem", 1)
    end_x = gathered(end_x, 1, "mem", n_mem // 2)
    scale = 1.0 / math.sqrt(members * npoints)
    grad_inner = gathered(jnp.concatenate([end_a[:r], end_x], 1) * scale, 0, "mem", 1)
    loss = jnp.sum(extra[v]) / npoints
    return (loss, gh, grad_inner, extra[:v] * (0.5 * scale))


def solution(mesh):
    in_specs = (P("mem", None, "grid"), P(None, "grid"), P("grid"), P(), P(), P(), P(), P())
    out_specs = (P(), P("mem", None, "grid"), P("grid", None), P())
    return jax.shard_map(shards, mesh=mesh, in_specs=in_specs, out_specs=out_specs, check_vma=False)
```

```python
import functools
import math

import jax
import jax.numpy as jnp
from jax import lax
from jax.experimental import pallas as pl
from jax.experimental.pallas import tpu as pltpu
from jax.sharding import PartitionSpec as P

EIGHTHS = (3, 3, 2)
TILE = 256
EPS = 0.0004
K0 = math.sqrt(2.0 / math.pi)
K1 = K0 * 0.044715
SLAB = 512
EXTRA_ROWS = 8
VMEM = 58 * 1024 * 1024
NT = (((1,), (1,)), ((), ()))


def column(row, size):
    r = lax.broadcasted_iota(jnp.int32, (size, size), 0)
    c = lax.broadcasted_iota(jnp.int32, (size, size), 1)
    return jnp.sum(jnp.where(r == c, row, 0.0), axis=1, keepdims=True)


def field_rows(v, mloc, m, r0):
    full = v // 8 * 8
    if r0 < full:
        return pl.ds(m * full + r0, 8)
    return pl.ds(mloc * full + m * (v - full), v - full)


def forward_kernel(mloc, hid_ref, w_ref, b_ref, wo_ref, bo_ref, act_ref, slope_ref, f_ref, bias, half, even, odd):
    step = pl.program_id(0)

    @pl.when(step == 0)
    def _():
        for k in range(bias.shape[0] // 128):
            bias[pl.ds(k * 128, 128), :] = jnp.broadcast_to(
                column(b_ref[:, pl.ds(k * 128, 128)], 128), (128, 128)
            )

        half[...] = wo_ref[...] * jnp.bfloat16(0.5)

    def both(m, fill, drain):
        h, t = fill.shape
        out = jnp.broadcast_to(column(bo_ref[...], bo_ref.shape[1]), (bo_ref.shape[1], t))
        for k in range(0, h, SLAB):
            slab = pl.ds(k, SLAB)
            fill[slab, :] = jnp.dot(
                w_ref[slab, :], hid_ref[0], preferred_element_type=jnp.float32
            )
            for r in range(k, k + SLAB, 16):
                rows = pl.ds(r, 16)
                x = drain[rows, :] + jnp.concatenate([bias[rows, :]] * (t // 128), axis=1)
                q = x * x * K1
                th = jnp.tanh(x * (K0 + q))
                up = 1.0 + th
                act_ref[0, rows, :] = (x * up).astype(jnp.bfloat16)
                slope_ref[0, rows, :] = up * (1.0 + (1.0 - th) * (x * (K0 + 3.0 * q)))
            out = out + jnp.dot(
                half[:, slab], act_ref[0, slab, :], preferred_element_type=jnp.float32
            )
        for r0 in range(0, out.shape[0], 8):
            f_ref[field_rows(out.shape[0], mloc, m, r0), :] = out[r0 : r0 + 8]

    @pl.when(step % 2 == 0)
    def _():
        both(1, even, odd)

    @pl.when(step % 2 == 1)
    def _():
        both(0, odd, even)


def forward(start, p, hidden, w_inner, b_inner, w_out, b_out):
    mloc, h, n = hidden.shape
    v = w_out.shape[0]
    t = TILE
    tiles = mloc * (p // t)
    assert mloc == 2
    whole = lambda s: (0, 0)
    once = pl.Buffered(1)

    def ahead(s):
        s = jnp.minimum(s, tiles - 1)
        return (s % mloc, 0, start // t + s // mloc)

    def behind(s):
        s = jnp.maximum(s - 1, 0)
        return (s % mloc, 0, s // mloc)

    return pl.pallas_call(
        functools.partial(forward_kernel, mloc),
        grid=(tiles + 1,),
        in_specs=[
            pl.BlockSpec((1, h, t), ahead),
            pl.BlockSpec((h, h), whole, pipeline_mode=once),
            pl.BlockSpec((1, h), whole, pipeline_mode=once),
            pl.BlockSpec((v, h), whole, pipeline_mode=once),
            pl.BlockSpec((1, v), whole, pipeline_mode=once),
        ],
        out_specs=[
            pl.BlockSpec((1, h, t), behind),
            pl.BlockSpec((1, h, t), behind),
            pl.BlockSpec((mloc * v, t), lambda s: (0, behind(s)[2])),
        ],
        out_shape=[
            jax.ShapeDtypeStruct((mloc, h, p), jnp.bfloat16),
            jax.ShapeDtypeStruct((mloc, h, p), jnp.float32),
            jax.ShapeDtypeStruct((mloc * v, p), jnp.float32),
        ],
        scratch_shapes=[
            pltpu.VMEM((h, 128), jnp.float32),
            pltpu.VMEM((v, h), jnp.bfloat16),
            pltpu.VMEM((h, t), jnp.float32),
            pltpu.VMEM((h, t), jnp.float32),
        ],
        compiler_params=pltpu.CompilerParams(vmem_limit_bytes=VMEM),
        cost_estimate=pl.CostEstimate(
            flops=2 * mloc * p * h * (h + v), bytes_accessed=mloc * p * h * 8 + 2 * h * h,
            transcendentals=mloc * p * h,
        ),
        name="forward_part",
    )(hidden, w_inner, b_inner, w_out, b_out)


def backward_kernel(
    first, last, dims, members,
    f_ref, fc_ref, fx_ref, fxc_ref, target_ref, area_ref, vw_ref, act_ref, slope_ref, hid_ref,
    wot_ref, acc_in, extra_in, gp_ref, extra_ref, *refs,
):
    if last:
        keep_a, send_a, keep_x, send_x, acc, *refs = refs
    else:
        acc, *refs = refs
    gf, gp, *refs = refs
    step = pl.program_id(0)
    mloc, _, t = hid_ref.shape
    v = target_ref.shape[0]
    h = wot_ref.shape[0]
    final = step == pl.num_programs(0) - 1
    if not first:
        earlier, sem = refs
        fetch = pltpu.make_async_copy(acc_in, earlier, sem)

        @pl.when(step == 0)
        def _():
            fetch.start()

    denom = members * (members - 1)
    vw = column(vw_ref[...], v)
    area = area_ref[...]
    loss = jnp.zeros((1, t), jnp.float32)
    for r0 in range(0, v, 8):
        rows = pl.ds(r0, min(8, v - r0))
        places = [field_rows(v, mloc, m, r0) for m in range(mloc)]
        own = [f_ref[place, :] for place in places]
        others = [ref[place, :] for ref in (fc_ref, fx_ref, fxc_ref) for place in places]
        target = target_ref[rows, :]
        dsum = [None] * mloc
        obs = []
        cross = jnp.zeros_like(target)
        inner = jnp.zeros_like(target)
        near = jnp.zeros_like(target)
        n_cross = n_inner = 0

        def pair(a, b):
            d = a - b
            s = d * d + EPS
            r = lax.rsqrt(s)
            return d * r, s * r

        def add(m, value):
            dsum[m] = value if dsum[m] is None else dsum[m] + value

        for i in range(mloc):
            sl, ph = pair(own[i], target)
            obs.append(sl)
            near = near + ph
            for b in others:
                sl, ph = pair(own[i], b)
                add(i, sl)
                cross = cross + ph
                n_cross += 1
            for j in range(i + 1, mloc):
                sl, ph = pair(own[i], own[j])
                add(i, sl)
                add(j, -sl)
                inner = inner + ph
                n_inner += 1
        weight = vw[r0 : r0 + 8] * area
        for m in range(mloc):
            gf[m, rows, :] = weight * (obs[m] * (1.0 / members) - dsum[m] * (1.0 / denom))
        near = (near - 0.02 * mloc) * (1.0 / members)
        pairs = (inner - 0.02 * n_inner) + 0.5 * (cross - 0.02 * n_cross)
        loss = loss + jnp.sum(weight * (near - pairs * (1.0 / denom)), axis=0, keepdims=True)
    for m in range(mloc):
        gf[m, pl.ds(v, gf.shape[1] - v), :] = jnp.zeros((gf.shape[1] - v, t), jnp.float32)

    g = jnp.concatenate([gf[m] for m in range(mloc)], axis=1).astype(jnp.bfloat16)
    for k in range(0, h, 256):
        rows = pl.ds(k, 256)
        ga = jnp.dot(wot_ref[rows, :], g, preferred_element_type=jnp.float32)
        for m in range(mloc):
            piece = (ga[:, m * t : (m + 1) * t] * slope_ref[m, rows, :]).astype(jnp.bfloat16)
            gp[rows, pl.ds(m * t, t)] = piece
            gp_ref[m, rows, :] = piece
    hid = jnp.concatenate([hid_ref[m] for m in range(mloc)], axis=1)
    act = jnp.concatenate([act_ref[m] for m in range(mloc)], axis=1)
    extra = lax.dot_general(g, act, NT, preferred_element_type=jnp.float32)

    def accumulate(base, extra_base):
        extra_ref[...] = extra if extra_base is None else extra_base[...] + extra
        for k in range(0, h, SLAB):
            rows = pl.ds(k, SLAB)
            prod = lax.dot_general(gp[rows, :], hid, NT, preferred_element_type=jnp.float32)
            acc[rows, :] = prod if base is None else base[rows, :] + prod

    @pl.when(step == 0)
    def _():
        accumulate(None, extra_in)

    @pl.when(step > 0)
    def _():
        accumulate(acc, extra_ref)

    extra_ref[pl.ds(v, 1), pl.ds(0, t)] += loss
    if not first:

        @pl.when(final)
        def _():
            fetch.wait()
            if not last:
                acc[...] += earlier[...]

    if last:
        n_hi, n_lo = dims

        @pl.when(final)
        def _():
            mem = lax.axis_index("mem")
            grid = lax.axis_index("grid")
            x, core = mem // 2, mem % 2
            hi, lo = grid // n_lo, grid % n_lo
            r = h // (2 * n_hi * n_lo)
            ca = keep_a.shape[3]
            cx = keep_x.shape[4]
            for dlo in range(n_lo):
                for dhi in range(n_hi):
                    g = lax.rem(hi + dhi, n_hi) * n_lo + lax.rem(lo + dlo, n_lo)
                    for c, part_a, part_x in ((core, keep_a, keep_x), (1 - core, send_a, send_x)):
                        r0 = pl.multiple_of((g * 2 + c) * r, r)
                        total = acc[pl.ds(r0, r), :] + earlier[pl.ds(r0, r), :]
                        part_a[dlo, dhi, pl.ds(0, r), :] = total[:, :ca]
                        e0 = (c * (n_hi * n_lo) + g) * EXTRA_ROWS
                        at = pl.multiple_of(
                            jnp.minimum(e0, extra_ref.shape[0] - EXTRA_ROWS), EXTRA_ROWS
                        )
                        for k in range(h // ca):
                            e = extra_ref[pl.ds(at, EXTRA_ROWS), pl.ds(k * ca, ca)]
                            part_a[dlo, dhi, pl.ds(r + k * EXTRA_ROWS, EXTRA_ROWS), :] = jnp.where(
                                e0 < extra_ref.shape[0], e, 0.0
                            )
                        left = total[:, ca : ca + cx]
                        right = total[:, ca + cx :]
                        part_x[0, dlo, dhi] = jnp.where(x == 0, left, right)
                        part_x[1, dlo, dhi] = jnp.where(x == 0, right, left)


def backward(start, p, first, last, dims, members, fields, rest, acc, extra):
    target, area, vw, act, slope, hidden, wot = rest
    mloc, h, n = hidden.shape
    v = target.shape[0]
    vp = wot.shape[1]
    t = TILE
    off = start // t
    once = pl.Buffered(1)
    f_spec = pl.BlockSpec((mloc * v, t), lambda s: (0, s))
    big = pl.BlockSpec((mloc, h, t), lambda s: (0, 0, s))
    whole = lambda s: (0, 0)
    const = lambda a: pl.BlockSpec(a.shape, whole, pipeline_mode=once)
    in_specs = [f_spec] * 4 + [
        pl.BlockSpec((v, t), lambda s: (0, off + s)),
        pl.BlockSpec((1, t), lambda s: (0, off + s)),
        const(vw), big, big,
        pl.BlockSpec((mloc, h, t), lambda s: (0, 0, off + s)),
        const(wot),
    ]
    args = [*fields, target, area, vw, act, slope, hidden, wot]
    kernel = functools.partial(backward_kernel, first, last, dims, members)
    if first:
        kernel_fn = lambda *refs: kernel(*refs[:11], None, None, *refs[11:])
    else:
        kernel_fn = kernel
        in_specs += [pl.BlockSpec(memory_space=pl.ANY), const(extra)]
        args += [acc, extra]
    out_specs = [big, pl.BlockSpec((vp, h), whole, pipeline_mode=once)]
    out_shape = [
        jax.ShapeDtypeStruct((mloc, h, p), jnp.bfloat16),
        jax.ShapeDtypeStruct((vp, h), jnp.float32),
    ]
    scratch = [
        pltpu.VMEM((mloc, vp, t), jnp.float32),
        pltpu.VMEM((h, mloc * t), jnp.bfloat16),
    ]
    if not first:
        scratch += [pltpu.VMEM((h, h), jnp.float32), pltpu.SemaphoreType.DMA]
    if last:
        n_hi, n_lo = dims
        r = h // (2 * n_hi * n_lo)
        ca = h // 2
        cx = (h - ca) // 2
        ra = r + h // ca * EXTRA_ROWS
        for shape in ((n_lo, n_hi, ra, ca), (n_lo, n_hi, ra, ca), (2, n_lo, n_hi, r, cx), (2, n_lo, n_hi, r, cx)):
            out_specs.append(
                pl.BlockSpec(shape, lambda s, k=len(shape): (0,) * k, pipeline_mode=once)
            )
            out_shape.append(jax.ShapeDtypeStruct(shape, jnp.float32))
        scratch = [pltpu.VMEM((h, h), jnp.float32)] + scratch
    else:
        out_specs.append(pl.BlockSpec((h, h), whole, pipeline_mode=once))
        out_shape.append(jax.ShapeDtypeStruct((h, h), jnp.float32))
    return pl.pallas_call(
        kernel_fn,
        grid=(p // t,),
        in_specs=in_specs,
        out_specs=out_specs,
        out_shape=out_shape,
        scratch_shapes=scratch,
        compiler_params=pltpu.CompilerParams(vmem_limit_bytes=VMEM),
        cost_estimate=pl.CostEstimate(
            flops=2 * mloc * p * h * (h + 2 * v), bytes_accessed=mloc * p * h * 10 + 10 * h * h,
            transcendentals=mloc * p * v * 8,
        ),
        name="backward_part",
    )(*args)


def input_kernel(wt_ref, gp_ref, *refs):
    refs[-1][0] = jnp.dot(wt_ref[...], gp_ref[0], preferred_element_type=jnp.float32).astype(
        jnp.bfloat16
    )


def input_gradient(start, p, n, wt, gp, gh):
    mloc, h, _ = gp.shape
    t = TILE
    off = start // t
    in_specs = [
        pl.BlockSpec((h, h), lambda m, s: (0, 0), pipeline_mode=pl.Buffered(1)),
        pl.BlockSpec((1, h, t), lambda m, s: (m, 0, s)),
    ]
    args = [wt, gp]
    if gh is not None:
        in_specs.append(pl.BlockSpec(memory_space=pl.ANY))
        args.append(gh)
    return pl.pallas_call(
        input_kernel,
        grid=(mloc, p // t),
        in_specs=in_specs,
        out_specs=pl.BlockSpec((1, h, t), lambda m, s: (m, 0, off + s)),
        out_shape=jax.ShapeDtypeStruct((mloc, h, n), jnp.bfloat16),
        input_output_aliases={} if gh is None else {2: 0},
        compiler_params=pltpu.CompilerParams(vmem_limit_bytes=VMEM),
        cost_estimate=pl.CostEstimate(
            flops=2 * mloc * p * h * h, bytes_accessed=mloc * p * h * 4 + 2 * h * h,
            transcendentals=0,
        ),
        name="grad_hidden_part",
    )(*args)


def shards(hidden, target, area, var_weight, w_inner, b_inner, w_out, b_out):
    mloc, h, n = hidden.shape
    n_mem = lax.axis_size("mem")
    n_grid = lax.axis_size("grid")
    members = mloc * n_mem
    npoints = n * n_grid
    v = w_out.shape[0]
    vp = 128
    n_lo = 2
    while n_lo * n_lo * 4 <= n_grid:
        n_lo *= 2
    n_hi = n_grid // n_lo

    swap_x = [(i, (i + n_mem // 2) % n_mem) for i in range(n_mem)]
    swap_core = [(i, i ^ 1) for i in range(n_mem)]

    def shift_lo(k):
        return [(a * n_lo + b, a * n_lo + (b + k) % n_lo) for a in range(n_hi) for b in range(n_lo)]

    def shift_hi(k):
        return [(a * n_lo + b, (a + k) % n_hi * n_lo + b) for a in range(n_hi) for b in range(n_lo)]

    to_x = lambda a: lax.ppermute(a, "mem", swap_x)
    to_core = lambda a: lax.ppermute(a, "mem", swap_core)
    to_lo = lambda a, k: lax.ppermute(a, "grid", shift_lo(k))
    to_hi = lambda a, k: lax.ppermute(a, "grid", shift_hi(k))

    unit = n // sum(EIGHTHS)
    starts = [unit * sum(EIGHTHS[:k]) for k in range(len(EIGHTHS))]
    spans = [(start, unit * size) for start, size in zip(starts, EIGHTHS)]
    parts = [
        forward(start, p, hidden, w_inner, b_inner.reshape(1, h), w_out, b_out.reshape(1, v))
        for start, p in spans
    ]
    exchanged = []
    for act, slope, fields in parts:
        far = to_x(fields)
        exchanged.append((fields, to_core(fields), far, to_core(far)))

    w_inner, w_out, _ = lax.optimization_barrier((w_inner, w_out, parts[1][2]))
    wt = w_inner.T
    wot = jnp.pad(w_out * jnp.bfloat16(0.5), ((0, vp - v), (0, 0))).T
    vw, area = var_weight.reshape(1, v), area.reshape(1, n)
    acc = extra = gh = None
    grad_pre = []
    for k, (start, p) in enumerate(spans):
        act, slope, _ = parts[k]
        first, last = k == 0, k == len(spans) - 1
        gp, extra, *accs = backward(
            start, p, first, last, (n_hi, n_lo), members, exchanged[k],
            (target, area, vw, act, slope, hidden, wot), acc, extra,
        )
        grad_pre.append(gp)
        acc = accs[0]
    keep_a, send_a, keep_x, send_x = accs
    wt, _ = lax.optimization_barrier((wt, extra))
    for (start, p), gp in zip(spans, grad_pre):
        gh = input_gradient(start, p, n, wt, gp, gh)

    def gathered(block, axis, name, bit):
        n = lax.axis_size(name)
        other = lax.ppermute(block, name, [(i, i ^ bit) for i in range(n)])
        return jnp.where(
            lax.axis_index(name) & bit == 0,
            jnp.concatenate([block, other], axis),
            jnp.concatenate([other, block], axis),
        )

    def along_lo(blocks):
        total = blocks(0)
        for k in range(1, n_lo):
            total = total + to_lo(blocks(k), k)
        return total

    def along_hi(blocks):
        total = blocks[0]
        for k in range(1, n_hi):
            total = total + to_hi(blocks[k], k)
        return total

    got_a = to_core(send_a)
    got_x = to_core(send_x)
    sum_a = along_lo(lambda k: keep_a[k] + got_a[k])
    own_x = keep_x[0] + got_x[0] + to_x(keep_x[1] + got_x[1])
    sum_x = along_lo(lambda k: own_x[k])
    end_a = along_hi(sum_a)
    end_x = along_hi(sum_x)
    end_a = end_a + to_x(end_a)
    r = h // (2 * n_grid)
    ca = end_a.shape[1]
    extra = jnp.concatenate(
        [end_a[r + k : r + k + EXTRA_ROWS] for k in range(0, end_a.shape[0] - r, EXTRA_ROWS)], 1
    )
    bit = 1
    while bit < n_grid:
        extra = gathered(extra, 0, "grid", bit)
        bit *= 2
    extra = gathered(extra, 0, "mem", 1)
    end_x = gathered(end_x, 1, "mem", n_mem // 2)
    scale = 1.0 / math.sqrt(members * npoints)
    grad_inner = gathered(jnp.concatenate([end_a[:r], end_x], 1) * scale, 0, "mem", 1)
    loss = jnp.sum(extra[v]) / npoints
    return (loss, gh, grad_inner, extra[:v] * (0.5 * scale))


def solution(mesh):
    in_specs = (P("mem", None, "grid"), P(None, "grid"), P("grid"), P(), P(), P(), P(), P())
    out_specs = (P(), P("mem", None, "grid"), P("grid", None), P())
    return jax.shard_map(shards, mesh=mesh, in_specs=in_specs, out_specs=out_specs, check_vma=False)
```

```python
import functools
import math

import jax
import jax.numpy as jnp
from jax import lax
from jax.experimental import pallas as pl
from jax.experimental.pallas import tpu as pltpu
from jax.sharding import PartitionSpec as P

EIGHTHS = (3, 3, 2)
TILE = 256
EPS = 0.0004
K0 = math.sqrt(2.0 / math.pi)
K1 = K0 * 0.044715
SLAB = 512
EXTRA_ROWS = 8
VMEM = 58 * 1024 * 1024
NT = (((1,), (1,)), ((), ()))


def column(row, size):
    r = lax.broadcasted_iota(jnp.int32, (size, size), 0)
    c = lax.broadcasted_iota(jnp.int32, (size, size), 1)
    return jnp.sum(jnp.where(r == c, row, 0.0), axis=1, keepdims=True)


def field_rows(v, mloc, m, r0):
    full = v // 8 * 8
    if r0 < full:
        return pl.ds(m * full + r0, 8)
    return pl.ds(mloc * full + m * (v - full), v - full)


def forward_kernel(mloc, hid_ref, w_ref, b_ref, wo_ref, bo_ref, act_ref, slope_ref, f_ref, bias, half, even, odd):
    step = pl.program_id(0)

    @pl.when(step == 0)
    def _():
        for k in range(bias.shape[0] // 128):
            bias[pl.ds(k * 128, 128), :] = jnp.broadcast_to(
                column(b_ref[:, pl.ds(k * 128, 128)], 128), (128, 128)
            )

        half[...] = wo_ref[...] * jnp.bfloat16(0.5)

    def both(m, fill, drain):
        h, t = fill.shape
        out = jnp.broadcast_to(column(bo_ref[...], bo_ref.shape[1]), (bo_ref.shape[1], t))
        for k in range(0, h, SLAB):
            slab = pl.ds(k, SLAB)
            fill[slab, :] = jnp.dot(
                w_ref[slab, :], hid_ref[0], preferred_element_type=jnp.float32
            )
            for r in range(k, k + SLAB, 16):
                rows = pl.ds(r, 16)
                x = drain[rows, :] + jnp.concatenate([bias[rows, :]] * (t // 128), axis=1)
                q = x * x * K1
                th = jnp.tanh(x * (K0 + q))
                up = 1.0 + th
                act = x * up
                act_ref[0, rows, :] = act.astype(jnp.bfloat16)
                slope_ref[0, rows, :] = up + act * ((1.0 - th) * (K0 + 3.0 * q))
            out = out + jnp.dot(
                half[:, slab], act_ref[0, slab, :], preferred_element_type=jnp.float32
            )
        for r0 in range(0, out.shape[0], 8):
            f_ref[field_rows(out.shape[0], mloc, m, r0), :] = out[r0 : r0 + 8]

    @pl.when(step % 2 == 0)
    def _():
        both(1, even, odd)

    @pl.when(step % 2 == 1)
    def _():
        both(0, odd, even)


def forward(start, p, hidden, w_inner, b_inner, w_out, b_out):
    mloc, h, n = hidden.shape
    v = w_out.shape[0]
    t = TILE
    tiles = mloc * (p // t)
    assert mloc == 2
    whole = lambda s: (0, 0)
    once = pl.Buffered(1)

    def ahead(s):
        s = jnp.minimum(s, tiles - 1)
        return (s % mloc, 0, start // t + s // mloc)

    def behind(s):
        s = jnp.maximum(s - 1, 0)
        return (s % mloc, 0, s // mloc)

    return pl.pallas_call(
        functools.partial(forward_kernel, mloc),
        grid=(tiles + 1,),
        in_specs=[
            pl.BlockSpec((1, h, t), ahead),
            pl.BlockSpec((h, h), whole, pipeline_mode=once),
            pl.BlockSpec((1, h), whole, pipeline_mode=once),
            pl.BlockSpec((v, h), whole, pipeline_mode=once),
            pl.BlockSpec((1, v), whole, pipeline_mode=once),
        ],
        out_specs=[
            pl.BlockSpec((1, h, t), behind),
            pl.BlockSpec((1, h, t), behind),
            pl.BlockSpec((mloc * v, t), lambda s: (0, behind(s)[2])),
        ],
        out_shape=[
            jax.ShapeDtypeStruct((mloc, h, p), jnp.bfloat16),
            jax.ShapeDtypeStruct((mloc, h, p), jnp.float32),
            jax.ShapeDtypeStruct((mloc * v, p), jnp.float32),
        ],
        scratch_shapes=[
            pltpu.VMEM((h, 128), jnp.float32),
            pltpu.VMEM((v, h), jnp.bfloat16),
            pltpu.VMEM((h, t), jnp.float32),
            pltpu.VMEM((h, t), jnp.float32),
        ],
        compiler_params=pltpu.CompilerParams(vmem_limit_bytes=VMEM),
        cost_estimate=pl.CostEstimate(
            flops=2 * mloc * p * h * (h + v), bytes_accessed=mloc * p * h * 8 + 2 * h * h,
            transcendentals=mloc * p * h,
        ),
        name="forward_part",
    )(hidden, w_inner, b_inner, w_out, b_out)


def backward_kernel(
    first, last, dims, members,
    f_ref, fc_ref, fx_ref, fxc_ref, target_ref, area_ref, vw_ref, act_ref, slope_ref, hid_ref,
    wot_ref, acc_in, extra_in, gp_ref, extra_ref, *refs,
):
    if last:
        keep_a, send_a, keep_x, send_x, acc, *refs = refs
    else:
        acc, *refs = refs
    gf, *refs = refs
    step = pl.program_id(0)
    mloc, _, t = hid_ref.shape
    v = target_ref.shape[0]
    h = wot_ref.shape[0]
    final = step == pl.num_programs(0) - 1
    if not first:
        earlier, sem = refs
        fetch = pltpu.make_async_copy(acc_in, earlier, sem)

        @pl.when(step == 0)
        def _():
            fetch.start()

    denom = members * (members - 1)
    vw = column(vw_ref[...], v)
    area = area_ref[...]
    loss = jnp.zeros((1, t), jnp.float32)
    for r0 in range(0, v, 8):
        rows = pl.ds(r0, min(8, v - r0))
        places = [field_rows(v, mloc, m, r0) for m in range(mloc)]
        own = [f_ref[place, :] for place in places]
        others = [ref[place, :] for ref in (fc_ref, fx_ref, fxc_ref) for place in places]
        target = target_ref[rows, :]
        dsum = [None] * mloc
        obs = []
        cross = jnp.zeros_like(target)
        inner = jnp.zeros_like(target)
        near = jnp.zeros_like(target)
        n_cross = n_inner = 0

        def pair(a, b):
            d = a - b
            s = d * d + EPS
            r = lax.rsqrt(s)
            return d * r, s * r

        def add(m, value):
            dsum[m] = value if dsum[m] is None else dsum[m] + value

        for i in range(mloc):
            sl, ph = pair(own[i], target)
            obs.append(sl)
            near = near + ph
            for b in others:
                sl, ph = pair(own[i], b)
                add(i, sl)
                cross = cross + ph
                n_cross += 1
            for j in range(i + 1, mloc):
                sl, ph = pair(own[i], own[j])
                add(i, sl)
                add(j, -sl)
                inner = inner + ph
                n_inner += 1
        weight = vw[r0 : r0 + 8] * area
        for m in range(mloc):
            gf[m, rows, :] = weight * (obs[m] * (1.0 / members) - dsum[m] * (1.0 / denom))
        near = (near - 0.02 * mloc) * (1.0 / members)
        pairs = (inner - 0.02 * n_inner) + 0.5 * (cross - 0.02 * n_cross)
        loss = loss + jnp.sum(weight * (near - pairs * (1.0 / denom)), axis=0, keepdims=True)
    for m in range(mloc):
        gf[m, pl.ds(v, gf.shape[1] - v), :] = jnp.zeros((gf.shape[1] - v, t), jnp.float32)

    g = jnp.concatenate([gf[m] for m in range(mloc)], axis=1).astype(jnp.bfloat16)
    for k in range(0, h, 256):
        rows = pl.ds(k, 256)
        ga = jnp.dot(wot_ref[rows, :], g, preferred_element_type=jnp.float32)
        for m in range(mloc):
            piece = (ga[:, m * t : (m + 1) * t] * slope_ref[m, rows, :]).astype(jnp.bfloat16)
            gp_ref[rows, pl.ds(m * t, t)] = piece
    hid = jnp.concatenate([hid_ref[m] for m in range(mloc)], axis=1)
    act = jnp.concatenate([act_ref[m] for m in range(mloc)], axis=1)
    extra = lax.dot_general(g, act, NT, preferred_element_type=jnp.float32)

    def accumulate(base, extra_base):
        extra_ref[...] = extra if extra_base is None else extra_base[...] + extra
        for k in range(0, h, SLAB):
            rows = pl.ds(k, SLAB)
            prod = lax.dot_general(gp_ref[rows, :], hid, NT, preferred_element_type=jnp.float32)
            acc[rows, :] = prod if base is None else base[rows, :] + prod

    @pl.when(step == 0)
    def _():
        accumulate(None, extra_in)

    @pl.when(step > 0)
    def _():
        accumulate(acc, extra_ref)

    extra_ref[pl.ds(v, 1), pl.ds(0, t)] += loss
    if not first:

        @pl.when(final)
        def _():
            fetch.wait()
            if not last:
                acc[...] += earlier[...]

    if last:
        n_hi, n_lo = dims

        @pl.when(final)
        def _():
            mem = lax.axis_index("mem")
            grid = lax.axis_index("grid")
            x, core = mem // 2, mem % 2
            hi, lo = grid // n_lo, grid % n_lo
            r = h // (2 * n_hi * n_lo)
            ca = keep_a.shape[3]
            cx = keep_x.shape[4]
            for dlo in range(n_lo):
                for dhi in range(n_hi):
                    g = lax.rem(hi + dhi, n_hi) * n_lo + lax.rem(lo + dlo, n_lo)
                    for c, part_a, part_x in ((core, keep_a, keep_x), (1 - core, send_a, send_x)):
                        r0 = pl.multiple_of((g * 2 + c) * r, r)
                        total = acc[pl.ds(r0, r), :] + earlier[pl.ds(r0, r), :]
                        part_a[dlo, dhi, pl.ds(0, r), :] = total[:, :ca]
                        e0 = dhi * n_lo + lax.rem(lo + dlo, n_lo)
                        e0 = (c * (n_hi * n_lo) + e0) * EXTRA_ROWS
                        at = pl.multiple_of(
                            jnp.minimum(e0, extra_ref.shape[0] - EXTRA_ROWS), EXTRA_ROWS
                        )
                        for k in range(h // ca):
                            e = extra_ref[pl.ds(at, EXTRA_ROWS), pl.ds(k * ca, ca)]
                            part_a[dlo, dhi, pl.ds(r + k * EXTRA_ROWS, EXTRA_ROWS), :] = jnp.where(
                                e0 < extra_ref.shape[0], e, 0.0
                            )
                        left = total[:, ca : ca + cx]
                        right = total[:, ca + cx :]
                        part_x[0, dlo, dhi] = jnp.where(x == 0, left, right)
                        part_x[1, dlo, dhi] = jnp.where(x == 0, right, left)


def backward(start, p, first, last, dims, members, fields, rest, acc, extra):
    target, area, vw, act, slope, hidden, wot = rest
    mloc, h, n = hidden.shape
    v = target.shape[0]
    vp = wot.shape[1]
    t = TILE
    off = start // t
    once = pl.Buffered(1)
    f_spec = pl.BlockSpec((mloc * v, t), lambda s: (0, s))
    big = pl.BlockSpec((mloc, h, t), lambda s: (0, 0, s))
    whole = lambda s: (0, 0)
    const = lambda a: pl.BlockSpec(a.shape, whole, pipeline_mode=once)
    in_specs = [f_spec] * 4 + [
        pl.BlockSpec((v, t), lambda s: (0, off + s)),
        pl.BlockSpec((1, t), lambda s: (0, off + s)),
        const(vw), big, big,
        pl.BlockSpec((mloc, h, t), lambda s: (0, 0, off + s)),
        const(wot),
    ]
    args = [*fields, target, area, vw, act, slope, hidden, wot]
    kernel = functools.partial(backward_kernel, first, last, dims, members)
    if first:
        kernel_fn = lambda *refs: kernel(*refs[:11], None, None, *refs[11:])
    else:
        kernel_fn = kernel
        in_specs += [pl.BlockSpec(memory_space=pl.ANY), const(extra)]
        args += [acc, extra]
    out_specs = [
        pl.BlockSpec((h, mloc * t), lambda s: (0, s)),
        pl.BlockSpec((vp, h), whole, pipeline_mode=once),
    ]
    out_shape = [
        jax.ShapeDtypeStruct((h, mloc * p), jnp.bfloat16),
        jax.ShapeDtypeStruct((vp, h), jnp.float32),
    ]
    scratch = [pltpu.VMEM((mloc, vp, t), jnp.float32)]
    if not first:
        scratch += [pltpu.VMEM((h, h), jnp.float32), pltpu.SemaphoreType.DMA]
    if last:
        n_hi, n_lo = dims
        r = h // (2 * n_hi * n_lo)
        ca = h // 2
        cx = (h - ca) // 2
        ra = r + h // ca * EXTRA_ROWS
        for shape in ((n_lo, n_hi, ra, ca), (n_lo, n_hi, ra, ca), (2, n_lo, n_hi, r, cx), (2, n_lo, n_hi, r, cx)):
            out_specs.append(
                pl.BlockSpec(shape, lambda s, k=len(shape): (0,) * k, pipeline_mode=once)
            )
            out_shape.append(jax.ShapeDtypeStruct(shape, jnp.float32))
        scratch = [pltpu.VMEM((h, h), jnp.float32)] + scratch
    else:
        out_specs.append(pl.BlockSpec((h, h), whole, pipeline_mode=once))
        out_shape.append(jax.ShapeDtypeStruct((h, h), jnp.float32))
    return pl.pallas_call(
        kernel_fn,
        grid=(p // t,),
        in_specs=in_specs,
        out_specs=out_specs,
        out_shape=out_shape,
        scratch_shapes=scratch,
        compiler_params=pltpu.CompilerParams(vmem_limit_bytes=VMEM),
        cost_estimate=pl.CostEstimate(
            flops=2 * mloc * p * h * (h + 2 * v), bytes_accessed=mloc * p * h * 10 + 10 * h * h,
            transcendentals=mloc * p * v * 8,
        ),
        name="backward_part",
    )(*args)


def input_kernel(wt_ref, gp_ref, *refs):
    mloc, h, t = refs[-1].shape
    for k in range(0, h, SLAB):
        rows = pl.ds(k, SLAB)
        out = jnp.dot(wt_ref[rows, :], gp_ref[...], preferred_element_type=jnp.float32)
        for m in range(mloc):
            refs[-1][m, rows, :] = out[:, m * t : (m + 1) * t].astype(jnp.bfloat16)


def input_gradient(start, p, n, wt, gp, gh):
    h = gp.shape[0]
    mloc = gp.shape[1] // p
    t = TILE
    off = start // t
    in_specs = [
        pl.BlockSpec((h, h), lambda s: (0, 0), pipeline_mode=pl.Buffered(1)),
        pl.BlockSpec((h, mloc * t), lambda s: (0, s)),
    ]
    args = [wt, gp]
    if gh is not None:
        in_specs.append(pl.BlockSpec(memory_space=pl.ANY))
        args.append(gh)
    return pl.pallas_call(
        input_kernel,
        grid=(p // t,),
        in_specs=in_specs,
        out_specs=pl.BlockSpec((mloc, h, t), lambda s: (0, 0, off + s)),
        out_shape=jax.ShapeDtypeStruct((mloc, h, n), jnp.bfloat16),
        input_output_aliases={} if gh is None else {2: 0},
        compiler_params=pltpu.CompilerParams(vmem_limit_bytes=VMEM),
        cost_estimate=pl.CostEstimate(
            flops=2 * h * h, bytes_accessed=2 * h * h, transcendentals=0
        ),
        name="grad_hidden_part",
    )(*args)


def after(value, *others):
    return lax.optimization_barrier((value,) + others)[0]


def shards(hidden, target, area, var_weight, w_inner, b_inner, w_out, b_out):
    mloc, h, n = hidden.shape
    n_mem = lax.axis_size("mem")
    n_grid = lax.axis_size("grid")
    members = mloc * n_mem
    npoints = n * n_grid
    v = w_out.shape[0]
    vp = 128
    n_lo = 2
    while n_lo * n_lo * 4 <= n_grid:
        n_lo *= 2
    n_hi = n_grid // n_lo

    swap_x = [(i, (i + n_mem // 2) % n_mem) for i in range(n_mem)]
    swap_core = [(i, i ^ 1) for i in range(n_mem)]

    def shift_lo(k):
        return [(a * n_lo + b, a * n_lo + (b + k) % n_lo) for a in range(n_hi) for b in range(n_lo)]

    def shift_hi(k):
        return [(a * n_lo + b, (a + k) % n_hi * n_lo + b) for a in range(n_hi) for b in range(n_lo)]

    to_x = lambda a: lax.ppermute(a, "mem", swap_x)
    to_core = lambda a: lax.ppermute(a, "mem", swap_core)
    to_lo = lambda a, k: lax.ppermute(a, "grid", shift_lo(k))
    to_hi = lambda a, k: lax.ppermute(a, "grid", shift_hi(k))

    unit = n // sum(EIGHTHS)
    starts = [unit * sum(EIGHTHS[:k]) for k in range(len(EIGHTHS))]
    spans = [(start, unit * size) for start, size in zip(starts, EIGHTHS)]
    parts = [
        forward(start, p, hidden, w_inner, b_inner.reshape(1, h), w_out, b_out.reshape(1, v))
        for start, p in spans
    ]
    far = [to_x(fields) for _, _, fields in parts]
    near = [to_core(fields) for _, _, fields in parts]
    w_out = after(w_out, parts[1][2])
    wot = jnp.pad(w_out * jnp.bfloat16(0.5), ((0, vp - v), (0, 0))).T
    vw, area = var_weight.reshape(1, v), area.reshape(1, n)
    acc = extra = gh = None
    grad_pre = []
    for k, (start, p) in enumerate(spans):
        act, slope, fields = parts[k]
        first, last = k == 0, k == len(spans) - 1
        if k >= 2:
            far[k] = after(far[k], grad_pre[k - 2])
        gp, extra, *accs = backward(
            start, p, first, last, (n_hi, n_lo), members,
            (fields, near[k], far[k], to_core(far[k])),
            (target, area, vw, act, slope, hidden, wot), acc, extra,
        )
        grad_pre.append(gp)
        acc = accs[0]
    keep_a, send_a, keep_x, send_x = accs
    wt = after(w_inner, extra).T

    def gathered(block, axis, name, bit):
        n = lax.axis_size(name)
        other = lax.ppermute(block, name, [(i, i ^ bit) for i in range(n)])
        return jnp.where(
            lax.axis_index(name) & bit == 0,
            jnp.concatenate([block, other], axis),
            jnp.concatenate([other, block], axis),
        )

    def along_lo(blocks, own):
        return sum([to_lo(blocks[k], k) for k in range(1, n_lo)], own[0])

    def beside(k, gh, start_after, wait_for):
        gh = input_gradient(*spans[k], n, wt, after(grad_pre[k], start_after), gh)
        return lax.optimization_barrier((gh, wait_for))

    r = h // (2 * n_grid)
    ca, cx = keep_a.shape[-1], keep_x.shape[-1]
    got_x = to_core(send_x)
    got_a = to_core(send_a)
    from_x = to_x(keep_x[1] + got_x[1])
    here_a = [keep_a[k] + got_a[k] for k in range(n_lo)]
    sum_a = along_lo(here_a, here_a)
    gh, keep_x = beside(0, gh, here_a[1], keep_x)
    own_x = keep_x[0] + got_x[0] + from_x
    own_x = [own_x[k] for k in range(n_lo)]
    gh, last_x = beside(2, gh, own_x[1], own_x[0])
    sum_x = along_lo(own_x, [last_x])
    pieces = [
        jnp.concatenate([sum_a[k, :r, c : c + cx] for c in range(0, ca, cx)] + [sum_x[k]], 0)
        for k in range(n_hi)
    ]
    from_hi = [to_hi(pieces[k], k) for k in range(1, n_hi)]
    gh, own = beside(1, gh, pieces[1], pieces[0])

    extra = sum_a[:, r:]
    extra = extra + to_x(extra)
    bit = n_lo
    while bit < n_grid:
        extra = extra + lax.ppermute(extra, "grid", [(i, i ^ bit) for i in range(n_grid)])
        bit *= 2

    total = after(sum(from_hi, own), extra)
    far = to_x(total)
    extra = extra[None]
    bit = 1
    while bit < n_lo:
        extra = gathered(extra, 0, "grid", bit)
        bit *= 2
    extra = gathered(extra[None], 0, "mem", 1)
    extra = extra.reshape(2, n_lo, n_hi, h // ca, EXTRA_ROWS, ca).transpose(0, 2, 1, 4, 3, 5)
    extra = extra.reshape(2 * n_grid * EXTRA_ROWS, h)

    done = h // cx // 2 * r
    both = total[:done] + far[:done]
    left, right = total[done:], far[done:]
    x = lax.axis_index("mem") // 2
    ends = [both[k : k + r] for k in range(0, done, r)]
    ends += [jnp.where(x == 0, left, right), jnp.where(x == 0, right, left)]
    scale = 1.0 / math.sqrt(members * npoints)
    grad_inner = gathered(jnp.concatenate(ends, 1) * scale, 0, "mem", 1)
    loss = jnp.sum(extra[v]) / npoints
    return (loss, gh, grad_inner, extra[:v] * (0.5 * scale))


def solution(mesh):
    in_specs = (P("mem", None, "grid"), P(None, "grid"), P("grid"), P(), P(), P(), P(), P())
    out_specs = (P(), P("mem", None, "grid"), P("grid", None), P())
    return jax.shard_map(shards, mesh=mesh, in_specs=in_specs, out_specs=out_specs, check_vma=False)
```

```python
import functools
import math

import jax
import jax.numpy as jnp
from jax import lax
from jax.experimental import pallas as pl
from jax.experimental.pallas import tpu as pltpu
from jax.sharding import PartitionSpec as P

EIGHTHS = (3, 3, 2)
TILE = 256
EPS = 0.0004
K0 = math.sqrt(2.0 / math.pi)
K1 = K0 * 0.044715
SLAB = 512
EXTRA_ROWS = 8
VMEM = 8 * 1024 * 1024
NT = (((1,), (1,)), ((), ()))


def column(row, size):
    r = lax.broadcasted_iota(jnp.int32, (size, size), 0)
    c = lax.broadcasted_iota(jnp.int32, (size, size), 1)
    return jnp.sum(jnp.where(r == c, row, 0.0), axis=1, keepdims=True)


def field_rows(v, mloc, m, r0):
    full = v // 8 * 8
    if r0 < full:
        return pl.ds(m * full + r0, 8)
    return pl.ds(mloc * full + m * (v - full), v - full)


def forward_kernel(mloc, hid_ref, w_ref, b_ref, wo_ref, bo_ref, act_ref, slope_ref, f_ref, bias, half, even, odd):
    step = pl.program_id(0)

    @pl.when(step == 0)
    def _():
        for k in range(bias.shape[0] // 128):
            bias[pl.ds(k * 128, 128), :] = jnp.broadcast_to(
                column(b_ref[:, pl.ds(k * 128, 128)], 128), (128, 128)
            )

        half[...] = wo_ref[...] * jnp.bfloat16(0.5)

    tile = lax.max(step - 1, 0) // mloc

    def both(m, fill, drain):
        h, t = fill.shape
        out = jnp.broadcast_to(column(bo_ref[...], bo_ref.shape[1]), (bo_ref.shape[1], t))
        for k in range(0, h, SLAB):
            slab = pl.ds(k, SLAB)
            fill[slab, :] = jnp.dot(
                w_ref[slab, :], hid_ref[0], preferred_element_type=jnp.float32
            )
            for r in range(k, k + SLAB, 16):
                rows = pl.ds(r, 16)
                x = drain[rows, :] + jnp.concatenate([bias[rows, :]] * (t // 128), axis=1)
                q = x * x * K1
                th = jnp.tanh(x * (K0 + q))
                up = 1.0 + th
                act = x * up
                act_ref[tile, m, rows, :] = act.astype(jnp.bfloat16)
                slope_ref[tile, m, rows, :] = up + act * ((1.0 - th) * (K0 + 3.0 * q))
            out = out + jnp.dot(
                half[:, slab], act_ref[tile, m, slab, :], preferred_element_type=jnp.float32
            )
        for r0 in range(0, out.shape[0], 8):
            f_ref[field_rows(out.shape[0], mloc, m, r0), :] = out[r0 : r0 + 8]

    @pl.when(step % 2 == 0)
    def _():
        both(1, even, odd)

    @pl.when(step % 2 == 1)
    def _():
        both(0, odd, even)


def forward(start, p, hidden, w_inner, b_inner, w_out, b_out):
    mloc, h, n = hidden.shape
    v = w_out.shape[0]
    t = TILE
    tiles = mloc * (p // t)
    assert mloc == 2
    whole = lambda s: (0, 0)
    once = pl.Buffered(1)

    def ahead(s):
        s = jnp.minimum(s, tiles - 1)
        return (s % mloc, 0, start // t + s // mloc)

    shape = (p // t, mloc, h, t)
    held = pl.BlockSpec(shape, lambda s: (0, 0, 0, 0))
    return pl.pallas_call(
        functools.partial(forward_kernel, mloc),
        grid=(tiles + 1,),
        in_specs=[
            pl.BlockSpec((1, h, t), ahead),
            pl.BlockSpec((h, h), whole, pipeline_mode=once),
            pl.BlockSpec((1, h), whole, pipeline_mode=once),
            pl.BlockSpec((v, h), whole, pipeline_mode=once),
            pl.BlockSpec((1, v), whole, pipeline_mode=once),
        ],
        out_specs=[
            held,
            held,
            pl.BlockSpec((mloc * v, t), lambda s: (0, jnp.maximum(s - 1, 0) // mloc)),
        ],
        out_shape=[
            pltpu.VMEM(shape, jnp.bfloat16),
            pltpu.VMEM(shape, jnp.float32),
            jax.ShapeDtypeStruct((mloc * v, p), jnp.float32),
        ],
        scratch_shapes=[
            pltpu.VMEM((h, 128), jnp.float32),
            pltpu.VMEM((v, h), jnp.bfloat16),
            pltpu.VMEM((h, t), jnp.float32),
            pltpu.VMEM((h, t), jnp.float32),
        ],
        compiler_params=pltpu.CompilerParams(vmem_limit_bytes=VMEM),
        cost_estimate=pl.CostEstimate(
            flops=2 * mloc * p * h * (h + v), bytes_accessed=mloc * p * h * 8 + 2 * h * h,
            transcendentals=mloc * p * h,
        ),
        name="forward_part",
    )(hidden, w_inner, b_inner, w_out, b_out)


def backward_kernel(
    first, last, dims, members,
    f_ref, fc_ref, fx_ref, fxc_ref, target_ref, area_ref, vw_ref, act_ref, slope_ref, hid_ref,
    wot_ref, acc_in, extra_in, gp_ref, extra_ref, *refs,
):
    acc, *refs = refs
    if last:
        keep_a, send_a, keep_x, send_x, *refs = refs
    (gf,) = refs
    step = pl.program_id(0)
    mloc, _, t = hid_ref.shape
    v = target_ref.shape[0]
    h = wot_ref.shape[0]
    denom = members * (members - 1)
    vw = column(vw_ref[...], v)
    area = area_ref[...]
    loss = jnp.zeros((1, t), jnp.float32)
    for r0 in range(0, v, 8):
        rows = pl.ds(r0, min(8, v - r0))
        places = [field_rows(v, mloc, m, r0) for m in range(mloc)]
        own = [f_ref[place, :] for place in places]
        others = [ref[place, :] for ref in (fc_ref, fx_ref, fxc_ref) for place in places]
        target = target_ref[rows, :]
        dsum = [None] * mloc
        obs = []
        cross = jnp.zeros_like(target)
        inner = jnp.zeros_like(target)
        near = jnp.zeros_like(target)
        n_cross = n_inner = 0

        def pair(a, b):
            d = a - b
            s = d * d + EPS
            r = lax.rsqrt(s)
            return d * r, s * r

        def add(m, value):
            dsum[m] = value if dsum[m] is None else dsum[m] + value

        for i in range(mloc):
            sl, ph = pair(own[i], target)
            obs.append(sl)
            near = near + ph
            for b in others:
                sl, ph = pair(own[i], b)
                add(i, sl)
                cross = cross + ph
                n_cross += 1
            for j in range(i + 1, mloc):
                sl, ph = pair(own[i], own[j])
                add(i, sl)
                add(j, -sl)
                inner = inner + ph
                n_inner += 1
        weight = vw[r0 : r0 + 8] * area
        for m in range(mloc):
            gf[m, rows, :] = weight * (obs[m] * (1.0 / members) - dsum[m] * (1.0 / denom))
        near = (near - 0.02 * mloc) * (1.0 / members)
        pairs = (inner - 0.02 * n_inner) + 0.5 * (cross - 0.02 * n_cross)
        loss = loss + jnp.sum(weight * (near - pairs * (1.0 / denom)), axis=0, keepdims=True)
    for m in range(mloc):
        gf[m, pl.ds(v, gf.shape[1] - v), :] = jnp.zeros((gf.shape[1] - v, t), jnp.float32)

    g = jnp.concatenate([gf[m] for m in range(mloc)], axis=1).astype(jnp.bfloat16)
    for k in range(0, h, 256):
        rows = pl.ds(k, 256)
        ga = jnp.dot(wot_ref[rows, :], g, preferred_element_type=jnp.float32)
        for m in range(mloc):
            piece = (ga[:, m * t : (m + 1) * t] * slope_ref[step, m, rows, :]).astype(jnp.bfloat16)
            gp_ref[step, rows, pl.ds(m * t, t)] = piece
    hid = jnp.concatenate([hid_ref[m] for m in range(mloc)], axis=1)
    act = jnp.concatenate([act_ref[step, m] for m in range(mloc)], axis=1)
    extra = lax.dot_general(g, act, NT, preferred_element_type=jnp.float32)

    def accumulate(base, extra_base):
        extra_ref[...] = extra if extra_base is None else extra_base[...] + extra
        for k in range(0, h, SLAB):
            rows = pl.ds(k, SLAB)
            prod = lax.dot_general(gp_ref[step, rows, :], hid, NT, preferred_element_type=jnp.float32)
            acc[rows, :] = prod if base is None else base[rows, :] + prod

    @pl.when(step == 0)
    def _():
        accumulate(acc_in, extra_in)

    @pl.when(step > 0)
    def _():
        accumulate(acc, extra_ref)

    extra_ref[pl.ds(v, 1), pl.ds(0, t)] += loss
    if last:
        n_hi, n_lo = dims

        @pl.when(step == pl.num_programs(0) - 1)
        def _():
            mem = lax.axis_index("mem")
            grid = lax.axis_index("grid")
            x, core = mem // 2, mem % 2
            hi, lo = grid // n_lo, grid % n_lo
            r = h // (2 * n_hi * n_lo)
            ca = keep_a.shape[3]
            cx = keep_x.shape[4]
            for dlo in range(n_lo):
                for dhi in range(n_hi):
                    g = lax.rem(hi + dhi, n_hi) * n_lo + lax.rem(lo + dlo, n_lo)
                    for c, part_a, part_x in ((core, keep_a, keep_x), (1 - core, send_a, send_x)):
                        r0 = pl.multiple_of((g * 2 + c) * r, r)
                        total = acc[pl.ds(r0, r), :]
                        part_a[dlo, dhi, pl.ds(0, r), :] = total[:, :ca]
                        e0 = dhi * n_lo + lax.rem(lo + dlo, n_lo)
                        e0 = (c * (n_hi * n_lo) + e0) * EXTRA_ROWS
                        at = pl.multiple_of(
                            jnp.minimum(e0, extra_ref.shape[0] - EXTRA_ROWS), EXTRA_ROWS
                        )
                        for k in range(h // ca):
                            e = extra_ref[pl.ds(at, EXTRA_ROWS), pl.ds(k * ca, ca)]
                            part_a[dlo, dhi, pl.ds(r + k * EXTRA_ROWS, EXTRA_ROWS), :] = jnp.where(
                                e0 < extra_ref.shape[0], e, 0.0
                            )
                        left = total[:, ca : ca + cx]
                        right = total[:, ca + cx :]
                        part_x[0, dlo, dhi] = jnp.where(x == 0, left, right)
                        part_x[1, dlo, dhi] = jnp.where(x == 0, right, left)


def backward(start, p, first, last, dims, members, fields, rest, acc, extra):
    target, area, vw, act, slope, hidden, wot = rest
    mloc, h, n = hidden.shape
    v = target.shape[0]
    vp = wot.shape[1]
    t = TILE
    off = start // t
    once = pl.Buffered(1)
    f_spec = pl.BlockSpec((mloc * v, t), lambda s: (0, s))
    whole = lambda s: (0, 0)
    const = lambda a: pl.BlockSpec(a.shape, whole, pipeline_mode=once)
    held = lambda a: pl.BlockSpec(a.shape, lambda s: (0,) * len(a.shape))
    in_specs = [f_spec] * 4 + [
        pl.BlockSpec((v, t), lambda s: (0, off + s)),
        pl.BlockSpec((1, t), lambda s: (0, off + s)),
        const(vw), held(act), held(slope),
        pl.BlockSpec((mloc, h, t), lambda s: (0, 0, off + s)),
        const(wot),
    ]
    act, slope = (pltpu.with_memory_space_constraint(a, pltpu.VMEM) for a in (act, slope))
    args = [*fields, target, area, vw, act, slope, hidden, wot]
    kernel = functools.partial(backward_kernel, first, last, dims, members)
    if first:
        kernel_fn = lambda *refs: kernel(*refs[:11], None, None, *refs[11:])
        aliases = {}
    else:
        kernel_fn = kernel
        in_specs += [held(acc), const(extra)]
        args += [acc, extra]
        aliases = {11: 2}
    out_shape = [
        pltpu.VMEM((p // t, h, mloc * t), jnp.bfloat16),
        jax.ShapeDtypeStruct((vp, h), jnp.float32),
        pltpu.VMEM((h, h), jnp.float32),
    ]
    if last:
        n_hi, n_lo = dims
        r = h // (2 * n_hi * n_lo)
        ca = h // 2
        cx = (h - ca) // 2
        ra = r + h // ca * EXTRA_ROWS
        out_shape += [pltpu.VMEM((n_lo, n_hi, ra, ca), jnp.float32)] * 2
        out_shape += [pltpu.VMEM((2, n_lo, n_hi, r, cx), jnp.float32)] * 2
    out_specs = [held(a) for a in out_shape]
    return pl.pallas_call(
        kernel_fn,
        grid=(p // t,),
        in_specs=in_specs,
        out_specs=out_specs,
        out_shape=out_shape,
        scratch_shapes=[pltpu.VMEM((mloc, vp, t), jnp.float32)],
        input_output_aliases=aliases,
        compiler_params=pltpu.CompilerParams(vmem_limit_bytes=VMEM),
        cost_estimate=pl.CostEstimate(
            flops=2 * mloc * p * h * (h + 2 * v), bytes_accessed=mloc * p * h * 10 + 10 * h * h,
            transcendentals=mloc * p * v * 8,
        ),
        name="backward_part",
    )(*args)


def input_kernel(wt_ref, gp_ref, *refs):
    mloc, h, t = refs[-1].shape
    for k in range(0, h, SLAB):
        rows = pl.ds(k, SLAB)
        out = jnp.dot(wt_ref[rows, :], gp_ref[pl.program_id(0)], preferred_element_type=jnp.float32)
        for m in range(mloc):
            refs[-1][m, rows, :] = out[:, m * t : (m + 1) * t].astype(jnp.bfloat16)


def input_gradient(start, p, n, wt, gp, gh):
    steps, h, width = gp.shape
    t = TILE
    mloc = width // t
    off = start // t
    in_specs = [
        pl.BlockSpec((h, h), lambda s: (0, 0), pipeline_mode=pl.Buffered(1)),
        pl.BlockSpec(gp.shape, lambda s: (0, 0, 0)),
    ]
    args = [wt, gp]
    if gh is not None:
        in_specs.append(pl.BlockSpec(memory_space=pl.ANY))
        args.append(gh)
    return pl.pallas_call(
        input_kernel,
        grid=(steps,),
        in_specs=in_specs,
        out_specs=pl.BlockSpec((mloc, h, t), lambda s: (0, 0, off + s)),
        out_shape=jax.ShapeDtypeStruct((mloc, h, n), jnp.bfloat16),
        input_output_aliases={} if gh is None else {2: 0},
        compiler_params=pltpu.CompilerParams(vmem_limit_bytes=VMEM),
        cost_estimate=pl.CostEstimate(
            flops=2 * h * h, bytes_accessed=2 * h * h, transcendentals=0
        ),
        name="grad_hidden_part",
    )(*args)


def after(value, *others):
    return lax.optimization_barrier((value,) + others)[0]


def shards(hidden, target, area, var_weight, w_inner, b_inner, w_out, b_out):
    mloc, h, n = hidden.shape
    n_mem = lax.axis_size("mem")
    n_grid = lax.axis_size("grid")
    members = mloc * n_mem
    npoints = n * n_grid
    v = w_out.shape[0]
    vp = 128
    n_lo = 2
    while n_lo * n_lo * 4 <= n_grid:
        n_lo *= 2
    n_hi = n_grid // n_lo

    swap_x = [(i, (i + n_mem // 2) % n_mem) for i in range(n_mem)]
    swap_core = [(i, i ^ 1) for i in range(n_mem)]

    def shift_lo(k):
        return [(a * n_lo + b, a * n_lo + (b + k) % n_lo) for a in range(n_hi) for b in range(n_lo)]

    def shift_hi(k):
        return [(a * n_lo + b, (a + k) % n_hi * n_lo + b) for a in range(n_hi) for b in range(n_lo)]

    to_x = lambda a: lax.ppermute(a, "mem", swap_x)
    to_core = lambda a: lax.ppermute(a, "mem", swap_core)
    to_lo = lambda a, k: lax.ppermute(a, "grid", shift_lo(k))
    to_hi = lambda a, k: lax.ppermute(a, "grid", shift_hi(k))

    hidden = pltpu.with_memory_space_constraint(hidden, pltpu.HBM)
    unit = n // sum(EIGHTHS)
    starts = [unit * sum(EIGHTHS[:k]) for k in range(len(EIGHTHS))]
    spans = [(start, unit * size) for start, size in zip(starts, EIGHTHS)]
    parts = [
        forward(start, p, hidden, w_inner, b_inner.reshape(1, h), w_out, b_out.reshape(1, v))
        for start, p in spans
    ]
    far = [to_x(fields) for _, _, fields in parts]
    near = [to_core(fields) for _, _, fields in parts]
    w_out = after(w_out, parts[1][2])
    wot = jnp.pad(w_out * jnp.bfloat16(0.5), ((0, vp - v), (0, 0))).T
    vw, area = var_weight.reshape(1, v), area.reshape(1, n)
    acc = extra = gh = None
    grad_pre = []
    for k, (start, p) in enumerate(spans):
        act, slope, fields = parts[k]
        first, last = k == 0, k == len(spans) - 1
        if k >= 2:
            far[k] = after(far[k], grad_pre[k - 2])
        gp, extra, acc, *accs = backward(
            start, p, first, last, (n_hi, n_lo), members,
            (fields, near[k], far[k], to_core(far[k])),
            (target, area, vw, act, slope, hidden, wot), acc, extra,
        )
        grad_pre.append(gp)
    keep_a, send_a, keep_x, send_x = accs
    wt = after(w_inner, extra).T

    def gathered(block, axis, name, bit):
        n = lax.axis_size(name)
        other = lax.ppermute(block, name, [(i, i ^ bit) for i in range(n)])
        return jnp.where(
            lax.axis_index(name) & bit == 0,
            jnp.concatenate([block, other], axis),
            jnp.concatenate([other, block], axis),
        )

    def along_lo(blocks, own):
        return sum([to_lo(blocks[k], k) for k in range(1, n_lo)], own[0])

    def beside(k, gh, start_after, wait_for):
        gh = input_gradient(*spans[k], n, wt, after(grad_pre[k], start_after), gh)
        return lax.optimization_barrier((gh, wait_for))

    r = h // (2 * n_grid)
    ca, cx = keep_a.shape[-1], keep_x.shape[-1]
    got_x = to_core(send_x)
    got_a = to_core(send_a)
    from_x = to_x(keep_x[1] + got_x[1])
    here_a = [keep_a[k] + got_a[k] for k in range(n_lo)]
    sum_a = along_lo(here_a, here_a)
    gh, keep_x = beside(0, gh, here_a[1], keep_x)
    own_x = keep_x[0] + got_x[0] + from_x
    own_x = [own_x[k] for k in range(n_lo)]
    gh, last_x = beside(2, gh, own_x[1], own_x[0])
    sum_x = along_lo(own_x, [last_x])
    pieces = [
        jnp.concatenate([sum_a[k, :r, c : c + cx] for c in range(0, ca, cx)] + [sum_x[k]], 0)
        for k in range(n_hi)
    ]
    from_hi = [to_hi(pieces[k], k) for k in range(1, n_hi)]
    gh, own = beside(1, gh, pieces[1], pieces[0])

    extra = sum_a[:, r:]
    extra = extra + to_x(extra)
    bit = n_lo
    while bit < n_grid:
        extra = extra + lax.ppermute(extra, "grid", [(i, i ^ bit) for i in range(n_grid)])
        bit *= 2

    total = after(sum(from_hi, own), extra)
    far = to_x(total)
    extra = extra[None]
    bit = 1
    while bit < n_lo:
        extra = gathered(extra, 0, "grid", bit)
        bit *= 2
    extra = gathered(extra[None], 0, "mem", 1)
    extra = extra.reshape(2, n_lo, n_hi, h // ca, EXTRA_ROWS, ca).transpose(0, 2, 1, 4, 3, 5)
    extra = extra.reshape(2 * n_grid * EXTRA_ROWS, h)

    done = h // cx // 2 * r
    both = total[:done] + far[:done]
    left, right = total[done:], far[done:]
    x = lax.axis_index("mem") // 2
    ends = [both[k : k + r] for k in range(0, done, r)]
    ends += [jnp.where(x == 0, left, right), jnp.where(x == 0, right, left)]
    scale = 1.0 / math.sqrt(members * npoints)
    grad_inner = gathered(jnp.concatenate(ends, 1) * scale, 0, "mem", 1)
    loss = jnp.sum(extra[v]) / npoints
    return (loss, gh, grad_inner, extra[:v] * (0.5 * scale))


def solution(mesh):
    in_specs = (P("mem", None, "grid"), P(None, "grid"), P("grid"), P(), P(), P(), P(), P())
    out_specs = (P(), P("mem", None, "grid"), P("grid", None), P())
    return jax.shard_map(shards, mesh=mesh, in_specs=in_specs, out_specs=out_specs, check_vma=False)
```

```python
import functools
import math

import jax
import jax.numpy as jnp
from jax import lax
from jax.experimental import pallas as pl
from jax.experimental.pallas import tpu as pltpu
from jax.sharding import PartitionSpec as P

EIGHTHS = (3, 3, 2)
TILE = 256
EPS = 0.0004
K0 = math.sqrt(2.0 / math.pi)
K1 = K0 * 0.044715
SLAB = 512
EXTRA_ROWS = 8
VMEM = 8 * 1024 * 1024
NT = (((1,), (1,)), ((), ()))


def column(row, size):
    r = lax.broadcasted_iota(jnp.int32, (size, size), 0)
    c = lax.broadcasted_iota(jnp.int32, (size, size), 1)
    return jnp.sum(jnp.where(r == c, row, 0.0), axis=1, keepdims=True)


def field_rows(v, mloc, m, r0):
    full = v // 8 * 8
    if r0 < full:
        return pl.ds(m * full + r0, 8)
    return pl.ds(mloc * full + m * (v - full), v - full)


def forward_kernel(mloc, hid_ref, w_ref, b_ref, wo_ref, bo_ref, act_ref, slope_ref, f_ref, bias, half, even, odd):
    step = pl.program_id(0)

    @pl.when(step == 0)
    def _():
        for k in range(bias.shape[0] // 128):
            bias[pl.ds(k * 128, 128), :] = jnp.broadcast_to(
                column(b_ref[:, pl.ds(k * 128, 128)], 128), (128, 128)
            )

        half[...] = wo_ref[...] * jnp.bfloat16(0.5)

    tile = lax.max(step - 1, 0) // mloc

    def both(m, fill, drain):
        h, t = fill.shape
        out = jnp.broadcast_to(column(bo_ref[...], bo_ref.shape[1]), (bo_ref.shape[1], t))
        for k in range(0, h, SLAB):
            slab = pl.ds(k, SLAB)
            fill[slab, :] = jnp.dot(
                w_ref[slab, :], hid_ref[0], preferred_element_type=jnp.float32
            )
            for r in range(k, k + SLAB, 16):
                rows = pl.ds(r, 16)
                x = drain[rows, :] + jnp.concatenate([bias[rows, :]] * (t // 128), axis=1)
                q = x * x * K1
                th = jnp.tanh(x * (K0 + q))
                up = 1.0 + th
                act = x * up
                act_ref[tile, m, rows, :] = act.astype(jnp.bfloat16)
                slope_ref[tile, m, rows, :] = up + act * ((1.0 - th) * (K0 + 3.0 * q))
            out = out + jnp.dot(
                half[:, slab], act_ref[tile, m, slab, :], preferred_element_type=jnp.float32
            )
        for r0 in range(0, out.shape[0], 8):
            f_ref[field_rows(out.shape[0], mloc, m, r0), :] = out[r0 : r0 + 8]

    @pl.when(step % 2 == 0)
    def _():
        both(1, even, odd)

    @pl.when(step % 2 == 1)
    def _():
        both(0, odd, even)


def forward(start, p, hidden, w_inner, b_inner, w_out, b_out):
    mloc, h, n = hidden.shape
    v = w_out.shape[0]
    t = TILE
    tiles = mloc * (p // t)
    assert mloc == 2
    whole = lambda s: (0, 0)
    once = pl.Buffered(1)

    def ahead(s):
        s = jnp.minimum(s, tiles - 1)
        return (s % mloc, 0, start // t + s // mloc)

    shape = (p // t, mloc, h, t)
    held = pl.BlockSpec(shape, lambda s: (0, 0, 0, 0))
    return pl.pallas_call(
        functools.partial(forward_kernel, mloc),
        grid=(tiles + 1,),
        in_specs=[
            pl.BlockSpec((1, h, t), ahead),
            pl.BlockSpec((h, h), whole, pipeline_mode=once),
            pl.BlockSpec((1, h), whole, pipeline_mode=once),
            pl.BlockSpec((v, h), whole, pipeline_mode=once),
            pl.BlockSpec((1, v), whole, pipeline_mode=once),
        ],
        out_specs=[
            held,
            held,
            pl.BlockSpec((mloc * v, t), lambda s: (0, jnp.maximum(s - 1, 0) // mloc)),
        ],
        out_shape=[
            pltpu.VMEM(shape, jnp.bfloat16),
            pltpu.VMEM(shape, jnp.float32),
            jax.ShapeDtypeStruct((mloc * v, p), jnp.float32),
        ],
        scratch_shapes=[
            pltpu.VMEM((h, 128), jnp.float32),
            pltpu.VMEM((v, h), jnp.bfloat16),
            pltpu.VMEM((h, t), jnp.float32),
            pltpu.VMEM((h, t), jnp.float32),
        ],
        compiler_params=pltpu.CompilerParams(vmem_limit_bytes=VMEM),
        cost_estimate=pl.CostEstimate(
            flops=2 * mloc * p * h * (h + v), bytes_accessed=mloc * p * h * 8 + 2 * h * h,
            transcendentals=mloc * p * h,
        ),
        name="forward_part",
    )(hidden, w_inner, b_inner, w_out, b_out)


def backward_kernel(
    first, last, dims, members,
    f_ref, fc_ref, fx_ref, fxc_ref, target_ref, area_ref, vw_ref, act_ref, slope_ref, hid_ref,
    wot_ref, acc_in, extra_in, gp_ref, extra_ref, *refs,
):
    acc, *refs = refs
    if last:
        keep_a, send_a, keep_x, send_x, *refs = refs
    (gf,) = refs
    step = pl.program_id(0)
    mloc, _, t = hid_ref.shape
    v = target_ref.shape[0]
    h = wot_ref.shape[0]
    denom = members * (members - 1)
    vw = column(vw_ref[...], v)
    area = area_ref[...]
    loss = jnp.zeros((1, t), jnp.float32)
    for r0 in range(0, v, 8):
        rows = pl.ds(r0, min(8, v - r0))
        places = [field_rows(v, mloc, m, r0) for m in range(mloc)]
        own = [f_ref[place, :] for place in places]
        others = [ref[place, :] for ref in (fc_ref, fx_ref, fxc_ref) for place in places]
        target = target_ref[rows, :]
        dsum = [None] * mloc
        obs = []
        cross = jnp.zeros_like(target)
        inner = jnp.zeros_like(target)
        near = jnp.zeros_like(target)
        n_cross = n_inner = 0

        def pair(a, b):
            d = a - b
            s = d * d + EPS
            r = lax.rsqrt(s)
            return d * r, s * r

        def add(m, value):
            dsum[m] = value if dsum[m] is None else dsum[m] + value

        for i in range(mloc):
            sl, ph = pair(own[i], target)
            obs.append(sl)
            near = near + ph
            for b in others:
                sl, ph = pair(own[i], b)
                add(i, sl)
                cross = cross + ph
                n_cross += 1
            for j in range(i + 1, mloc):
                sl, ph = pair(own[i], own[j])
                add(i, sl)
                add(j, -sl)
                inner = inner + ph
                n_inner += 1
        weight = vw[r0 : r0 + 8] * area
        for m in range(mloc):
            gf[m, rows, :] = weight * (obs[m] * (1.0 / members) - dsum[m] * (1.0 / denom))
        near = (near - 0.02 * mloc) * (1.0 / members)
        pairs = (inner - 0.02 * n_inner) + 0.5 * (cross - 0.02 * n_cross)
        loss = loss + jnp.sum(weight * (near - pairs * (1.0 / denom)), axis=0, keepdims=True)
    for m in range(mloc):
        gf[m, pl.ds(v, gf.shape[1] - v), :] = jnp.zeros((gf.shape[1] - v, t), jnp.float32)

    g = jnp.concatenate([gf[m] for m in range(mloc)], axis=1).astype(jnp.bfloat16)
    for k in range(0, h, 256):
        rows = pl.ds(k, 256)
        ga = jnp.dot(wot_ref[rows, :], g, preferred_element_type=jnp.float32)
        for m in range(mloc):
            piece = (ga[:, m * t : (m + 1) * t] * slope_ref[step, m, rows, :]).astype(jnp.bfloat16)
            gp_ref[step, rows, pl.ds(m * t, t)] = piece
    hid = jnp.concatenate([hid_ref[m] for m in range(mloc)], axis=1)
    act = jnp.concatenate([act_ref[step, m] for m in range(mloc)], axis=1)
    extra = lax.dot_general(g, act, NT, preferred_element_type=jnp.float32)

    def accumulate(base, extra_base):
        extra_ref[...] = extra if extra_base is None else extra_base[...] + extra
        for k in range(0, h, SLAB):
            rows = pl.ds(k, SLAB)
            prod = lax.dot_general(gp_ref[step, rows, :], hid, NT, preferred_element_type=jnp.float32)
            acc[rows, :] = prod if base is None else base[rows, :] + prod

    @pl.when(step == 0)
    def _():
        accumulate(acc_in, extra_in)

    @pl.when(step > 0)
    def _():
        accumulate(acc, extra_ref)

    extra_ref[pl.ds(v, 1), pl.ds(0, t)] += loss
    if last:
        n_hi, n_lo = dims

        @pl.when(step == pl.num_programs(0) - 1)
        def _():
            mem = lax.axis_index("mem")
            grid = lax.axis_index("grid")
            x, core = mem // 2, mem % 2
            hi, lo = grid // n_lo, grid % n_lo
            r = h // (2 * n_hi * n_lo)
            ca = keep_a.shape[3]
            cx = keep_x.shape[4]
            for dlo in range(n_lo):
                for dhi in range(n_hi):
                    g = lax.rem(hi + dhi, n_hi) * n_lo + lax.rem(lo + dlo, n_lo)
                    block = dhi * n_lo + lax.rem(lo + dlo, n_lo)
                    for c, part_a, part_x in ((core, keep_a, keep_x), (1 - core, send_a, send_x)):
                        r0 = pl.multiple_of((g * 2 + c) * r, r)
                        total = acc[pl.ds(r0, r), :]
                        part_a[dlo, dhi] = total[:, :ca]
                        e0 = (c * (n_hi * n_lo) + block) * EXTRA_ROWS
                        at = pl.multiple_of(
                            jnp.minimum(e0, extra_ref.shape[0] - EXTRA_ROWS), EXTRA_ROWS
                        )
                        e = jnp.where(
                            e0 < extra_ref.shape[0], extra_ref[pl.ds(at, EXTRA_ROWS), :], 0.0
                        )
                        for d in range(2):
                            own = x == 0 if d == 0 else x == 1
                            part_x[d, dlo, dhi, pl.ds(0, r), :] = jnp.where(
                                own, total[:, ca : ca + cx], total[:, ca + cx :]
                            )
                            side = jnp.where(own, e[:, : h // 2], e[:, h // 2 :])
                            for k in range(h // 2 // cx):
                                part_x[d, dlo, dhi, pl.ds(r + k * EXTRA_ROWS, EXTRA_ROWS), :] = (
                                    side[:, k * cx : (k + 1) * cx]
                                )


def backward(start, p, first, last, dims, members, fields, rest, acc, extra):
    target, area, vw, act, slope, hidden, wot = rest
    mloc, h, n = hidden.shape
    v = target.shape[0]
    vp = wot.shape[1]
    t = TILE
    off = start // t
    once = pl.Buffered(1)
    f_spec = pl.BlockSpec((mloc * v, t), lambda s: (0, s))
    whole = lambda s: (0, 0)
    const = lambda a: pl.BlockSpec(a.shape, whole, pipeline_mode=once)
    held = lambda a: pl.BlockSpec(a.shape, lambda s: (0,) * len(a.shape))
    in_specs = [f_spec] * 4 + [
        pl.BlockSpec((v, t), lambda s: (0, off + s)),
        pl.BlockSpec((1, t), lambda s: (0, off + s)),
        const(vw), held(act), held(slope),
        pl.BlockSpec((mloc, h, t), lambda s: (0, 0, off + s)),
        const(wot),
    ]
    act, slope = (pltpu.with_memory_space_constraint(a, pltpu.VMEM) for a in (act, slope))
    args = [*fields, target, area, vw, act, slope, hidden, wot]
    kernel = functools.partial(backward_kernel, first, last, dims, members)
    if first:
        kernel_fn = lambda *refs: kernel(*refs[:11], None, None, *refs[11:])
        aliases = {}
    else:
        kernel_fn = kernel
        in_specs += [held(acc), const(extra)]
        args += [acc, extra]
        aliases = {11: 2}
    out_shape = [
        pltpu.VMEM((p // t, h, mloc * t), jnp.bfloat16),
        jax.ShapeDtypeStruct((vp, h), jnp.float32),
        pltpu.VMEM((h, h), jnp.float32),
    ]
    if last:
        n_hi, n_lo = dims
        r = h // (2 * n_hi * n_lo)
        ca = h // 2
        cx = (h - ca) // 2
        rx = r + h // 2 // cx * EXTRA_ROWS
        out_shape += [pltpu.VMEM((n_lo, n_hi, r, ca), jnp.float32)] * 2
        out_shape += [pltpu.VMEM((2, n_lo, n_hi, rx, cx), jnp.float32)] * 2
    out_specs = [held(a) for a in out_shape]
    return pl.pallas_call(
        kernel_fn,
        grid=(p // t,),
        in_specs=in_specs,
        out_specs=out_specs,
        out_shape=out_shape,
        scratch_shapes=[pltpu.VMEM((mloc, vp, t), jnp.float32)],
        input_output_aliases=aliases,
        compiler_params=pltpu.CompilerParams(vmem_limit_bytes=VMEM),
        cost_estimate=pl.CostEstimate(
            flops=2 * mloc * p * h * (h + 2 * v), bytes_accessed=mloc * p * h * 10 + 10 * h * h,
            transcendentals=mloc * p * v * 8,
        ),
        name="backward_part",
    )(*args)


def transposes_kernel(w_ref, wo_ref, wt_ref, wot_ref):
    wt_ref[...] = w_ref[...].astype(jnp.float32).T.astype(jnp.bfloat16)

    @pl.when(pl.program_id(0) == 0)
    def _():
        v, h = wo_ref.shape
        rows = jnp.concatenate(
            [wo_ref[...].astype(jnp.float32) * 0.5, jnp.zeros((wot_ref.shape[1] - v, h), jnp.float32)], 0
        )
        wot_ref[...] = rows.T.astype(jnp.bfloat16)


def transposes(w_inner, w_out, vp):
    v, h = w_out.shape
    t = TILE
    return pl.pallas_call(
        transposes_kernel,
        grid=(h // t,),
        in_specs=[
            pl.BlockSpec((t, h), lambda s: (s, 0)),
            pl.BlockSpec((v, h), lambda s: (0, 0)),
        ],
        out_specs=[
            pl.BlockSpec((h, t), lambda s: (0, s)),
            pl.BlockSpec((h, vp), lambda s: (0, 0)),
        ],
        out_shape=[pltpu.VMEM((h, h), jnp.bfloat16), pltpu.VMEM((h, vp), jnp.bfloat16)],
        compiler_params=pltpu.CompilerParams(vmem_limit_bytes=VMEM),
        name="transposes",
    )(w_inner, w_out)


def input_kernel(wt_ref, gp_ref, *refs):
    mloc, h, t = refs[-1].shape
    for k in range(0, h, SLAB):
        rows = pl.ds(k, SLAB)
        out = jnp.dot(wt_ref[rows, :], gp_ref[pl.program_id(0)], preferred_element_type=jnp.float32)
        for m in range(mloc):
            refs[-1][m, rows, :] = out[:, m * t : (m + 1) * t].astype(jnp.bfloat16)


def input_gradient(start, p, n, wt, gp, gh):
    steps, h, width = gp.shape
    t = TILE
    mloc = width // t
    off = start // t
    in_specs = [
        pl.BlockSpec((h, h), lambda s: (0, 0), pipeline_mode=pl.Buffered(1)),
        pl.BlockSpec(gp.shape, lambda s: (0, 0, 0)),
    ]
    args = [wt, gp]
    if gh is not None:
        in_specs.append(pl.BlockSpec(memory_space=pl.ANY))
        args.append(gh)
    return pl.pallas_call(
        input_kernel,
        grid=(steps,),
        in_specs=in_specs,
        out_specs=pl.BlockSpec((mloc, h, t), lambda s: (0, 0, off + s)),
        out_shape=jax.ShapeDtypeStruct((mloc, h, n), jnp.bfloat16),
        input_output_aliases={} if gh is None else {2: 0},
        compiler_params=pltpu.CompilerParams(vmem_limit_bytes=VMEM),
        cost_estimate=pl.CostEstimate(
            flops=2 * h * h, bytes_accessed=2 * h * h, transcendentals=0
        ),
        name="grad_hidden_part",
    )(*args)


def after(value, *others):
    return lax.optimization_barrier((value,) + others)[0]


def shards(hidden, target, area, var_weight, w_inner, b_inner, w_out, b_out):
    mloc, h, n = hidden.shape
    n_mem = lax.axis_size("mem")
    n_grid = lax.axis_size("grid")
    members = mloc * n_mem
    npoints = n * n_grid
    v = w_out.shape[0]
    vp = 128
    n_lo = 2
    while n_lo * n_lo * 4 <= n_grid:
        n_lo *= 2
    n_hi = n_grid // n_lo

    swap_x = [(i, (i + n_mem // 2) % n_mem) for i in range(n_mem)]
    swap_core = [(i, i ^ 1) for i in range(n_mem)]

    def shift_lo(k):
        return [(a * n_lo + b, a * n_lo + (b + k) % n_lo) for a in range(n_hi) for b in range(n_lo)]

    def shift_hi(k):
        return [(a * n_lo + b, (a + k) % n_hi * n_lo + b) for a in range(n_hi) for b in range(n_lo)]

    to_x = lambda a: lax.ppermute(a, "mem", swap_x)
    to_core = lambda a: lax.ppermute(a, "mem", swap_core)
    to_lo = lambda a, k: lax.ppermute(a, "grid", shift_lo(k))
    to_hi = lambda a, k: lax.ppermute(a, "grid", shift_hi(k))

    mem, grid = lax.axis_index("mem"), lax.axis_index("grid")
    at_zero = {("mem", bit): mem & bit == 0 for bit in (1, n_mem // 2)}
    bit = 1
    while bit < n_lo:
        at_zero["grid", bit] = grid & bit == 0
        bit *= 2
    hidden, at_zero = lax.optimization_barrier((hidden, at_zero))
    hidden, w_out, b_inner, b_out = (
        pltpu.with_memory_space_constraint(a, pltpu.HBM)
        for a in (hidden, w_out, b_inner.reshape(1, h), b_out.reshape(1, v))
    )
    unit = n // sum(EIGHTHS)
    starts = [unit * sum(EIGHTHS[:k]) for k in range(len(EIGHTHS))]
    spans = [(start, unit * size) for start, size in zip(starts, EIGHTHS)]
    parts = [
        forward(start, p, hidden, w_inner, b_inner, w_out, b_out)
        for start, p in spans
    ]
    far = [to_x(fields) for _, _, fields in parts]
    near = [to_core(fields) for _, _, fields in parts]
    wt, wot = transposes(after(w_inner, parts[-1][2]), w_out, vp)
    vw, area = var_weight.reshape(1, v), area.reshape(1, n)
    acc = extra = gh = None
    grad_pre = []
    for k, (start, p) in enumerate(spans):
        act, slope, fields = parts[k]
        first, last = k == 0, k == len(spans) - 1
        if k >= 2:
            far[k] = after(far[k], grad_pre[k - 2])
        gp, extra, acc, *accs = backward(
            start, p, first, last, (n_hi, n_lo), members,
            (fields, near[k], far[k], to_core(far[k])),
            (target, area, vw, act, slope, hidden, wot), acc, extra,
        )
        grad_pre.append(gp)
    keep_a, send_a, keep_x, send_x = accs

    def gathered(block, axis, name, bit):
        n = lax.axis_size(name)
        other = lax.ppermute(block, name, [(i, i ^ bit) for i in range(n)])
        return ordered(block, other, axis, name, bit)

    def ordered(block, other, axis, name, bit):
        return jnp.where(
            at_zero[name, bit],
            jnp.concatenate([block, other], axis),
            jnp.concatenate([other, block], axis),
        )

    def along_lo(blocks, own):
        return sum([to_lo(blocks[k], k) for k in range(1, n_lo)], own[0])

    def beside(k, gh, start_after, wait_for):
        gh = input_gradient(*spans[k], n, wt, after(grad_pre[k], start_after), gh)
        return lax.optimization_barrier((gh, wait_for))

    r = h // (2 * n_grid)
    ca, cx = keep_a.shape[-1], keep_x.shape[-1]
    got_x = to_core(send_x)
    got_a = to_core(send_a)
    from_x = to_x(keep_x[1] + got_x[1])
    here_a = [keep_a[k] + got_a[k] for k in range(n_lo)]
    sum_a = along_lo(here_a, here_a)
    gh, keep_x = beside(0, gh, here_a[1], keep_x)
    own_x = keep_x[0] + got_x[0] + from_x
    own_x = [own_x[k] for k in range(n_lo)]
    gh, last_x = beside(2, gh, own_x[1], own_x[0])
    sum_x = along_lo(own_x, [last_x])
    extra = sum_x[:, r:].reshape(-1, cx)
    pieces = [
        jnp.concatenate(
            [sum_a[k][:, c : c + cx] for c in range(0, ca, cx)] + [sum_x[k, :r], extra], 0
        )
        for k in range(n_hi)
    ]
    from_hi = [to_hi(pieces[k], k) for k in range(1, n_hi)]
    gh, own = beside(1, gh, pieces[1], pieces[0])
    total = sum(from_hi, own)
    far = to_x(total)

    na, nx = ca // cx * r, (ca // cx + 1) * r
    both = total[:na] + far[:na]
    ends = [both[k : k + r] for k in range(0, na, r)]
    ends.append(ordered(total[na:nx], far[na:nx], 1, "mem", n_mem // 2))
    scale = 1.0 / math.sqrt(members * npoints)
    grad_inner = gathered(jnp.concatenate(ends, 1) * scale, 0, "mem", 1)

    extra = ordered(total[nx:][None], far[nx:][None], 0, "mem", n_mem // 2)
    extra = extra[None]
    bit = 1
    while bit < n_lo:
        extra = gathered(extra, 0, "grid", bit)
        bit *= 2
    extra = gathered(extra[None], 0, "mem", 1)
    extra = extra.reshape(2, n_lo, 2, n_hi, h // 2 // cx, EXTRA_ROWS, cx)
    extra = extra.transpose(0, 3, 1, 5, 2, 4, 6).reshape(2 * n_grid * EXTRA_ROWS, h)
    loss = jnp.sum(extra[v]) / npoints
    return (loss, gh, grad_inner, extra[:v] * (0.5 * scale))


def solution(mesh):
    in_specs = (P("mem", None, "grid"), P(None, "grid"), P("grid"), P(), P(), P(), P(), P())
    out_specs = (P(), P("mem", None, "grid"), P("grid", None), P())
    return jax.shard_map(shards, mesh=mesh, in_specs=in_specs, out_specs=out_specs, check_vma=False)
```

```python
import functools
import math

import jax
import jax.numpy as jnp
from jax import lax
from jax.experimental import pallas as pl
from jax.experimental.pallas import tpu as pltpu
from jax.sharding import PartitionSpec as P

EIGHTHS = (2, 3, 3)
TILE = 256
EPS = 0.0004
K0 = math.sqrt(2.0 / math.pi)
K1 = K0 * 0.044715
SLAB = 512
EXTRA_ROWS = 8
VMEM = 8 * 1024 * 1024
NT = (((1,), (1,)), ((), ()))


def column(row, size):
    r = lax.broadcasted_iota(jnp.int32, (size, size), 0)
    c = lax.broadcasted_iota(jnp.int32, (size, size), 1)
    return jnp.sum(jnp.where(r == c, row, 0.0), axis=1, keepdims=True)


def field_rows(v, mloc, m, r0):
    full = v // 8 * 8
    if r0 < full:
        return pl.ds(m * full + r0, 8)
    return pl.ds(mloc * full + m * (v - full), v - full)


def forward_kernel(mloc, hid_ref, w_ref, b_ref, wo_ref, bo_ref, act_ref, slope_ref, f_ref, bias, half, even, odd):
    step = pl.program_id(0)

    @pl.when(step == 0)
    def _():
        for k in range(bias.shape[0] // 128):
            bias[pl.ds(k * 128, 128), :] = jnp.broadcast_to(
                column(b_ref[:, pl.ds(k * 128, 128)], 128), (128, 128)
            )

        half[...] = wo_ref[...] * jnp.bfloat16(0.5)

    tile = lax.max(step - 1, 0) // mloc

    def both(m, fill, drain):
        h, t = fill.shape
        out = jnp.broadcast_to(column(bo_ref[...], bo_ref.shape[1]), (bo_ref.shape[1], t))
        for k in range(0, h, SLAB):
            slab = pl.ds(k, SLAB)
            fill[slab, :] = jnp.dot(
                w_ref[slab, :], hid_ref[0], preferred_element_type=jnp.float32
            )
            for r in range(k, k + SLAB, 16):
                rows = pl.ds(r, 16)
                x = drain[rows, :] + jnp.concatenate([bias[rows, :]] * (t // 128), axis=1)
                q = x * x * K1
                th = jnp.tanh(x * (K0 + q))
                up = 1.0 + th
                act = x * up
                act_ref[tile, m, rows, :] = act.astype(jnp.bfloat16)
                slope_ref[tile, m, rows, :] = up + act * ((1.0 - th) * (K0 + 3.0 * q))
            out = out + jnp.dot(
                half[:, slab], act_ref[tile, m, slab, :], preferred_element_type=jnp.float32
            )
        for r0 in range(0, out.shape[0], 8):
            f_ref[field_rows(out.shape[0], mloc, m, r0), :] = out[r0 : r0 + 8]

    @pl.when(step % 2 == 0)
    def _():
        both(1, even, odd)

    @pl.when(step % 2 == 1)
    def _():
        both(0, odd, even)


def forward(start, p, hidden, w_inner, b_inner, w_out, b_out):
    mloc, h, n = hidden.shape
    v = w_out.shape[0]
    t = TILE
    tiles = mloc * (p // t)
    assert mloc == 2
    whole = lambda s: (0, 0)
    once = pl.Buffered(1)

    def ahead(s):
        s = jnp.minimum(s, tiles - 1)
        return (s % mloc, 0, start // t + s // mloc)

    shape = (p // t, mloc, h, t)
    held = pl.BlockSpec(shape, lambda s: (0, 0, 0, 0))
    return pl.pallas_call(
        functools.partial(forward_kernel, mloc),
        grid=(tiles + 1,),
        in_specs=[
            pl.BlockSpec((1, h, t), ahead),
            pl.BlockSpec((h, h), whole, pipeline_mode=once),
            pl.BlockSpec((1, h), whole, pipeline_mode=once),
            pl.BlockSpec((v, h), whole, pipeline_mode=once),
            pl.BlockSpec((1, v), whole, pipeline_mode=once),
        ],
        out_specs=[
            held,
            held,
            pl.BlockSpec((mloc * v, t), lambda s: (0, jnp.maximum(s - 1, 0) // mloc)),
        ],
        out_shape=[
            pltpu.VMEM(shape, jnp.bfloat16),
            pltpu.VMEM(shape, jnp.float32),
            jax.ShapeDtypeStruct((mloc * v, p), jnp.float32),
        ],
        scratch_shapes=[
            pltpu.VMEM((h, 128), jnp.float32),
            pltpu.VMEM((v, h), jnp.bfloat16),
            pltpu.VMEM((h, t), jnp.float32),
            pltpu.VMEM((h, t), jnp.float32),
        ],
        compiler_params=pltpu.CompilerParams(vmem_limit_bytes=VMEM),
        cost_estimate=pl.CostEstimate(
            flops=2 * h * h, bytes_accessed=2 * h * h, transcendentals=0
        ),
        name="forward_part",
    )(hidden, w_inner, b_inner, w_out, b_out)


def backward_kernel(
    first, last, dims, members,
    f_ref, fc_ref, fx_ref, fxc_ref, target_ref, area_ref, vw_ref, act_ref, slope_ref, hid_ref,
    wot_ref, acc_in, extra_in, gp_ref, extra_ref, *refs,
):
    acc, *refs = refs
    if last:
        keep_x, send_x, keep_y, send_y, *refs = refs
    (gf,) = refs
    step = pl.program_id(0)
    mloc, _, t = hid_ref.shape
    v = target_ref.shape[0]
    h = wot_ref.shape[0]
    denom = members * (members - 1)
    vw = column(vw_ref[...], v)
    area = area_ref[...]
    loss = jnp.zeros((1, t), jnp.float32)
    for r0 in range(0, v, 8):
        rows = pl.ds(r0, min(8, v - r0))
        places = [field_rows(v, mloc, m, r0) for m in range(mloc)]
        own = [f_ref[place, :] for place in places]
        others = [ref[place, :] for ref in (fc_ref, fx_ref, fxc_ref) for place in places]
        target = target_ref[rows, :]
        dsum = [None] * mloc
        obs = []
        cross = jnp.zeros_like(target)
        inner = jnp.zeros_like(target)
        near = jnp.zeros_like(target)
        n_cross = n_inner = 0

        def pair(a, b):
            d = a - b
            s = d * d + EPS
            r = lax.rsqrt(s)
            return d * r, s * r

        def add(m, value):
            dsum[m] = value if dsum[m] is None else dsum[m] + value

        for i in range(mloc):
            sl, ph = pair(own[i], target)
            obs.append(sl)
            near = near + ph
            for b in others:
                sl, ph = pair(own[i], b)
                add(i, sl)
                cross = cross + ph
                n_cross += 1
            for j in range(i + 1, mloc):
                sl, ph = pair(own[i], own[j])
                add(i, sl)
                add(j, -sl)
                inner = inner + ph
                n_inner += 1
        weight = vw[r0 : r0 + 8] * area
        for m in range(mloc):
            gf[m, rows, :] = weight * (obs[m] * (1.0 / members) - dsum[m] * (1.0 / denom))
        near = (near - 0.02 * mloc) * (1.0 / members)
        pairs = (inner - 0.02 * n_inner) + 0.5 * (cross - 0.02 * n_cross)
        loss = loss + jnp.sum(weight * (near - pairs * (1.0 / denom)), axis=0, keepdims=True)
    for m in range(mloc):
        gf[m, pl.ds(v, gf.shape[1] - v), :] = jnp.zeros((gf.shape[1] - v, t), jnp.float32)

    g = jnp.concatenate([gf[m] for m in range(mloc)], axis=1).astype(jnp.bfloat16)
    for k in range(0, h, 256):
        rows = pl.ds(k, 256)
        ga = jnp.dot(wot_ref[rows, :], g, preferred_element_type=jnp.float32)
        for m in range(mloc):
            piece = (ga[:, m * t : (m + 1) * t] * slope_ref[step, m, rows, :]).astype(jnp.bfloat16)
            gp_ref[step, rows, pl.ds(m * t, t)] = piece
    hid = jnp.concatenate([hid_ref[m] for m in range(mloc)], axis=1)
    act = jnp.concatenate([act_ref[step, m] for m in range(mloc)], axis=1)
    extra = lax.dot_general(g, act, NT, preferred_element_type=jnp.float32)

    def accumulate(base, extra_base):
        extra_ref[...] = extra if extra_base is None else extra_base[...] + extra
        for k in range(0, h, SLAB):
            rows = pl.ds(k, SLAB)
            prod = lax.dot_general(gp_ref[step, rows, :], hid, NT, preferred_element_type=jnp.float32)
            acc[rows, :] = prod if base is None else base[rows, :] + prod

    @pl.when(step == 0)
    def _():
        accumulate(acc_in, extra_in)

    @pl.when(step > 0)
    def _():
        accumulate(acc, extra_ref)

    extra_ref[pl.ds(v, 1), pl.ds(0, t)] += loss
    if last:
        n_hi, n_lo = dims

        @pl.when(step == pl.num_programs(0) - 1)
        def _():
            mem = lax.axis_index("mem")
            grid = lax.axis_index("grid")
            x, core = mem // 2, mem % 2
            hi, lo = grid // n_lo, grid % n_lo
            r = h // (2 * n_hi * n_lo)
            cx = keep_x.shape[4]
            for dlo in range(n_lo):
                for dhi in range(n_hi):
                    g = lax.rem(hi + dhi, n_hi) * n_lo + lax.rem(lo + dlo, n_lo)
                    block = dhi * n_lo + lax.rem(lo + dlo, n_lo)
                    for c, to_x, to_y in ((core, keep_x, keep_y), (1 - core, send_x, send_y)):
                        r0 = pl.multiple_of((g * 2 + c) * r, r)
                        total = acc[pl.ds(r0, r), :]
                        e0 = (c * (n_hi * n_lo) + block) * EXTRA_ROWS
                        at = pl.multiple_of(
                            jnp.minimum(e0, extra_ref.shape[0] - EXTRA_ROWS), EXTRA_ROWS
                        )
                        e = jnp.where(
                            e0 < extra_ref.shape[0], extra_ref[pl.ds(at, EXTRA_ROWS), :], 0.0
                        )
                        for values, rows in ((total, pl.ds(0, r)), (e, pl.ds(r, EXTRA_ROWS))):
                            q = [values[:, k * cx : (k + 1) * cx] for k in range(4)]
                            for d in range(2):
                                own = x == d
                                to_x[d, dlo, dhi, rows, :] = jnp.where(own, q[0], q[1])
                                to_y[dlo, d, dhi, rows, :] = jnp.where(own, q[2], q[3])


def backward(start, p, first, last, dims, members, fields, rest, acc, extra):
    target, area, vw, act, slope, hidden, wot = rest
    mloc, h, n = hidden.shape
    v = target.shape[0]
    vp = wot.shape[1]
    t = TILE
    off = start // t
    once = pl.Buffered(1)
    f_spec = pl.BlockSpec((mloc * v, t), lambda s: (0, s))
    whole = lambda s: (0, 0)
    const = lambda a: pl.BlockSpec(a.shape, whole, pipeline_mode=once)
    held = lambda a: pl.BlockSpec(a.shape, lambda s: (0,) * len(a.shape))
    in_specs = [f_spec] * 4 + [
        pl.BlockSpec((v, t), lambda s: (0, off + s)),
        pl.BlockSpec((1, t), lambda s: (0, off + s)),
        const(vw), held(act), held(slope),
        pl.BlockSpec((mloc, h, t), lambda s: (0, 0, off + s)),
        const(wot),
    ]
    act, slope = (pltpu.with_memory_space_constraint(a, pltpu.VMEM) for a in (act, slope))
    args = [*fields, target, area, vw, act, slope, hidden, wot]
    kernel = functools.partial(backward_kernel, first, last, dims, members)
    if first:
        kernel_fn = lambda *refs: kernel(*refs[:11], None, None, *refs[11:])
        aliases = {}
    else:
        kernel_fn = kernel
        in_specs += [held(acc), const(extra)]
        args += [acc, extra]
        aliases = {11: 2}
    out_shape = [
        pltpu.VMEM((p // t, h, mloc * t), jnp.bfloat16),
        jax.ShapeDtypeStruct((vp, h), jnp.float32),
        pltpu.VMEM((h, h), jnp.float32),
    ]
    if last:
        n_hi, n_lo = dims
        r = h // (2 * n_hi * n_lo)
        cx = h // 4
        out_shape += [pltpu.VMEM((2, n_lo, n_hi, r + EXTRA_ROWS, cx), jnp.float32)] * 2
        out_shape += [pltpu.VMEM((n_lo, 2, n_hi, r + EXTRA_ROWS, cx), jnp.float32)] * 2
    out_specs = [held(a) for a in out_shape]
    return pl.pallas_call(
        kernel_fn,
        grid=(p // t,),
        in_specs=in_specs,
        out_specs=out_specs,
        out_shape=out_shape,
        scratch_shapes=[pltpu.VMEM((mloc, vp, t), jnp.float32)],
        input_output_aliases=aliases,
        compiler_params=pltpu.CompilerParams(vmem_limit_bytes=VMEM),
        cost_estimate=pl.CostEstimate(
            flops=2 * h * h, bytes_accessed=2 * h * h, transcendentals=0
        ),
        name="backward_part",
    )(*args)


def transposes_kernel(w_ref, wo_ref, wt_ref, wot_ref):
    wt_ref[...] = w_ref[...].astype(jnp.float32).T.astype(jnp.bfloat16)

    @pl.when(pl.program_id(0) == 0)
    def _():
        v, h = wo_ref.shape
        rows = jnp.concatenate(
            [wo_ref[...].astype(jnp.float32) * 0.5, jnp.zeros((wot_ref.shape[1] - v, h), jnp.float32)], 0
        )
        wot_ref[...] = rows.T.astype(jnp.bfloat16)


def transposes(w_inner, w_out, vp):
    v, h = w_out.shape
    t = TILE
    return pl.pallas_call(
        transposes_kernel,
        grid=(h // t,),
        in_specs=[
            pl.BlockSpec((t, h), lambda s: (s, 0)),
            pl.BlockSpec((v, h), lambda s: (0, 0)),
        ],
        out_specs=[
            pl.BlockSpec((h, t), lambda s: (0, s)),
            pl.BlockSpec((h, vp), lambda s: (0, 0)),
        ],
        out_shape=[pltpu.VMEM((h, h), jnp.bfloat16), pltpu.VMEM((h, vp), jnp.bfloat16)],
        compiler_params=pltpu.CompilerParams(vmem_limit_bytes=VMEM),
        cost_estimate=pl.CostEstimate(flops=2 * h, bytes_accessed=2 * h, transcendentals=0),
        name="transposes",
    )(w_inner, w_out)


def input_kernel(wt_ref, gp_ref, *refs):
    mloc, h, t = refs[-1].shape
    for k in range(0, h, SLAB):
        rows = pl.ds(k, SLAB)
        out = jnp.dot(wt_ref[rows, :], gp_ref[pl.program_id(0)], preferred_element_type=jnp.float32)
        for m in range(mloc):
            refs[-1][m, rows, :] = out[:, m * t : (m + 1) * t].astype(jnp.bfloat16)


def input_gradient(start, p, n, wt, gp, gh):
    steps, h, width = gp.shape
    t = TILE
    mloc = width // t
    off = start // t
    in_specs = [
        pl.BlockSpec((h, h), lambda s: (0, 0), pipeline_mode=pl.Buffered(1)),
        pl.BlockSpec(gp.shape, lambda s: (0, 0, 0)),
    ]
    args = [wt, gp]
    if gh is not None:
        in_specs.append(pl.BlockSpec(memory_space=pl.ANY))
        args.append(gh)
    return pl.pallas_call(
        input_kernel,
        grid=(steps,),
        in_specs=in_specs,
        out_specs=pl.BlockSpec((mloc, h, t), lambda s: (0, 0, off + s)),
        out_shape=jax.ShapeDtypeStruct((mloc, h, n), jnp.bfloat16),
        input_output_aliases={} if gh is None else {2: 0},
        compiler_params=pltpu.CompilerParams(vmem_limit_bytes=VMEM),
        cost_estimate=pl.CostEstimate(
            flops=2 * h * h, bytes_accessed=2 * h * h, transcendentals=0
        ),
        name="grad_hidden_part",
    )(*args)


def after(value, *others):
    return lax.optimization_barrier((value,) + others)[0]


def shards(hidden, target, area, var_weight, w_inner, b_inner, w_out, b_out):
    mloc, h, n = hidden.shape
    n_mem = lax.axis_size("mem")
    n_grid = lax.axis_size("grid")
    members = mloc * n_mem
    npoints = n * n_grid
    v = w_out.shape[0]
    vp = 128
    n_lo = 2
    while n_lo * n_lo * 4 <= n_grid:
        n_lo *= 2
    n_hi = n_grid // n_lo

    swap_x = [(i, (i + n_mem // 2) % n_mem) for i in range(n_mem)]
    swap_core = [(i, i ^ 1) for i in range(n_mem)]

    def shift_lo(k):
        return [(a * n_lo + b, a * n_lo + (b + k) % n_lo) for a in range(n_hi) for b in range(n_lo)]

    def shift_hi(k):
        return [(a * n_lo + b, (a + k) % n_hi * n_lo + b) for a in range(n_hi) for b in range(n_lo)]

    to_x = lambda a: lax.ppermute(a, "mem", swap_x)
    to_core = lambda a: lax.ppermute(a, "mem", swap_core)
    to_lo = lambda a, k: lax.ppermute(a, "grid", shift_lo(k))
    to_hi = lambda a, k: lax.ppermute(a, "grid", shift_hi(k))

    mem, grid = lax.axis_index("mem"), lax.axis_index("grid")
    at_zero = {("mem", bit): mem & bit == 0 for bit in (1, n_mem // 2)}
    bit = 1
    while bit < n_lo:
        at_zero["grid", bit] = grid & bit == 0
        bit *= 2
    hidden, at_zero = lax.optimization_barrier((hidden, at_zero))
    hidden, w_out, b_inner, b_out = (
        pltpu.with_memory_space_constraint(a, pltpu.HBM)
        for a in (hidden, w_out, b_inner.reshape(1, h), b_out.reshape(1, v))
    )
    unit = n // sum(EIGHTHS)
    starts = [unit * sum(EIGHTHS[:k]) for k in range(len(EIGHTHS))]
    spans = [(start, unit * size) for start, size in zip(starts, EIGHTHS)]
    parts = []
    for start, p in spans:
        if parts:
            b_out = after(b_out, parts[-1][2])
        parts.append(forward(start, p, hidden, w_inner, b_inner, w_out, b_out))
    far = [to_x(fields) for _, _, fields in parts]
    near = [to_core(fields) for _, _, fields in parts]
    wt, wot = transposes(after(w_inner, parts[-1][2]), w_out, vp)
    vw, area = var_weight.reshape(1, v), area.reshape(1, n)
    acc = extra = gh = None
    grad_pre = []
    for k, (start, p) in enumerate(spans):
        act, slope, fields = parts[k]
        first, last = k == 0, k == len(spans) - 1
        if k:
            far[k] = after(far[k], parts[-1][2] if k == 1 else grad_pre[k - 2])
        gp, extra, acc, *accs = backward(
            start, p, first, last, (n_hi, n_lo), members,
            (fields, near[k], far[k], to_core(far[k])),
            (target, area, vw, act, slope, hidden, wot), acc, extra,
        )
        grad_pre.append(gp)
    keep_x, send_x, keep_y, send_y = accs

    def gathered(block, axis, name, bit):
        n = lax.axis_size(name)
        other = lax.ppermute(block, name, [(i, i ^ bit) for i in range(n)])
        return ordered(block, other, axis, name, bit)

    def ordered(block, other, axis, name, bit):
        return jnp.where(
            at_zero[name, bit],
            jnp.concatenate([block, other], axis),
            jnp.concatenate([other, block], axis),
        )

    def beside(k, gh, start_after, wait_for):
        gh = input_gradient(*spans[k], n, wt, after(grad_pre[k], start_after), gh)
        return lax.optimization_barrier((gh, wait_for))

    r, cx = h // (2 * n_grid), keep_x.shape[-1]
    others = range(1, n_lo)
    got_x = to_core(send_x)
    got_y = to_core(send_y)
    out_x = keep_x[1] + got_x[1]
    out_y = [keep_y[k] + got_y[k] for k in others]
    from_x = to_x(out_x)
    from_y = [to_lo(out_y[k - 1], k) for k in others]
    gh, (keep_x, keep_y) = beside(0, gh, (out_x, out_y), (keep_x, keep_y))
    own_x = keep_x[0] + got_x[0] + from_x
    own_y = sum(from_y, keep_y[0] + got_y[0])
    own_x, own_y = [own_x[k] for k in range(n_lo)], [own_y[k] for k in range(2)]
    from_y = [to_lo(own_x[k], k) for k in others]
    from_x = to_x(own_y[1])
    gh, (own_x, own_y) = beside(2, gh, (own_x[1:], own_y[1]), (own_x[0], own_y[0]))
    sums = [sum(from_y, own_x), own_y + from_x]

    extra = [part[:, r:].reshape(-1, cx) for part in sums]
    pieces = [jnp.concatenate([part[k, :r] for part in sums] + extra, 0) for k in range(n_hi)]
    from_hi = [to_hi(pieces[k], k) for k in range(1, n_hi)]
    gh, own = beside(1, gh, pieces[1:], pieces[0])
    total = sum(from_hi, own)
    far = to_x(total)

    scale = 1.0 / math.sqrt(members * npoints)
    halves = [ordered(total[k : k + r], far[k : k + r], 1, "mem", n_mem // 2) for k in (0, r)]
    grad_inner = gathered(jnp.concatenate(halves, 1) * scale, 0, "mem", 1)

    extra = ordered(total[2 * r :][None], far[2 * r :][None], 0, "mem", n_mem // 2)[None]
    bit = 1
    while bit < n_lo:
        extra = gathered(extra, 0, "grid", bit)
        bit *= 2
    extra = gathered(extra[None], 0, "mem", 1)
    extra = extra.reshape(2, n_lo, 2, 2, n_hi, EXTRA_ROWS, cx)
    extra = extra.transpose(0, 4, 1, 5, 3, 2, 6).reshape(2 * n_grid * EXTRA_ROWS, h)
    loss = jnp.sum(extra[v]) / npoints
    return (loss, gh, grad_inner, extra[:v] * (0.5 * scale))


def solution(mesh):
    in_specs = (P("mem", None, "grid"), P(None, "grid"), P("grid"), P(), P(), P(), P(), P())
    out_specs = (P(), P("mem", None, "grid"), P("grid", None), P())
    return jax.shard_map(shards, mesh=mesh, in_specs=in_specs, out_specs=out_specs, check_vma=False)
```

```python
import functools
import math

import jax
import jax.numpy as jnp
from jax import lax
from jax.experimental import pallas as pl
from jax.experimental.pallas import tpu as pltpu
from jax.sharding import PartitionSpec as P

EIGHTHS = (2, 2, 2, 2)
TILE = 256
EPS = 0.0004
K0 = math.sqrt(2.0 / math.pi)
K1 = K0 * 0.044715
SLAB = 512
EXTRA_ROWS = 8
VMEM = 8 * 1024 * 1024
NT = (((1,), (1,)), ((), ()))


def column(row, size):
    r = lax.broadcasted_iota(jnp.int32, (size, size), 0)
    c = lax.broadcasted_iota(jnp.int32, (size, size), 1)
    return jnp.sum(jnp.where(r == c, row, 0.0), axis=1, keepdims=True)


def field_rows(v, mloc, m, r0):
    full = v // 8 * 8
    if r0 < full:
        return pl.ds(m * full + r0, 8)
    return pl.ds(mloc * full + m * (v - full), v - full)


def forward_kernel(mloc, hid_ref, w_ref, b_ref, wo_ref, bo_ref, act_ref, slope_ref, f_ref, bias, half, even, odd):
    step = pl.program_id(0)

    @pl.when(step == 0)
    def _():
        for k in range(bias.shape[0] // 128):
            bias[pl.ds(k * 128, 128), :] = jnp.broadcast_to(
                column(b_ref[:, pl.ds(k * 128, 128)], 128), (128, 128)
            )

        half[...] = wo_ref[...] * jnp.bfloat16(0.5)

    tile = lax.max(step - 1, 0) // mloc

    def both(m, fill, drain):
        h, t = fill.shape
        out = jnp.broadcast_to(column(bo_ref[...], bo_ref.shape[1]), (bo_ref.shape[1], t))
        for k in range(0, h, SLAB):
            slab = pl.ds(k, SLAB)
            fill[slab, :] = jnp.dot(
                w_ref[slab, :], hid_ref[0], preferred_element_type=jnp.float32
            )
            for r in range(k, k + SLAB, 32):
                rows = pl.ds(r, 32)
                x = drain[rows, :] + jnp.concatenate([bias[rows, :]] * (t // 128), axis=1)
                q = x * x * K1
                th = jnp.tanh(x * (K0 + q))
                up = 1.0 + th
                act = x * up
                act_ref[tile, m, rows, :] = act.astype(jnp.bfloat16)
                slope_ref[tile, m, rows, :] = up + act * ((1.0 - th) * (K0 + 3.0 * q))
            out = out + jnp.dot(
                half[:, slab], act_ref[tile, m, slab, :], preferred_element_type=jnp.float32
            )
        for r0 in range(0, out.shape[0], 8):
            f_ref[field_rows(out.shape[0], mloc, m, r0), :] = out[r0 : r0 + 8]

    @pl.when(step % 2 == 0)
    def _():
        both(1, even, odd)

    @pl.when(step % 2 == 1)
    def _():
        both(0, odd, even)


def forward(start, p, hidden, w_inner, b_inner, w_out, b_out):
    mloc, h, n = hidden.shape
    v = w_out.shape[0]
    t = TILE
    tiles = mloc * (p // t)
    assert mloc == 2
    whole = lambda s: (0, 0)
    once = pl.Buffered(1)

    def ahead(s):
        s = jnp.minimum(s, tiles - 1)
        return (s % mloc, 0, start // t + s // mloc)

    shape = (p // t, mloc, h, t)
    held = pl.BlockSpec(shape, lambda s: (0, 0, 0, 0))
    return pl.pallas_call(
        functools.partial(forward_kernel, mloc),
        grid=(tiles + 1,),
        in_specs=[
            pl.BlockSpec((1, h, t), ahead),
            pl.BlockSpec((h, h), whole, pipeline_mode=once),
            pl.BlockSpec((1, h), whole, pipeline_mode=once),
            pl.BlockSpec((v, h), whole, pipeline_mode=once),
            pl.BlockSpec((1, v), whole, pipeline_mode=once),
        ],
        out_specs=[
            held,
            held,
            pl.BlockSpec((mloc * v, t), lambda s: (0, jnp.maximum(s - 1, 0) // mloc)),
        ],
        out_shape=[
            pltpu.VMEM(shape, jnp.bfloat16),
            pltpu.VMEM(shape, jnp.float32),
            jax.ShapeDtypeStruct((mloc * v, p), jnp.float32),
        ],
        scratch_shapes=[
            pltpu.VMEM((h, 128), jnp.float32),
            pltpu.VMEM((v, h), jnp.bfloat16),
            pltpu.VMEM((h, t), jnp.float32),
            pltpu.VMEM((h, t), jnp.float32),
        ],
        compiler_params=pltpu.CompilerParams(vmem_limit_bytes=VMEM),
        cost_estimate=pl.CostEstimate(
            flops=2 * h * h, bytes_accessed=2 * h * h, transcendentals=0
        ),
        name="forward_part",
    )(hidden, w_inner, b_inner, w_out, b_out)


def backward_kernel(
    first, last, dims, members,
    f_ref, fc_ref, fx_ref, fxc_ref, target_ref, area_ref, vw_ref, act_ref, slope_ref, hid_ref,
    wot_ref, acc_in, extra_in, gp_ref, extra_ref, *refs,
):
    acc, *refs = refs
    if last:
        keep_x, send_x, keep_y, send_y, *refs = refs
    (gf,) = refs
    step = pl.program_id(0)
    mloc, _, t = hid_ref.shape
    v = target_ref.shape[0]
    h = wot_ref.shape[0]
    denom = members * (members - 1)
    vw = column(vw_ref[...], v)
    area = area_ref[...]
    loss = jnp.zeros((1, t), jnp.float32)
    for r0 in range(0, v, 8):
        rows = pl.ds(r0, min(8, v - r0))
        places = [field_rows(v, mloc, m, r0) for m in range(mloc)]
        own = [f_ref[place, :] for place in places]
        others = [ref[place, :] for ref in (fc_ref, fx_ref, fxc_ref) for place in places]
        target = target_ref[rows, :]
        dsum = [None] * mloc
        obs = []
        cross = jnp.zeros_like(target)
        inner = jnp.zeros_like(target)
        near = jnp.zeros_like(target)
        n_cross = n_inner = 0

        def pair(a, b):
            d = a - b
            s = d * d + EPS
            r = lax.rsqrt(s)
            return d * r, s * r

        def add(m, value):
            dsum[m] = value if dsum[m] is None else dsum[m] + value

        for i in range(mloc):
            sl, ph = pair(own[i], target)
            obs.append(sl)
            near = near + ph
            for b in others:
                sl, ph = pair(own[i], b)
                add(i, sl)
                cross = cross + ph
                n_cross += 1
            for j in range(i + 1, mloc):
                sl, ph = pair(own[i], own[j])
                add(i, sl)
                add(j, -sl)
                inner = inner + ph
                n_inner += 1
        weight = vw[r0 : r0 + 8] * area
        for m in range(mloc):
            gf[m, rows, :] = weight * (obs[m] * (1.0 / members) - dsum[m] * (1.0 / denom))
        near = (near - 0.02 * mloc) * (1.0 / members)
        pairs = (inner - 0.02 * n_inner) + 0.5 * (cross - 0.02 * n_cross)
        loss = loss + jnp.sum(weight * (near - pairs * (1.0 / denom)), axis=0, keepdims=True)
    for m in range(mloc):
        gf[m, pl.ds(v, gf.shape[1] - v), :] = jnp.zeros((gf.shape[1] - v, t), jnp.float32)

    g = jnp.concatenate([gf[m] for m in range(mloc)], axis=1).astype(jnp.bfloat16)
    for k in range(0, h, 256):
        rows = pl.ds(k, 256)
        ga = jnp.dot(wot_ref[rows, :], g, preferred_element_type=jnp.float32)
        for m in range(mloc):
            piece = (ga[:, m * t : (m + 1) * t] * slope_ref[step, m, rows, :]).astype(jnp.bfloat16)
            gp_ref[step, rows, pl.ds(m * t, t)] = piece
    hid = jnp.concatenate([hid_ref[m] for m in range(mloc)], axis=1)
    act = jnp.concatenate([act_ref[step, m] for m in range(mloc)], axis=1)
    extra = lax.dot_general(g, act, NT, preferred_element_type=jnp.float32)

    def accumulate(base, extra_base):
        extra_ref[...] = extra if extra_base is None else extra_base[...] + extra
        for k in range(0, h, SLAB):
            rows = pl.ds(k, SLAB)
            prod = lax.dot_general(gp_ref[step, rows, :], hid, NT, preferred_element_type=jnp.float32)
            acc[rows, :] = prod if base is None else base[rows, :] + prod

    @pl.when(step == 0)
    def _():
        accumulate(acc_in, extra_in)

    @pl.when(step > 0)
    def _():
        accumulate(acc, extra_ref)

    extra_ref[pl.ds(v, 1), pl.ds(0, t)] += loss
    if last:
        n_hi, n_lo = dims

        @pl.when(step == pl.num_programs(0) - 1)
        def _():
            mem = lax.axis_index("mem")
            grid = lax.axis_index("grid")
            x, core = mem // 2, mem % 2
            hi, lo = grid // n_lo, grid % n_lo
            r = h // (2 * n_hi * n_lo)
            cx = keep_x.shape[4]
            for dlo in range(n_lo):
                for dhi in range(n_hi):
                    g = lax.rem(hi + dhi, n_hi) * n_lo + lax.rem(lo + dlo, n_lo)
                    block = dhi * n_lo + lax.rem(lo + dlo, n_lo)
                    for c, to_x, to_y in ((core, keep_x, keep_y), (1 - core, send_x, send_y)):
                        r0 = pl.multiple_of((g * 2 + c) * r, r)
                        total = acc[pl.ds(r0, r), :]
                        e0 = (c * (n_hi * n_lo) + block) * EXTRA_ROWS
                        at = pl.multiple_of(
                            jnp.minimum(e0, extra_ref.shape[0] - EXTRA_ROWS), EXTRA_ROWS
                        )
                        e = jnp.where(
                            e0 < extra_ref.shape[0], extra_ref[pl.ds(at, EXTRA_ROWS), :], 0.0
                        )
                        for values, rows in ((total, pl.ds(0, r)), (e, pl.ds(r, EXTRA_ROWS))):
                            q = [values[:, k * cx : (k + 1) * cx] for k in range(4)]
                            for d in range(2):
                                own = x == d
                                to_x[d, dlo, dhi, rows, :] = jnp.where(own, q[0], q[1])
                                to_y[dlo, d, dhi, rows, :] = jnp.where(own, q[2], q[3])


def backward(start, p, first, last, dims, members, fields, rest, acc, extra):
    target, area, vw, act, slope, hidden, wot = rest
    mloc, h, n = hidden.shape
    v = target.shape[0]
    vp = wot.shape[1]
    t = TILE
    off = start // t
    once = pl.Buffered(1)
    f_spec = pl.BlockSpec((mloc * v, t), lambda s: (0, s))
    whole = lambda s: (0, 0)
    const = lambda a: pl.BlockSpec(a.shape, whole, pipeline_mode=once)
    held = lambda a: pl.BlockSpec(a.shape, lambda s: (0,) * len(a.shape))
    in_specs = [f_spec] * 4 + [
        pl.BlockSpec((v, t), lambda s: (0, off + s)),
        pl.BlockSpec((1, t), lambda s: (0, off + s)),
        const(vw), held(act), held(slope),
        pl.BlockSpec((mloc, h, t), lambda s: (0, 0, off + s)),
        const(wot),
    ]
    act, slope = (pltpu.with_memory_space_constraint(a, pltpu.VMEM) for a in (act, slope))
    args = [*fields, target, area, vw, act, slope, hidden, wot]
    kernel = functools.partial(backward_kernel, first, last, dims, members)
    if first:
        kernel_fn = lambda *refs: kernel(*refs[:11], None, None, *refs[11:])
        aliases = {}
    else:
        kernel_fn = kernel
        in_specs += [held(acc), const(extra)]
        args += [acc, extra]
        aliases = {11: 2}
    out_shape = [
        pltpu.VMEM((p // t, h, mloc * t), jnp.bfloat16),
        jax.ShapeDtypeStruct((vp, h), jnp.float32),
        pltpu.VMEM((h, h), jnp.float32),
    ]
    if last:
        n_hi, n_lo = dims
        r = h // (2 * n_hi * n_lo)
        cx = h // 4
        out_shape += [pltpu.VMEM((2, n_lo, n_hi, r + EXTRA_ROWS, cx), jnp.float32)] * 2
        out_shape += [pltpu.VMEM((n_lo, 2, n_hi, r + EXTRA_ROWS, cx), jnp.float32)] * 2
    out_specs = [held(a) for a in out_shape]
    return pl.pallas_call(
        kernel_fn,
        grid=(p // t,),
        in_specs=in_specs,
        out_specs=out_specs,
        out_shape=out_shape,
        scratch_shapes=[pltpu.VMEM((mloc, vp, t), jnp.float32)],
        input_output_aliases=aliases,
        compiler_params=pltpu.CompilerParams(vmem_limit_bytes=VMEM),
        cost_estimate=pl.CostEstimate(
            flops=2 * h * h, bytes_accessed=2 * h * h, transcendentals=0
        ),
        name="backward_part",
    )(*args)


def transposes_kernel(w_ref, wo_ref, wt_ref, wot_ref):
    wt_ref[...] = w_ref[...].astype(jnp.float32).T.astype(jnp.bfloat16)

    @pl.when(pl.program_id(0) == 0)
    def _():
        v, h = wo_ref.shape
        rows = jnp.concatenate(
            [wo_ref[...].astype(jnp.float32) * 0.5, jnp.zeros((wot_ref.shape[1] - v, h), jnp.float32)], 0
        )
        wot_ref[...] = rows.T.astype(jnp.bfloat16)


def transposes(w_inner, w_out, vp):
    v, h = w_out.shape
    t = TILE
    return pl.pallas_call(
        transposes_kernel,
        grid=(h // t,),
        in_specs=[
            pl.BlockSpec((t, h), lambda s: (s, 0)),
            pl.BlockSpec((v, h), lambda s: (0, 0)),
        ],
        out_specs=[
            pl.BlockSpec((h, t), lambda s: (0, s)),
            pl.BlockSpec((h, vp), lambda s: (0, 0)),
        ],
        out_shape=[pltpu.VMEM((h, h), jnp.bfloat16), pltpu.VMEM((h, vp), jnp.bfloat16)],
        compiler_params=pltpu.CompilerParams(vmem_limit_bytes=VMEM),
        cost_estimate=pl.CostEstimate(flops=2 * h, bytes_accessed=2 * h, transcendentals=0),
        name="transposes",
    )(w_inner, w_out)


def input_kernel(wt_ref, gp_ref, *refs):
    mloc, h, t = refs[-1].shape
    for k in range(0, h, SLAB):
        rows = pl.ds(k, SLAB)
        out = jnp.dot(wt_ref[rows, :], gp_ref[pl.program_id(0)], preferred_element_type=jnp.float32)
        for m in range(mloc):
            refs[-1][m, rows, :] = out[:, m * t : (m + 1) * t].astype(jnp.bfloat16)


def input_gradient(start, p, n, wt, gp, gh):
    steps, h, width = gp.shape
    t = TILE
    mloc = width // t
    off = start // t
    in_specs = [
        pl.BlockSpec((h, h), lambda s: (0, 0), pipeline_mode=pl.Buffered(1)),
        pl.BlockSpec(gp.shape, lambda s: (0, 0, 0)),
    ]
    args = [wt, gp]
    if gh is not None:
        in_specs.append(pl.BlockSpec(memory_space=pl.ANY))
        args.append(gh)
    return pl.pallas_call(
        input_kernel,
        grid=(steps,),
        in_specs=in_specs,
        out_specs=pl.BlockSpec((mloc, h, t), lambda s: (0, 0, off + s)),
        out_shape=jax.ShapeDtypeStruct((mloc, h, n), jnp.bfloat16),
        input_output_aliases={} if gh is None else {2: 0},
        compiler_params=pltpu.CompilerParams(vmem_limit_bytes=VMEM),
        cost_estimate=pl.CostEstimate(
            flops=2 * h * h, bytes_accessed=2 * h * h, transcendentals=0
        ),
        name="grad_hidden_part",
    )(*args)


def after(value, *others):
    return lax.optimization_barrier((value,) + others)[0]


def shards(hidden, target, area, var_weight, w_inner, b_inner, w_out, b_out):
    mloc, h, n = hidden.shape
    n_mem = lax.axis_size("mem")
    n_grid = lax.axis_size("grid")
    members = mloc * n_mem
    npoints = n * n_grid
    v = w_out.shape[0]
    vp = 128
    n_lo = 2
    while n_lo * n_lo * 4 <= n_grid:
        n_lo *= 2
    n_hi = n_grid // n_lo

    swap_x = [(i, (i + n_mem // 2) % n_mem) for i in range(n_mem)]
    swap_core = [(i, i ^ 1) for i in range(n_mem)]

    def shift_lo(k):
        return [(a * n_lo + b, a * n_lo + (b + k) % n_lo) for a in range(n_hi) for b in range(n_lo)]

    def shift_hi(k):
        return [(a * n_lo + b, (a + k) % n_hi * n_lo + b) for a in range(n_hi) for b in range(n_lo)]

    to_x = lambda a: lax.ppermute(a, "mem", swap_x)
    to_core = lambda a: lax.ppermute(a, "mem", swap_core)
    to_lo = lambda a, k: lax.ppermute(a, "grid", shift_lo(k))
    to_hi = lambda a, k: lax.ppermute(a, "grid", shift_hi(k))

    mem, grid = lax.axis_index("mem"), lax.axis_index("grid")
    at_zero = {("mem", bit): mem & bit == 0 for bit in (1, n_mem // 2)}
    bit = 1
    while bit < n_lo:
        at_zero["grid", bit] = grid & bit == 0
        bit *= 2
    hidden, at_zero = lax.optimization_barrier((hidden, at_zero))
    hidden, w_out, b_inner, b_out = (
        pltpu.with_memory_space_constraint(a, pltpu.HBM)
        for a in (hidden, w_out, b_inner.reshape(1, h), b_out.reshape(1, v))
    )
    unit = n // sum(EIGHTHS)
    starts = [unit * sum(EIGHTHS[:k]) for k in range(len(EIGHTHS))]
    spans = [(start, unit * size) for start, size in zip(starts, EIGHTHS)]
    parts = []
    for start, p in spans:
        w = w_inner
        if parts:
            b_out = after(b_out, parts[-1][2])
        else:
            w = pltpu.with_memory_space_constraint(w_inner, pltpu.HBM)
        parts.append(forward(start, p, hidden, w, b_inner, w_out, b_out))
    far = [to_x(fields) for _, _, fields in parts]
    near = [to_core(fields) for _, _, fields in parts]
    wt, wot = transposes(after(w_inner, parts[-1][2]), w_out, vp)
    vw, area = var_weight.reshape(1, v), area.reshape(1, n)
    acc = extra = gh = None
    grad_pre = []
    for k, (start, p) in enumerate(spans):
        act, slope, fields = parts[k]
        first, last = k == 0, k == len(spans) - 1
        if k:
            far[k] = after(far[k], parts[-1][2] if k == 1 else grad_pre[k - 2])
        gp, extra, acc, *accs = backward(
            start, p, first, last, (n_hi, n_lo), members,
            (fields, near[k], far[k], to_core(far[k])),
            (target, area, vw, act, slope, hidden, wot), acc, extra,
        )
        grad_pre.append(gp)
    keep_x, send_x, keep_y, send_y = accs

    def gathered(block, axis, name, bit):
        n = lax.axis_size(name)
        other = lax.ppermute(block, name, [(i, i ^ bit) for i in range(n)])
        return ordered(block, other, axis, name, bit)

    def ordered(block, other, axis, name, bit):
        return jnp.where(
            at_zero[name, bit],
            jnp.concatenate([block, other], axis),
            jnp.concatenate([other, block], axis),
        )

    def beside(k, gh, start_after, wait_for):
        gh = input_gradient(*spans[k], n, wt, after(grad_pre[k], start_after), gh)
        return lax.optimization_barrier((gh, wait_for))

    r, cx = h // (2 * n_grid), keep_x.shape[-1]
    others = range(1, n_lo)
    got_x = to_core(send_x)
    got_y = to_core(send_y)
    out_x = keep_x[1] + got_x[1]
    out_y = [keep_y[k] + got_y[k] for k in others]
    from_x = to_x(out_x)
    from_y = [to_lo(out_y[k - 1], k) for k in others]
    gh, (keep_x, keep_y) = beside(0, gh, (out_x, out_y), (keep_x, keep_y))
    gh, (keep_x, keep_y) = beside(1, gh, (out_x, out_y), (keep_x, keep_y))
    own_x = keep_x[0] + got_x[0] + from_x
    own_y = sum(from_y, keep_y[0] + got_y[0])
    own_x, own_y = [own_x[k] for k in range(n_lo)], [own_y[k] for k in range(2)]
    from_y = [to_lo(own_x[k], k) for k in others]
    from_x = to_x(own_y[1])
    gh, (own_x, own_y) = beside(2, gh, (own_x[1:], own_y[1]), (own_x[0], own_y[0]))
    sums = [sum(from_y, own_x), own_y + from_x]

    extra = [part[:, r:].reshape(-1, cx) for part in sums]
    pieces = [jnp.concatenate([part[k, :r] for part in sums] + extra, 0) for k in range(n_hi)]
    from_hi = [to_hi(pieces[k], k) for k in range(1, n_hi)]
    gh, own = beside(3, gh, pieces[1:], pieces[0])
    total = sum(from_hi, own)
    far = to_x(total)

    scale = 1.0 / math.sqrt(members * npoints)
    halves = [ordered(total[k : k + r], far[k : k + r], 1, "mem", n_mem // 2) for k in (0, r)]
    grad_inner = gathered(jnp.concatenate(halves, 1) * scale, 0, "mem", 1)

    extra = ordered(total[2 * r :][None], far[2 * r :][None], 0, "mem", n_mem // 2)[None]
    bit = 1
    while bit < n_lo:
        extra = gathered(extra, 0, "grid", bit)
        bit *= 2
    extra = gathered(extra[None], 0, "mem", 1)
    extra = extra.reshape(2, n_lo, 2, 2, n_hi, EXTRA_ROWS, cx)
    extra = extra.transpose(0, 4, 1, 5, 3, 2, 6).reshape(2 * n_grid * EXTRA_ROWS, h)
    loss = jnp.sum(extra[v]) / npoints
    return (loss, gh, grad_inner, extra[:v] * (0.5 * scale))


def solution(mesh):
    in_specs = (P("mem", None, "grid"), P(None, "grid"), P("grid"), P(), P(), P(), P(), P())
    out_specs = (P(), P("mem", None, "grid"), P("grid", None), P())
    return jax.shard_map(shards, mesh=mesh, in_specs=in_specs, out_specs=out_specs, check_vma=False)
```

```python
import functools
import math

import jax
import jax.numpy as jnp
from jax import lax
from jax.experimental import pallas as pl
from jax.experimental.pallas import tpu as pltpu
from jax.sharding import PartitionSpec as P

EIGHTHS = (2, 2, 2, 2)
TILE = 256
EPS = 0.0004
K0 = math.sqrt(2.0 / math.pi)
K1 = K0 * 0.044715
SLAB = 512
EXTRA_ROWS = 8
VMEM = 8 * 1024 * 1024
NT = (((1,), (1,)), ((), ()))


def column(row, size):
    r = lax.broadcasted_iota(jnp.int32, (size, size), 0)
    c = lax.broadcasted_iota(jnp.int32, (size, size), 1)
    return jnp.sum(jnp.where(r == c, row, 0.0), axis=1, keepdims=True)


def field_rows(v, mloc, m, r0):
    full = v // 8 * 8
    if r0 < full:
        return pl.ds(m * full + r0, 8)
    return pl.ds(mloc * full + m * (v - full), v - full)


def forward_kernel(hid_ref, w_ref, b_ref, wo_ref, bo_ref, act_ref, slope_ref, f_ref, bias, half, fields, *slabs):
    step = pl.program_id(0)
    last = pl.num_programs(0) - 1
    mloc, h, t = hid_ref.shape
    v = half.shape[0]
    size = h // len(slabs)

    @pl.when(step == 0)
    def _():
        for k in range(h // 128):
            bias[pl.ds(k * 128, 128), :] = jnp.broadcast_to(
                column(b_ref[:, pl.ds(k * 128, 128)], 128), (128, 128)
            )
        half[...] = wo_ref[...] * jnp.bfloat16(0.5)

    def multiply(k):
        hid = jnp.concatenate([hid_ref[m] for m in range(mloc)], axis=1)
        rows = pl.ds(k * size, size)
        slabs[k][...] = jnp.dot(w_ref[rows, :], hid, preferred_element_type=jnp.float32)

    def gelu(tile, k):
        for r in range(0, size, 16):
            rows = pl.ds(k * size + r, 16)
            b = jnp.concatenate([bias[rows, :]] * (t // 128), axis=1)
            for m in range(mloc):
                x = slabs[k][pl.ds(r, 16), pl.ds(m * t, t)] + b
                q = x * x * K1
                th = jnp.tanh(x * (K0 + q))
                up = 1.0 + th
                act = x * up
                act_ref[tile, m, rows, :] = act.astype(jnp.bfloat16)
                slope_ref[tile, m, rows, :] = up + act * ((1.0 - th) * (K0 + 3.0 * q))
        rows = pl.ds(k * size, size)
        act = jnp.concatenate([act_ref[tile, m, rows, :] for m in range(mloc)], axis=1)
        return jnp.dot(half[:, rows], act, preferred_element_type=jnp.float32)

    def finish():
        out = fields[...] + gelu(step - 1, 1)
        for m in range(mloc):
            for r0 in range(0, v, 8):
                f_ref[field_rows(v, mloc, m, r0), :] = out[r0 : r0 + 8, m * t : (m + 1) * t]

    def begin():
        multiply(1)
        fields[...] = gelu(step, 0) + column(bo_ref[...], v)

    @pl.when(step == 0)
    def _():
        multiply(0)
        begin()

    @pl.when((step > 0) & (step < last))
    def _():
        multiply(0)
        finish()
        begin()

    @pl.when(step == last)
    def _():
        finish()


def forward(start, p, hidden, w_inner, b_inner, w_out, b_out, vmem):
    mloc, h, n = hidden.shape
    v = w_out.shape[0]
    t = TILE
    tiles = p // t
    whole = lambda s: (0, 0)
    once = pl.Buffered(1)
    shape = (p // t, mloc, h, t)
    held = pl.BlockSpec(shape, lambda s: (0, 0, 0, 0))
    return pl.pallas_call(
        forward_kernel,
        grid=(tiles + 1,),
        in_specs=[
            pl.BlockSpec((mloc, h, t), lambda s: (0, 0, start // t + jnp.minimum(s, tiles - 1))),
            pl.BlockSpec((h, h), whole, pipeline_mode=once),
            pl.BlockSpec((1, h), whole, pipeline_mode=once),
            pl.BlockSpec((v, h), whole, pipeline_mode=once),
            pl.BlockSpec((1, v), whole, pipeline_mode=once),
        ],
        out_specs=[
            held,
            held,
            pl.BlockSpec((mloc * v, t), lambda s: (0, jnp.maximum(s - 1, 0))),
        ],
        out_shape=[
            pltpu.VMEM(shape, jnp.bfloat16),
            pltpu.VMEM(shape, jnp.float32),
            jax.ShapeDtypeStruct((mloc * v, p), jnp.float32),
        ],
        scratch_shapes=[
            pltpu.VMEM((h, 128), jnp.float32),
            pltpu.VMEM((v, h), jnp.bfloat16),
            pltpu.VMEM((v, mloc * t), jnp.float32),
            pltpu.VMEM((h // 2, mloc * t), jnp.float32),
            pltpu.VMEM((h // 2, mloc * t), jnp.float32),
        ],
        compiler_params=pltpu.CompilerParams(vmem_limit_bytes=vmem),
        cost_estimate=pl.CostEstimate(
            flops=2 * h * h, bytes_accessed=2 * h * h, transcendentals=0
        ),
        name="forward_part",
    )(hidden, w_inner, b_inner, w_out, b_out)


def backward_kernel(
    first, last, dims, members,
    f_ref, fc_ref, fx_ref, fxc_ref, target_ref, area_ref, vw_ref, act_ref, slope_ref, hid_ref,
    wot_ref, acc_in, extra_in, gp_ref, extra_ref, *refs,
):
    acc, *refs = refs
    if last:
        keep_x, send_x, keep_y, send_y, *refs = refs
    (gf,) = refs
    step = pl.program_id(0)
    end = pl.num_programs(0) - 1
    mloc, _, t = hid_ref.shape
    v = target_ref.shape[0]
    h = wot_ref.shape[0]
    denom = members * (members - 1)

    def pair(a, b):
        d = a - b
        s = d * d + EPS
        r = lax.rsqrt(s)
        return d * r, s * r

    def scores(r0, vw, area):
        rows = pl.ds(r0, min(8, v - r0))
        places = [field_rows(v, mloc, m, r0) for m in range(mloc)]
        own = [f_ref[place, :] for place in places]
        others = [ref[place, :] for ref in (fc_ref, fx_ref, fxc_ref) for place in places]
        target = target_ref[rows, :]
        dsum = [jnp.zeros_like(target) for _ in range(mloc)]
        obs = []
        cross = inner = near = jnp.zeros_like(target)
        n_cross = n_inner = 0
        for i in range(mloc):
            sl, ph = pair(own[i], target)
            obs.append(sl)
            near = near + ph
            for b in others:
                sl, ph = pair(own[i], b)
                dsum[i] = dsum[i] + sl
                cross = cross + ph
                n_cross += 1
            for j in range(i + 1, mloc):
                sl, ph = pair(own[i], own[j])
                dsum[i] = dsum[i] + sl
                dsum[j] = dsum[j] - sl
                inner = inner + ph
                n_inner += 1
        weight = vw[r0 : r0 + 8] * area
        for m in range(mloc):
            gf[m, rows, :] = weight * (obs[m] * (1.0 / members) - dsum[m] * (1.0 / denom))
        near = (near - 0.02 * mloc) * (1.0 / members)
        pairs = (inner - 0.02 * n_inner) + 0.5 * (cross - 0.02 * n_cross)
        return jnp.sum(weight * (near - pairs * (1.0 / denom)), axis=0, keepdims=True)

    def weights(k):
        rows = pl.ds(k, SLAB)
        hid = jnp.concatenate([hid_ref[m] for m in range(mloc)], axis=1)
        acc[rows, :] += lax.dot_general(
            gp_ref[step - 1, rows, :], hid, NT, preferred_element_type=jnp.float32
        )

    def work(with_weights):
        vw, area = column(vw_ref[...], v), area_ref[...]
        starts = list(range(0, v, 8))
        slabs = list(range(0, h, SLAB)) if with_weights else [None]
        loss = jnp.zeros((1, t), jnp.float32)
        for k, slab in enumerate(slabs):
            if with_weights:
                weights(slab)
            for r0 in starts[k :: len(slabs)]:
                loss = loss + scores(r0, vw, area)
        for m in range(mloc):
            gf[m, pl.ds(v, gf.shape[1] - v), :] = jnp.zeros((gf.shape[1] - v, t), jnp.float32)
        g = jnp.concatenate([gf[m] for m in range(mloc)], axis=1).astype(jnp.bfloat16)
        for k in range(0, h, 256):
            rows = pl.ds(k, 256)
            ga = jnp.dot(wot_ref[rows, :], g, preferred_element_type=jnp.float32)
            for m in range(mloc):
                piece = ga[:, m * t : (m + 1) * t] * slope_ref[step, m, rows, :]
                gp_ref[step, rows, pl.ds(m * t, t)] = piece.astype(jnp.bfloat16)
        act = jnp.concatenate([act_ref[step, m] for m in range(mloc)], axis=1)
        extra_ref[...] += lax.dot_general(g, act, NT, preferred_element_type=jnp.float32)
        extra_ref[pl.ds(v, 1), pl.ds(0, t)] += loss

    @pl.when(step == 0)
    def _():
        if first:
            acc[...] = jnp.zeros_like(acc)
            extra_ref[...] = jnp.zeros_like(extra_ref)
        else:
            extra_ref[...] = extra_in[...]
        work(False)

    @pl.when((step > 0) & (step < end))
    def _():
        work(True)

    @pl.when(step == end)
    def _():
        for k in range(0, h, SLAB):
            weights(k)

    if last:
        n_hi, n_lo = dims

        @pl.when(step == end)
        def _():
            mem = lax.axis_index("mem")
            grid = lax.axis_index("grid")
            x, core = mem // 2, mem % 2
            hi, lo = grid // n_lo, grid % n_lo
            r = h // (2 * n_hi * n_lo)
            cx = keep_x.shape[4]
            for dlo in range(n_lo):
                for dhi in range(n_hi):
                    g = lax.rem(hi + dhi, n_hi) * n_lo + lax.rem(lo + dlo, n_lo)
                    block = dhi * n_lo + lax.rem(lo + dlo, n_lo)
                    for c, to_x, to_y in ((core, keep_x, keep_y), (1 - core, send_x, send_y)):
                        r0 = pl.multiple_of((g * 2 + c) * r, r)
                        total = acc[pl.ds(r0, r), :]
                        e0 = (c * (n_hi * n_lo) + block) * EXTRA_ROWS
                        at = pl.multiple_of(
                            jnp.minimum(e0, extra_ref.shape[0] - EXTRA_ROWS), EXTRA_ROWS
                        )
                        e = jnp.where(
                            e0 < extra_ref.shape[0], extra_ref[pl.ds(at, EXTRA_ROWS), :], 0.0
                        )
                        for values, rows in ((total, pl.ds(0, r)), (e, pl.ds(r, EXTRA_ROWS))):
                            q = [values[:, k * cx : (k + 1) * cx] for k in range(4)]
                            for d in range(2):
                                own = x == d
                                to_x[d, dlo, dhi, rows, :] = jnp.where(own, q[0], q[1])
                                to_y[dlo, d, dhi, rows, :] = jnp.where(own, q[2], q[3])


def backward(start, p, first, last, dims, members, fields, rest, acc, extra):
    target, area, vw, act, slope, hidden, wot = rest
    mloc, h, n = hidden.shape
    v = target.shape[0]
    vp = wot.shape[1]
    t = TILE
    off = start // t
    once = pl.Buffered(1)
    steps = p // t
    ahead = lambda s: jnp.minimum(s, steps - 1)
    f_spec = pl.BlockSpec((mloc * v, t), lambda s: (0, ahead(s)))
    whole = lambda s: (0, 0)
    const = lambda a: pl.BlockSpec(a.shape, whole, pipeline_mode=once)
    held = lambda a: pl.BlockSpec(a.shape, lambda s: (0,) * len(a.shape))
    in_specs = [f_spec] * 4 + [
        pl.BlockSpec((v, t), lambda s: (0, off + ahead(s))),
        pl.BlockSpec((1, t), lambda s: (0, off + ahead(s))),
        const(vw), held(act), held(slope),
        pl.BlockSpec((mloc, h, t), lambda s: (0, 0, off + jnp.maximum(s - 1, 0))),
        const(wot),
    ]
    act, slope = (pltpu.with_memory_space_constraint(a, pltpu.VMEM) for a in (act, slope))
    args = [*fields, target, area, vw, act, slope, hidden, wot]
    kernel = functools.partial(backward_kernel, first, last, dims, members)
    if first:
        kernel_fn = lambda *refs: kernel(*refs[:11], None, None, *refs[11:])
        aliases = {}
    else:
        kernel_fn = kernel
        in_specs += [held(acc), const(extra)]
        args += [acc, extra]
        aliases = {11: 2}
    out_shape = [
        pltpu.VMEM((p // t, h, mloc * t), jnp.bfloat16),
        jax.ShapeDtypeStruct((vp, h), jnp.float32),
        pltpu.VMEM((h, h), jnp.float32),
    ]
    if last:
        n_hi, n_lo = dims
        r = h // (2 * n_hi * n_lo)
        cx = h // 4
        out_shape += [pltpu.VMEM((2, n_lo, n_hi, r + EXTRA_ROWS, cx), jnp.float32)] * 2
        out_shape += [pltpu.VMEM((n_lo, 2, n_hi, r + EXTRA_ROWS, cx), jnp.float32)] * 2
    out_specs = [held(a) for a in out_shape]
    return pl.pallas_call(
        kernel_fn,
        grid=(steps + 1,),
        in_specs=in_specs,
        out_specs=out_specs,
        out_shape=out_shape,
        scratch_shapes=[pltpu.VMEM((mloc, vp, t), jnp.float32)],
        input_output_aliases=aliases,
        compiler_params=pltpu.CompilerParams(vmem_limit_bytes=VMEM),
        cost_estimate=pl.CostEstimate(
            flops=2 * h * h, bytes_accessed=2 * h * h, transcendentals=0
        ),
        name="backward_part",
    )(*args)


def transposes_kernel(w_ref, wo_ref, wt_ref, wot_ref):
    wt_ref[...] = w_ref[...].astype(jnp.float32).T.astype(jnp.bfloat16)

    @pl.when(pl.program_id(0) == 0)
    def _():
        v, h = wo_ref.shape
        rows = jnp.concatenate(
            [wo_ref[...].astype(jnp.float32) * 0.5, jnp.zeros((wot_ref.shape[1] - v, h), jnp.float32)], 0
        )
        wot_ref[...] = rows.T.astype(jnp.bfloat16)


def transposes(w_inner, w_out, vp):
    v, h = w_out.shape
    t = TILE
    return pl.pallas_call(
        transposes_kernel,
        grid=(h // t,),
        in_specs=[
            pl.BlockSpec((t, h), lambda s: (s, 0)),
            pl.BlockSpec((v, h), lambda s: (0, 0)),
        ],
        out_specs=[
            pl.BlockSpec((h, t), lambda s: (0, s)),
            pl.BlockSpec((h, vp), lambda s: (0, 0)),
        ],
        out_shape=[pltpu.VMEM((h, h), jnp.bfloat16), pltpu.VMEM((h, vp), jnp.bfloat16)],
        compiler_params=pltpu.CompilerParams(vmem_limit_bytes=VMEM),
        cost_estimate=pl.CostEstimate(flops=2 * h, bytes_accessed=2 * h, transcendentals=0),
        name="transposes",
    )(w_inner, w_out)


def input_kernel(wt_ref, gp_ref, *refs):
    mloc, h, t = refs[-1].shape
    for k in range(0, h, SLAB):
        rows = pl.ds(k, SLAB)
        out = jnp.dot(wt_ref[rows, :], gp_ref[pl.program_id(0)], preferred_element_type=jnp.float32)
        for m in range(mloc):
            refs[-1][m, rows, :] = out[:, m * t : (m + 1) * t].astype(jnp.bfloat16)


def input_gradient(start, p, n, wt, gp, gh):
    steps, h, width = gp.shape
    t = TILE
    mloc = width // t
    off = start // t
    in_specs = [
        pl.BlockSpec((h, h), lambda s: (0, 0), pipeline_mode=pl.Buffered(1)),
        pl.BlockSpec(gp.shape, lambda s: (0, 0, 0)),
    ]
    args = [wt, gp]
    if gh is not None:
        in_specs.append(pl.BlockSpec(memory_space=pl.ANY))
        args.append(gh)
    return pl.pallas_call(
        input_kernel,
        grid=(steps,),
        in_specs=in_specs,
        out_specs=pl.BlockSpec((mloc, h, t), lambda s: (0, 0, off + s)),
        out_shape=jax.ShapeDtypeStruct((mloc, h, n), jnp.bfloat16),
        input_output_aliases={} if gh is None else {2: 0},
        compiler_params=pltpu.CompilerParams(vmem_limit_bytes=VMEM),
        cost_estimate=pl.CostEstimate(
            flops=2 * h * h, bytes_accessed=2 * h * h, transcendentals=0
        ),
        name="grad_hidden_part",
    )(*args)


def after(value, *others):
    return lax.optimization_barrier((value,) + others)[0]


def shards(hidden, target, area, var_weight, w_inner, b_inner, w_out, b_out):
    mloc, h, n = hidden.shape
    n_mem = lax.axis_size("mem")
    n_grid = lax.axis_size("grid")
    members = mloc * n_mem
    npoints = n * n_grid
    v = w_out.shape[0]
    vp = 128
    n_lo = 2
    while n_lo * n_lo * 4 <= n_grid:
        n_lo *= 2
    n_hi = n_grid // n_lo

    swap_x = [(i, (i + n_mem // 2) % n_mem) for i in range(n_mem)]
    swap_core = [(i, i ^ 1) for i in range(n_mem)]

    def shift_lo(k):
        return [(a * n_lo + b, a * n_lo + (b + k) % n_lo) for a in range(n_hi) for b in range(n_lo)]

    def shift_hi(k):
        return [(a * n_lo + b, (a + k) % n_hi * n_lo + b) for a in range(n_hi) for b in range(n_lo)]

    to_x = lambda a: lax.ppermute(a, "mem", swap_x)
    to_core = lambda a: lax.ppermute(a, "mem", swap_core)
    to_lo = lambda a, k: lax.ppermute(a, "grid", shift_lo(k))
    to_hi = lambda a, k: lax.ppermute(a, "grid", shift_hi(k))

    mem, grid = lax.axis_index("mem"), lax.axis_index("grid")
    at_zero = {("mem", bit): mem & bit == 0 for bit in (1, n_mem // 2)}
    bit = 1
    while bit < n_lo:
        at_zero["grid", bit] = grid & bit == 0
        bit *= 2
    hidden, at_zero = lax.optimization_barrier((hidden, at_zero))
    hidden, w_out, b_inner, b_out = (
        pltpu.with_memory_space_constraint(a, pltpu.HBM)
        for a in (hidden, w_out, b_inner.reshape(1, h), b_out.reshape(1, v))
    )
    unit = n // sum(EIGHTHS)
    starts = [unit * sum(EIGHTHS[:k]) for k in range(len(EIGHTHS))]
    spans = [(start, unit * size) for start, size in zip(starts, EIGHTHS)]
    parts = []
    for start, p in spans:
        w, vmem = w_inner, VMEM
        if parts:
            b_out = after(b_out, parts[-1][2])
        else:
            w = pltpu.with_memory_space_constraint(w_inner, pltpu.HBM)
            vmem += 4 * h * h
        parts.append(forward(start, p, hidden, w, b_inner, w_out, b_out, vmem))
    far = [to_x(fields) for _, _, fields in parts]
    near = [to_core(fields) for _, _, fields in parts]
    wt, wot = transposes(after(w_inner, parts[-1][2]), w_out, vp)
    vw, area = var_weight.reshape(1, v), area.reshape(1, n)
    acc = extra = gh = None
    grad_pre = []
    for k, (start, p) in enumerate(spans):
        act, slope, fields = parts[k]
        first, last = k == 0, k == len(spans) - 1
        if k:
            far[k] = after(far[k], parts[-1][2] if k == 1 else grad_pre[k - 2])
        gp, extra, acc, *accs = backward(
            start, p, first, last, (n_hi, n_lo), members,
            (fields, near[k], far[k], to_core(far[k])),
            (target, area, vw, act, slope, hidden, wot), acc, extra,
        )
        grad_pre.append(gp)
    keep_x, send_x, keep_y, send_y = accs

    def gathered(block, axis, name, bit):
        n = lax.axis_size(name)
        other = lax.ppermute(block, name, [(i, i ^ bit) for i in range(n)])
        return ordered(block, other, axis, name, bit)

    def ordered(block, other, axis, name, bit):
        return jnp.where(
            at_zero[name, bit],
            jnp.concatenate([block, other], axis),
            jnp.concatenate([other, block], axis),
        )

    def beside(k, gh, start_after, wait_for):
        gh = input_gradient(*spans[k], n, wt, after(grad_pre[k], start_after), gh)
        return lax.optimization_barrier((gh, wait_for))

    r, cx = h // (2 * n_grid), keep_x.shape[-1]
    others = range(1, n_lo)
    got_x = to_core(send_x)
    got_y = to_core(send_y)
    out_x = keep_x[1] + got_x[1]
    out_y = [keep_y[k] + got_y[k] for k in others]
    from_x = to_x(out_x)
    from_y = [to_lo(out_y[k - 1], k) for k in others]
    gh, (keep_x, keep_y) = beside(0, gh, (out_x, out_y), (keep_x, keep_y))
    gh, (keep_x, keep_y) = beside(1, gh, (out_x, out_y), (keep_x, keep_y))
    own_x = keep_x[0] + got_x[0] + from_x
    own_y = sum(from_y, keep_y[0] + got_y[0])
    own_x, own_y = [own_x[k] for k in range(n_lo)], [own_y[k] for k in range(2)]
    from_y = [to_lo(own_x[k], k) for k in others]
    from_x = to_x(own_y[1])
    gh, (own_x, own_y) = beside(2, gh, (own_x[1:], own_y[1]), (own_x[0], own_y[0]))
    sums = [sum(from_y, own_x), own_y + from_x]

    extra = [part[:, r:].reshape(-1, cx) for part in sums]
    pieces = [jnp.concatenate([part[k, :r] for part in sums] + extra, 0) for k in range(n_hi)]
    from_hi = [to_hi(pieces[k], k) for k in range(1, n_hi)]
    gh, own = beside(3, gh, pieces[1:], pieces[0])
    total = sum(from_hi, own)
    far = to_x(total)

    scale = 1.0 / math.sqrt(members * npoints)
    halves = [ordered(total[k : k + r], far[k : k + r], 1, "mem", n_mem // 2) for k in (0, r)]
    grad_inner = gathered(jnp.concatenate(halves, 1) * scale, 0, "mem", 1)

    extra = ordered(total[2 * r :][None], far[2 * r :][None], 0, "mem", n_mem // 2)[None]
    bit = 1
    while bit < n_lo:
        extra = gathered(extra, 0, "grid", bit)
        bit *= 2
    extra = gathered(extra[None], 0, "mem", 1)
    extra = extra.reshape(2, n_lo, 2, 2, n_hi, EXTRA_ROWS, cx)
    extra = extra.transpose(0, 4, 1, 5, 3, 2, 6).reshape(2 * n_grid * EXTRA_ROWS, h)
    loss = jnp.sum(extra[v]) / npoints
    return (loss, gh, grad_inner, extra[:v] * (0.5 * scale))


def solution(mesh):
    in_specs = (P("mem", None, "grid"), P(None, "grid"), P("grid"), P(), P(), P(), P(), P())
    out_specs = (P(), P("mem", None, "grid"), P("grid", None), P())
    return jax.shard_map(shards, mesh=mesh, in_specs=in_specs, out_specs=out_specs, check_vma=False)
```

```python
import functools
import math

import jax
import jax.numpy as jnp
from jax import lax
from jax.experimental import pallas as pl
from jax.experimental.pallas import tpu as pltpu
from jax.sharding import PartitionSpec as P

EIGHTHS = (2, 3, 3)
TILE = 256
EPS = 0.0004
K0 = math.sqrt(2.0 / math.pi)
K1 = K0 * 0.044715
SLAB = 512
EXTRA_ROWS = 8
VMEM = 8 * 1024 * 1024
NT = (((1,), (1,)), ((), ()))


def column(row, size):
    r = lax.broadcasted_iota(jnp.int32, (size, size), 0)
    c = lax.broadcasted_iota(jnp.int32, (size, size), 1)
    return jnp.sum(jnp.where(r == c, row, 0.0), axis=1, keepdims=True)


def field_rows(v, mloc, m, r0):
    full = v // 8 * 8
    if r0 < full:
        return pl.ds(m * full + r0, 8)
    return pl.ds(mloc * full + m * (v - full), v - full)


def forward_kernel(hid_ref, w_ref, b_ref, wo_ref, bo_ref, act_ref, slope_ref, f_ref, bias, half, fields, *slabs):
    step = pl.program_id(0)
    last = pl.num_programs(0) - 1
    mloc, h, t = hid_ref.shape
    v = half.shape[0]
    size = h // len(slabs)

    @pl.when(step == 0)
    def _():
        for k in range(h // 128):
            bias[pl.ds(k * 128, 128), :] = jnp.broadcast_to(
                column(b_ref[:, pl.ds(k * 128, 128)], 128), (128, 128)
            )
        half[...] = wo_ref[...] * jnp.bfloat16(0.5)

    def multiply(k):
        hid = jnp.concatenate([hid_ref[m] for m in range(mloc)], axis=1)
        rows = pl.ds(k * size, size)
        slabs[k][...] = jnp.dot(w_ref[rows, :], hid, preferred_element_type=jnp.float32)

    def gelu(tile, k):
        for r in range(0, size, 16):
            rows = pl.ds(k * size + r, 16)
            b = jnp.concatenate([bias[rows, :]] * (t // 128), axis=1)
            for m in range(mloc):
                x = slabs[k][pl.ds(r, 16), pl.ds(m * t, t)] + b
                q = x * x * K1
                th = jnp.tanh(x * (K0 + q))
                up = 1.0 + th
                act = x * up
                act_ref[tile, m, rows, :] = act.astype(jnp.bfloat16)
                slope_ref[tile, m, rows, :] = up + act * ((1.0 - th) * (K0 + 3.0 * q))
        rows = pl.ds(k * size, size)
        act = jnp.concatenate([act_ref[tile, m, rows, :] for m in range(mloc)], axis=1)
        return jnp.dot(half[:, rows], act, preferred_element_type=jnp.float32)

    def finish():
        out = fields[...] + gelu(lax.max(step - 1, 0), 1)
        for m in range(mloc):
            for r0 in range(0, v, 8):
                f_ref[field_rows(v, mloc, m, r0), :] = out[r0 : r0 + 8, m * t : (m + 1) * t]

    @pl.when(step < last)
    def _():
        multiply(0)
        finish()
        multiply(1)
        fields[...] = gelu(step, 0) + column(bo_ref[...], v)

    @pl.when(step == last)
    def _():
        finish()


def forward(start, p, hidden, w_inner, b_inner, w_out, b_out, vmem):
    mloc, h, n = hidden.shape
    v = w_out.shape[0]
    t = TILE
    tiles = p // t
    whole = lambda s: (0, 0)
    once = pl.Buffered(1)
    shape = (p // t, mloc, h, t)
    held = pl.BlockSpec(shape, lambda s: (0, 0, 0, 0))
    return pl.pallas_call(
        forward_kernel,
        grid=(tiles + 1,),
        in_specs=[
            pl.BlockSpec((mloc, h, t), lambda s: (0, 0, start // t + jnp.minimum(s, tiles - 1))),
            pl.BlockSpec((h, h), whole, pipeline_mode=once),
            pl.BlockSpec((1, h), whole, pipeline_mode=once),
            pl.BlockSpec((v, h), whole, pipeline_mode=once),
            pl.BlockSpec((1, v), whole, pipeline_mode=once),
        ],
        out_specs=[
            held,
            held,
            pl.BlockSpec((mloc * v, t), lambda s: (0, jnp.maximum(s - 1, 0))),
        ],
        out_shape=[
            pltpu.VMEM(shape, jnp.bfloat16),
            pltpu.VMEM(shape, jnp.float32),
            jax.ShapeDtypeStruct((mloc * v, p), jnp.float32),
        ],
        scratch_shapes=[
            pltpu.VMEM((h, 128), jnp.float32),
            pltpu.VMEM((v, h), jnp.bfloat16),
            pltpu.VMEM((v, mloc * t), jnp.float32),
            pltpu.VMEM((h // 2, mloc * t), jnp.float32),
            pltpu.VMEM((h // 2, mloc * t), jnp.float32),
        ],
        compiler_params=pltpu.CompilerParams(vmem_limit_bytes=vmem),
        cost_estimate=pl.CostEstimate(
            flops=2 * h * h, bytes_accessed=2 * h * h, transcendentals=0
        ),
        name="forward_part",
    )(hidden, w_inner, b_inner, w_out, b_out)


def backward_kernel(
    first, last, dims, members,
    f_ref, fc_ref, fx_ref, fxc_ref, target_ref, area_ref, vw_ref, act_ref, slope_ref, hid_ref,
    wot_ref, acc_in, extra_in, gp_ref, extra_ref, *refs,
):
    acc, *refs = refs
    if last:
        keep_x, send_x, keep_y, send_y, *refs = refs
    (gf,) = refs
    step = pl.program_id(0)
    end = pl.num_programs(0) - 1
    mloc, _, t = hid_ref.shape
    v = target_ref.shape[0]
    h = wot_ref.shape[0]
    denom = members * (members - 1)

    def pair(a, b):
        d = a - b
        s = d * d + EPS
        r = lax.rsqrt(s)
        return d * r, s * r

    def scores(r0, vw, area):
        rows = pl.ds(r0, min(8, v - r0))
        places = [field_rows(v, mloc, m, r0) for m in range(mloc)]
        own = [f_ref[place, :] for place in places]
        others = [ref[place, :] for ref in (fc_ref, fx_ref, fxc_ref) for place in places]
        target = target_ref[rows, :]
        dsum = [jnp.zeros_like(target) for _ in range(mloc)]
        obs = []
        cross = inner = near = jnp.zeros_like(target)
        n_cross = n_inner = 0
        for i in range(mloc):
            sl, ph = pair(own[i], target)
            obs.append(sl)
            near = near + ph
            for b in others:
                sl, ph = pair(own[i], b)
                dsum[i] = dsum[i] + sl
                cross = cross + ph
                n_cross += 1
            for j in range(i + 1, mloc):
                sl, ph = pair(own[i], own[j])
                dsum[i] = dsum[i] + sl
                dsum[j] = dsum[j] - sl
                inner = inner + ph
                n_inner += 1
        weight = vw[r0 : r0 + 8] * area
        for m in range(mloc):
            gf[m, rows, :] = weight * (obs[m] * (1.0 / members) - dsum[m] * (1.0 / denom))
        near = (near - 0.02 * mloc) * (1.0 / members)
        pairs = (inner - 0.02 * n_inner) + 0.5 * (cross - 0.02 * n_cross)
        return jnp.sum(weight * (near - pairs * (1.0 / denom)), axis=0, keepdims=True)

    def weights(k):
        rows = pl.ds(k, SLAB)
        hid = jnp.concatenate([hid_ref[m] for m in range(mloc)], axis=1)
        acc[rows, :] += lax.dot_general(
            gp_ref[step - 1, rows, :], hid, NT, preferred_element_type=jnp.float32
        )

    def work(with_weights):
        vw, area = column(vw_ref[...], v), area_ref[...]
        starts = list(range(0, v, 8))
        slabs = list(range(0, h, SLAB)) if with_weights else [None]
        loss = jnp.zeros((1, t), jnp.float32)
        for k, slab in enumerate(slabs):
            if with_weights:
                weights(slab)
            for r0 in starts[k :: len(slabs)]:
                loss = loss + scores(r0, vw, area)
        for m in range(mloc):
            gf[m, pl.ds(v, gf.shape[1] - v), :] = jnp.zeros((gf.shape[1] - v, t), jnp.float32)
        g = jnp.concatenate([gf[m] for m in range(mloc)], axis=1).astype(jnp.bfloat16)
        for k in range(0, h, 256):
            rows = pl.ds(k, 256)
            ga = jnp.dot(wot_ref[rows, :], g, preferred_element_type=jnp.float32)
            for m in range(mloc):
                piece = ga[:, m * t : (m + 1) * t] * slope_ref[step, m, rows, :]
                gp_ref[step, rows, pl.ds(m * t, t)] = piece.astype(jnp.bfloat16)
        act = jnp.concatenate([act_ref[step, m] for m in range(mloc)], axis=1)
        extra_ref[...] += lax.dot_general(g, act, NT, preferred_element_type=jnp.float32)
        extra_ref[pl.ds(v, 1), pl.ds(0, t)] += loss

    @pl.when(step == 0)
    def _():
        if first:
            acc[...] = jnp.zeros_like(acc)
            extra_ref[...] = jnp.zeros_like(extra_ref)
        else:
            extra_ref[...] = extra_in[...]
        work(False)

    @pl.when((step > 0) & (step < end))
    def _():
        work(True)

    @pl.when(step == end)
    def _():
        for k in range(0, h, SLAB):
            weights(k)

    if last:
        n_hi, n_lo = dims

        @pl.when(step == end)
        def _():
            mem = lax.axis_index("mem")
            grid = lax.axis_index("grid")
            x, core = mem // 2, mem % 2
            hi, lo = grid // n_lo, grid % n_lo
            r = h // (2 * n_hi * n_lo)
            cx = keep_x.shape[4]
            for dlo in range(n_lo):
                for dhi in range(n_hi):
                    g = lax.rem(hi + dhi, n_hi) * n_lo + lax.rem(lo + dlo, n_lo)
                    block = dhi * n_lo + lax.rem(lo + dlo, n_lo)
                    for c, to_x, to_y in ((core, keep_x, keep_y), (1 - core, send_x, send_y)):
                        r0 = pl.multiple_of((g * 2 + c) * r, r)
                        total = acc[pl.ds(r0, r), :]
                        e0 = (c * (n_hi * n_lo) + block) * EXTRA_ROWS
                        at = pl.multiple_of(
                            jnp.minimum(e0, extra_ref.shape[0] - EXTRA_ROWS), EXTRA_ROWS
                        )
                        e = jnp.where(
                            e0 < extra_ref.shape[0], extra_ref[pl.ds(at, EXTRA_ROWS), :], 0.0
                        )
                        for values, rows in ((total, pl.ds(0, r)), (e, pl.ds(r, EXTRA_ROWS))):
                            q = [values[:, k * cx : (k + 1) * cx] for k in range(4)]
                            for d in range(2):
                                own = x == d
                                to_x[d, dlo, dhi, rows, :] = jnp.where(own, q[0], q[1])
                                to_y[dlo, d, dhi, rows, :] = jnp.where(own, q[2], q[3])


def backward(start, p, first, last, dims, members, fields, rest, acc, extra):
    target, area, vw, act, slope, hidden, wot = rest
    mloc, h, n = hidden.shape
    v = target.shape[0]
    vp = wot.shape[1]
    t = TILE
    off = start // t
    once = pl.Buffered(1)
    steps = p // t
    ahead = lambda s: jnp.minimum(s, steps - 1)
    f_spec = pl.BlockSpec((mloc * v, t), lambda s: (0, ahead(s)))
    whole = lambda s: (0, 0)
    const = lambda a: pl.BlockSpec(a.shape, whole, pipeline_mode=once)
    held = lambda a: pl.BlockSpec(a.shape, lambda s: (0,) * len(a.shape))
    in_specs = [f_spec] * 4 + [
        pl.BlockSpec((v, t), lambda s: (0, off + ahead(s))),
        pl.BlockSpec((1, t), lambda s: (0, off + ahead(s))),
        const(vw), held(act), held(slope),
        pl.BlockSpec((mloc, h, t), lambda s: (0, 0, off + jnp.maximum(s - 1, 0))),
        const(wot),
    ]
    act, slope = (pltpu.with_memory_space_constraint(a, pltpu.VMEM) for a in (act, slope))
    args = [*fields, target, area, vw, act, slope, hidden, wot]
    kernel = functools.partial(backward_kernel, first, last, dims, members)
    if first:
        kernel_fn = lambda *refs: kernel(*refs[:11], None, None, *refs[11:])
        aliases = {}
    else:
        kernel_fn = kernel
        in_specs += [held(acc), const(extra)]
        args += [acc, extra]
        aliases = {11: 2}
    out_shape = [
        pltpu.VMEM((p // t, h, mloc * t), jnp.bfloat16),
        jax.ShapeDtypeStruct((vp, h), jnp.float32),
        pltpu.VMEM((h, h), jnp.float32),
    ]
    if last:
        n_hi, n_lo = dims
        r = h // (2 * n_hi * n_lo)
        cx = h // 4
        out_shape += [pltpu.VMEM((2, n_lo, n_hi, r + EXTRA_ROWS, cx), jnp.float32)] * 2
        out_shape += [pltpu.VMEM((n_lo, 2, n_hi, r + EXTRA_ROWS, cx), jnp.float32)] * 2
    out_specs = [held(a) for a in out_shape]
    return pl.pallas_call(
        kernel_fn,
        grid=(steps + 1,),
        in_specs=in_specs,
        out_specs=out_specs,
        out_shape=out_shape,
        scratch_shapes=[pltpu.VMEM((mloc, vp, t), jnp.float32)],
        input_output_aliases=aliases,
        compiler_params=pltpu.CompilerParams(vmem_limit_bytes=VMEM),
        cost_estimate=pl.CostEstimate(
            flops=2 * h * h, bytes_accessed=2 * h * h, transcendentals=0
        ),
        name="backward_part",
    )(*args)


def transposes_kernel(w_ref, wo_ref, wt_ref, wot_ref):
    wt_ref[...] = w_ref[...].astype(jnp.float32).T.astype(jnp.bfloat16)

    @pl.when(pl.program_id(0) == 0)
    def _():
        v, h = wo_ref.shape
        rows = jnp.concatenate(
            [wo_ref[...].astype(jnp.float32) * 0.5, jnp.zeros((wot_ref.shape[1] - v, h), jnp.float32)], 0
        )
        wot_ref[...] = rows.T.astype(jnp.bfloat16)


def transposes(w_inner, w_out, vp):
    v, h = w_out.shape
    t = TILE
    return pl.pallas_call(
        transposes_kernel,
        grid=(h // t,),
        in_specs=[
            pl.BlockSpec((t, h), lambda s: (s, 0)),
            pl.BlockSpec((v, h), lambda s: (0, 0)),
        ],
        out_specs=[
            pl.BlockSpec((h, t), lambda s: (0, s)),
            pl.BlockSpec((h, vp), lambda s: (0, 0)),
        ],
        out_shape=[pltpu.VMEM((h, h), jnp.bfloat16), pltpu.VMEM((h, vp), jnp.bfloat16)],
        compiler_params=pltpu.CompilerParams(vmem_limit_bytes=VMEM),
        cost_estimate=pl.CostEstimate(flops=2 * h, bytes_accessed=2 * h, transcendentals=0),
        name="transposes",
    )(w_inner, w_out)


def input_kernel(wt_ref, gp_ref, *refs):
    mloc, h, t = refs[-1].shape
    for k in range(0, h, SLAB):
        rows = pl.ds(k, SLAB)
        out = jnp.dot(wt_ref[rows, :], gp_ref[pl.program_id(0)], preferred_element_type=jnp.float32)
        for m in range(mloc):
            refs[-1][m, rows, :] = out[:, m * t : (m + 1) * t].astype(jnp.bfloat16)


def input_gradient(start, p, n, wt, gp, gh):
    steps, h, width = gp.shape
    t = TILE
    mloc = width // t
    off = start // t
    in_specs = [
        pl.BlockSpec((h, h), lambda s: (0, 0), pipeline_mode=pl.Buffered(1)),
        pl.BlockSpec(gp.shape, lambda s: (0, 0, 0)),
    ]
    args = [wt, gp]
    if gh is not None:
        in_specs.append(pl.BlockSpec(memory_space=pl.ANY))
        args.append(gh)
    return pl.pallas_call(
        input_kernel,
        grid=(steps,),
        in_specs=in_specs,
        out_specs=pl.BlockSpec((mloc, h, t), lambda s: (0, 0, off + s)),
        out_shape=jax.ShapeDtypeStruct((mloc, h, n), jnp.bfloat16),
        input_output_aliases={} if gh is None else {2: 0},
        compiler_params=pltpu.CompilerParams(vmem_limit_bytes=VMEM),
        cost_estimate=pl.CostEstimate(
            flops=2 * h * h, bytes_accessed=2 * h * h, transcendentals=0
        ),
        name="grad_hidden_part",
    )(*args)


def after(value, *others):
    return lax.optimization_barrier((value,) + others)[0]


def shards(hidden, target, area, var_weight, w_inner, b_inner, w_out, b_out):
    mloc, h, n = hidden.shape
    n_mem = lax.axis_size("mem")
    n_grid = lax.axis_size("grid")
    members = mloc * n_mem
    npoints = n * n_grid
    v = w_out.shape[0]
    vp = 128
    n_lo = 2
    while n_lo * n_lo * 4 <= n_grid:
        n_lo *= 2
    n_hi = n_grid // n_lo

    swap_x = [(i, (i + n_mem // 2) % n_mem) for i in range(n_mem)]
    swap_core = [(i, i ^ 1) for i in range(n_mem)]

    def shift_lo(k):
        return [(a * n_lo + b, a * n_lo + (b + k) % n_lo) for a in range(n_hi) for b in range(n_lo)]

    def shift_hi(k):
        return [(a * n_lo + b, (a + k) % n_hi * n_lo + b) for a in range(n_hi) for b in range(n_lo)]

    to_x = lambda a: lax.ppermute(a, "mem", swap_x)
    to_core = lambda a: lax.ppermute(a, "mem", swap_core)
    to_lo = lambda a, k: lax.ppermute(a, "grid", shift_lo(k))
    to_hi = lambda a, k: lax.ppermute(a, "grid", shift_hi(k))

    mem, grid = lax.axis_index("mem"), lax.axis_index("grid")
    at_zero = {("mem", bit): mem & bit == 0 for bit in (1, n_mem // 2)}
    bit = 1
    while bit < n_lo:
        at_zero["grid", bit] = grid & bit == 0
        bit *= 2
    hidden, at_zero = lax.optimization_barrier((hidden, at_zero))
    hidden, w_out, b_inner, b_out = (
        pltpu.with_memory_space_constraint(a, pltpu.HBM)
        for a in (hidden, w_out, b_inner.reshape(1, h), b_out.reshape(1, v))
    )
    unit = n // sum(EIGHTHS)
    starts = [unit * sum(EIGHTHS[:k]) for k in range(len(EIGHTHS))]
    spans = [(start, unit * size) for start, size in zip(starts, EIGHTHS)]
    parts, far = [], []
    for start, p in spans:
        w, vmem = w_inner, VMEM
        if parts:
            b_out = after(b_out, parts[-1][2])
        else:
            w = pltpu.with_memory_space_constraint(w_inner, pltpu.HBM)
            vmem += 4 * h * h
        parts.append(forward(start, p, hidden, w, b_inner, w_out, b_out, vmem))
        far.append(to_x(parts[-1][2]))
    near = [to_core(fields) for _, _, fields in parts]
    wt, wot = transposes(after(w_inner, parts[-1][2]), w_out, vp)
    vw, area = var_weight.reshape(1, v), area.reshape(1, n)
    acc = extra = gh = None
    grad_pre = []
    for k, (start, p) in enumerate(spans):
        act, slope, fields = parts[k]
        first, last = k == 0, k == len(spans) - 1
        if k:
            far[k] = after(far[k], parts[-1][2] if k == 1 else grad_pre[k - 2])
        gp, extra, acc, *accs = backward(
            start, p, first, last, (n_hi, n_lo), members,
            (fields, near[k], far[k], to_core(far[k])),
            (target, area, vw, act, slope, hidden, wot), acc, extra,
        )
        grad_pre.append(gp)
    keep_x, send_x, keep_y, send_y = accs

    def gathered(block, axis, name, bit):
        n = lax.axis_size(name)
        other = lax.ppermute(block, name, [(i, i ^ bit) for i in range(n)])
        return ordered(block, other, axis, name, bit)

    def ordered(block, other, axis, name, bit):
        return jnp.where(
            at_zero[name, bit],
            jnp.concatenate([block, other], axis),
            jnp.concatenate([other, block], axis),
        )

    def beside(k, gh, start_after, wait_for):
        gh = input_gradient(*spans[k], n, wt, after(grad_pre[k], start_after), gh)
        return lax.optimization_barrier((gh, wait_for))

    r, cx = h // (2 * n_grid), keep_x.shape[-1]
    others = range(1, n_lo)
    got_x = to_core(send_x)
    got_y = to_core(send_y)
    out_x = keep_x[1] + got_x[1]
    out_y = [keep_y[k] + got_y[k] for k in others]
    from_x = to_x(out_x)
    from_y = [to_lo(out_y[k - 1], k) for k in others]
    gh, (keep_x, keep_y) = beside(0, gh, (out_x, out_y), (keep_x, keep_y))
    own_x = keep_x[0] + got_x[0] + from_x
    own_y = sum(from_y, keep_y[0] + got_y[0])
    own_x, own_y = [own_x[k] for k in range(n_lo)], [own_y[k] for k in range(2)]
    from_y = [to_lo(own_x[k], k) for k in others]
    from_x = to_x(own_y[1])
    gh, (own_x, own_y) = beside(1, gh, (own_x[1:], own_y[1]), (own_x[0], own_y[0]))
    sums = [sum(from_y, own_x), own_y + from_x]

    extra = [part[:, r:].reshape(-1, cx) for part in sums]
    pieces = [jnp.concatenate([part[k, :r] for part in sums] + extra, 0) for k in range(n_hi)]
    from_hi = [to_hi(pieces[k], k) for k in range(1, n_hi)]
    gh, own = beside(2, gh, pieces[1:], pieces[0])
    total = sum(from_hi, own)
    far = to_x(total)
    mine = total[2 * r :][None]
    beyond = lax.ppermute(mine, "grid", [(g, g ^ 1) for g in range(n_grid)])
    pairs = [(m * n_grid + g, (m + n_mem // 2) % n_mem * n_grid + (g ^ 1)) for m in range(n_mem) for g in range(n_grid)]
    across = lax.ppermute(mine, ("mem", "grid"), pairs)

    scale = 1.0 / math.sqrt(members * npoints)
    halves = [ordered(total[k : k + r], far[k : k + r], 1, "mem", n_mem // 2) for k in (0, r)]
    grad_inner = gathered(jnp.concatenate(halves, 1) * scale, 0, "mem", 1)

    sides = [ordered(mine, far[2 * r :][None], 0, "mem", n_mem // 2)]
    sides.append(ordered(beyond, across, 0, "mem", n_mem // 2))
    extra = ordered(*(side[None] for side in sides), 0, "grid", 1)
    bit = 2
    while bit < n_lo:
        extra = gathered(extra, 0, "grid", bit)
        bit *= 2
    extra = gathered(extra[None], 0, "mem", 1)
    extra = extra.reshape(2, n_lo, 2, 2, n_hi, EXTRA_ROWS, cx)
    extra = extra.transpose(0, 4, 1, 5, 3, 2, 6).reshape(2 * n_grid * EXTRA_ROWS, h)
    loss = jnp.sum(extra[v]) / npoints
    return (loss, gh, grad_inner, extra[:v] * (0.5 * scale))


def solution(mesh):
    in_specs = (P("mem", None, "grid"), P(None, "grid"), P("grid"), P(), P(), P(), P(), P())
    out_specs = (P(), P("mem", None, "grid"), P("grid", None), P())
    return jax.shard_map(shards, mesh=mesh, in_specs=in_specs, out_specs=out_specs, check_vma=False)
```

```python
import functools
import math

import jax
import jax.numpy as jnp
from jax import lax
from jax.experimental import pallas as pl
from jax.experimental.pallas import tpu as pltpu
from jax.sharding import PartitionSpec as P

EIGHTHS = (2, 2, 2, 2)
TILE = 256
EPS = 0.0004
K0 = math.sqrt(2.0 / math.pi)
K1 = K0 * 0.044715
SLAB = 512
EXTRA_ROWS = 8
VMEM = 8 * 1024 * 1024
NT = (((1,), (1,)), ((), ()))


def column(row, size):
    r = lax.broadcasted_iota(jnp.int32, (size, size), 0)
    c = lax.broadcasted_iota(jnp.int32, (size, size), 1)
    return jnp.sum(jnp.where(r == c, row, 0.0), axis=1, keepdims=True)


def field_rows(v, mloc, m, r0):
    full = v // 8 * 8
    if r0 < full:
        return pl.ds(m * full + r0, 8)
    return pl.ds(mloc * full + m * (v - full), v - full)


def forward_kernel(hid_ref, w_ref, b_ref, wo_ref, bo_ref, act_ref, slope_ref, f_ref, bias, half, *slabs):
    step = pl.program_id(0)
    mloc, h, t = hid_ref.shape
    v = half.shape[0]
    size = h // len(slabs)

    @pl.when(step == 0)
    def _():
        for k in range(h // 128):
            bias[pl.ds(k * 128, 128), :] = jnp.broadcast_to(
                column(b_ref[:, pl.ds(k * 128, 128)], 128), (128, 128)
            )
        half[...] = wo_ref[...] * jnp.bfloat16(0.5)

    hid = jnp.concatenate([hid_ref[m] for m in range(mloc)], axis=1)
    for k, slab in enumerate(slabs):
        rows = pl.ds(k * size, size)
        slab[...] = jnp.dot(w_ref[rows, :], hid, preferred_element_type=jnp.float32)
    out = jnp.broadcast_to(column(bo_ref[...], v), (v, mloc * t))
    for k, slab in enumerate(slabs):
        for r in range(0, size, 16):
            rows = pl.ds(k * size + r, 16)
            b = jnp.concatenate([bias[rows, :]] * (t // 128), axis=1)
            for m in range(mloc):
                x = slab[pl.ds(r, 16), pl.ds(m * t, t)] + b
                q = x * x * K1
                th = jnp.tanh(x * (K0 + q))
                up = 1.0 + th
                act = x * up
                act_ref[step, m, rows, :] = act.astype(jnp.bfloat16)
                slope_ref[step, m, rows, :] = up + act * ((1.0 - th) * (K0 + 3.0 * q))
        rows = pl.ds(k * size, size)
        act = jnp.concatenate([act_ref[step, m, rows, :] for m in range(mloc)], axis=1)
        out = out + jnp.dot(half[:, rows], act, preferred_element_type=jnp.float32)
    for m in range(mloc):
        for r0 in range(0, v, 8):
            f_ref[field_rows(v, mloc, m, r0), :] = out[r0 : r0 + 8, m * t : (m + 1) * t]


def forward(start, p, hidden, w_inner, b_inner, w_out, b_out, vmem):
    mloc, h, n = hidden.shape
    v = w_out.shape[0]
    t = TILE
    tiles = p // t
    whole = lambda s: (0, 0)
    once = pl.Buffered(1)
    shape = (p // t, mloc, h, t)
    held = pl.BlockSpec(shape, lambda s: (0, 0, 0, 0))
    return pl.pallas_call(
        forward_kernel,
        grid=(tiles,),
        in_specs=[
            pl.BlockSpec((mloc, h, t), lambda s: (0, 0, start // t + s)),
            pl.BlockSpec((h, h), whole, pipeline_mode=once),
            pl.BlockSpec((1, h), whole, pipeline_mode=once),
            pl.BlockSpec((v, h), whole, pipeline_mode=once),
            pl.BlockSpec((1, v), whole, pipeline_mode=once),
        ],
        out_specs=[
            held,
            held,
            pl.BlockSpec((mloc * v, t), lambda s: (0, s)),
        ],
        out_shape=[
            pltpu.VMEM(shape, jnp.bfloat16),
            pltpu.VMEM(shape, jnp.float32),
            jax.ShapeDtypeStruct((mloc * v, p), jnp.float32),
        ],
        scratch_shapes=[
            pltpu.VMEM((h, 128), jnp.float32),
            pltpu.VMEM((v, h), jnp.bfloat16),
            pltpu.VMEM((h // 2, mloc * t), jnp.float32),
            pltpu.VMEM((h // 2, mloc * t), jnp.float32),
        ],
        compiler_params=pltpu.CompilerParams(vmem_limit_bytes=vmem),
        cost_estimate=pl.CostEstimate(
            flops=2 * h * h, bytes_accessed=2 * h * h, transcendentals=0
        ),
        name="forward_part",
    )(hidden, w_inner, b_inner, w_out, b_out)


def backward_kernel(
    first, last, dims, members,
    f_ref, fc_ref, fx_ref, fxc_ref, target_ref, area_ref, vw_ref, act_ref, slope_ref, hid_ref,
    wot_ref, acc_in, extra_in, gp_ref, extra_ref, *refs,
):
    acc, *refs = refs
    if last:
        keep_x, send_x, keep_y, send_y, *refs = refs
    (gf,) = refs
    step = pl.program_id(0)
    end = pl.num_programs(0) - 1
    mloc, _, t = hid_ref.shape
    v = target_ref.shape[0]
    h = wot_ref.shape[0]
    denom = members * (members - 1)

    def pair(a, b):
        d = a - b
        s = d * d + EPS
        r = lax.rsqrt(s)
        return d * r, s * r

    def scores(r0, vw, area):
        rows = pl.ds(r0, min(8, v - r0))
        places = [field_rows(v, mloc, m, r0) for m in range(mloc)]
        own = [f_ref[place, :] for place in places]
        others = [ref[place, :] for ref in (fc_ref, fx_ref, fxc_ref) for place in places]
        target = target_ref[rows, :]
        dsum = [jnp.zeros_like(target) for _ in range(mloc)]
        obs = []
        cross = inner = near = jnp.zeros_like(target)
        n_cross = n_inner = 0
        for i in range(mloc):
            sl, ph = pair(own[i], target)
            obs.append(sl)
            near = near + ph
            for b in others:
                sl, ph = pair(own[i], b)
                dsum[i] = dsum[i] + sl
                cross = cross + ph
                n_cross += 1
            for j in range(i + 1, mloc):
                sl, ph = pair(own[i], own[j])
                dsum[i] = dsum[i] + sl
                dsum[j] = dsum[j] - sl
                inner = inner + ph
                n_inner += 1
        weight = vw[r0 : r0 + 8] * area
        for m in range(mloc):
            gf[m, rows, :] = weight * (obs[m] * (1.0 / members) - dsum[m] * (1.0 / denom))
        near = (near - 0.02 * mloc) * (1.0 / members)
        pairs = (inner - 0.02 * n_inner) + 0.5 * (cross - 0.02 * n_cross)
        return jnp.sum(weight * (near - pairs * (1.0 / denom)), axis=0, keepdims=True)

    def weights(k):
        rows = pl.ds(k, SLAB)
        hid = jnp.concatenate([hid_ref[m] for m in range(mloc)], axis=1)
        acc[rows, :] += lax.dot_general(
            gp_ref[step - 1, rows, :], hid, NT, preferred_element_type=jnp.float32
        )

    def work(with_weights):
        vw, area = column(vw_ref[...], v), area_ref[...]
        starts = list(range(0, v, 8))
        slabs = list(range(0, h, SLAB)) if with_weights else [None]
        loss = jnp.zeros((1, t), jnp.float32)
        for k, slab in enumerate(slabs):
            if with_weights:
                weights(slab)
            for r0 in starts[k :: len(slabs)]:
                loss = loss + scores(r0, vw, area)
        for m in range(mloc):
            gf[m, pl.ds(v, gf.shape[1] - v), :] = jnp.zeros((gf.shape[1] - v, t), jnp.float32)
        g = jnp.concatenate([gf[m] for m in range(mloc)], axis=1).astype(jnp.bfloat16)
        for k in range(0, h, 256):
            rows = pl.ds(k, 256)
            ga = jnp.dot(wot_ref[rows, :], g, preferred_element_type=jnp.float32)
            for m in range(mloc):
                piece = ga[:, m * t : (m + 1) * t] * slope_ref[step, m, rows, :]
                gp_ref[step, rows, pl.ds(m * t, t)] = piece.astype(jnp.bfloat16)
        act = jnp.concatenate([act_ref[step, m] for m in range(mloc)], axis=1)
        extra_ref[...] += lax.dot_general(g, act, NT, preferred_element_type=jnp.float32)
        extra_ref[pl.ds(v, 1), pl.ds(0, t)] += loss

    @pl.when(step == 0)
    def _():
        if first:
            acc[...] = jnp.zeros_like(acc)
            extra_ref[...] = jnp.zeros_like(extra_ref)
        else:
            extra_ref[...] = extra_in[...]
        work(False)

    @pl.when((step > 0) & (step < end))
    def _():
        work(True)

    @pl.when(step == end)
    def _():
        for k in range(0, h, SLAB):
            weights(k)

    if last:
        n_hi, n_lo = dims

        @pl.when(step == end)
        def _():
            mem = lax.axis_index("mem")
            grid = lax.axis_index("grid")
            x, core = mem // 2, mem % 2
            hi, lo = grid // n_lo, grid % n_lo
            r = h // (2 * n_hi * n_lo)
            cx = keep_x.shape[4]
            for dlo in range(n_lo):
                for dhi in range(n_hi):
                    g = lax.rem(hi + dhi, n_hi) * n_lo + lax.rem(lo + dlo, n_lo)
                    block = dhi * n_lo + lax.rem(lo + dlo, n_lo)
                    for c, to_x, to_y in ((core, keep_x, keep_y), (1 - core, send_x, send_y)):
                        r0 = pl.multiple_of((g * 2 + c) * r, r)
                        total = acc[pl.ds(r0, r), :]
                        e0 = (c * (n_hi * n_lo) + block) * EXTRA_ROWS
                        at = pl.multiple_of(
                            jnp.minimum(e0, extra_ref.shape[0] - EXTRA_ROWS), EXTRA_ROWS
                        )
                        e = jnp.where(
                            e0 < extra_ref.shape[0], extra_ref[pl.ds(at, EXTRA_ROWS), :], 0.0
                        )
                        for values, rows in ((total, pl.ds(0, r)), (e, pl.ds(r, EXTRA_ROWS))):
                            q = [values[:, k * cx : (k + 1) * cx] for k in range(4)]
                            for d in range(2):
                                own = x == d
                                to_x[d, dlo, dhi, rows, :] = jnp.where(own, q[0], q[1])
                                to_y[dlo, d, dhi, rows, :] = jnp.where(own, q[2], q[3])


def backward(start, p, first, last, dims, members, fields, rest, acc, extra):
    target, area, vw, act, slope, hidden, wot = rest
    mloc, h, n = hidden.shape
    v = target.shape[0]
    vp = wot.shape[1]
    t = TILE
    off = start // t
    once = pl.Buffered(1)
    steps = p // t
    ahead = lambda s: jnp.minimum(s, steps - 1)
    f_spec = pl.BlockSpec((mloc * v, t), lambda s: (0, ahead(s)))
    whole = lambda s: (0, 0)
    const = lambda a: pl.BlockSpec(a.shape, whole, pipeline_mode=once)
    held = lambda a: pl.BlockSpec(a.shape, lambda s: (0,) * len(a.shape))
    in_specs = [f_spec] * 4 + [
        pl.BlockSpec((v, t), lambda s: (0, off + ahead(s))),
        pl.BlockSpec((1, t), lambda s: (0, off + ahead(s))),
        const(vw), held(act), held(slope),
        pl.BlockSpec((mloc, h, t), lambda s: (0, 0, off + jnp.maximum(s - 1, 0))),
        const(wot),
    ]
    act, slope = (pltpu.with_memory_space_constraint(a, pltpu.VMEM) for a in (act, slope))
    args = [*fields, target, area, vw, act, slope, hidden, wot]
    kernel = functools.partial(backward_kernel, first, last, dims, members)
    if first:
        kernel_fn = lambda *refs: kernel(*refs[:11], None, None, *refs[11:])
        aliases = {}
    else:
        kernel_fn = kernel
        in_specs += [held(acc), const(extra)]
        args += [acc, extra]
        aliases = {11: 2}
    out_shape = [
        pltpu.VMEM((p // t, h, mloc * t), jnp.bfloat16),
        jax.ShapeDtypeStruct((vp, h), jnp.float32),
        pltpu.VMEM((h, h), jnp.float32),
    ]
    if last:
        n_hi, n_lo = dims
        r = h // (2 * n_hi * n_lo)
        cx = h // 4
        out_shape += [pltpu.VMEM((2, n_lo, n_hi, r + EXTRA_ROWS, cx), jnp.float32)] * 2
        out_shape += [pltpu.VMEM((n_lo, 2, n_hi, r + EXTRA_ROWS, cx), jnp.float32)] * 2
    out_specs = [held(a) for a in out_shape]
    return pl.pallas_call(
        kernel_fn,
        grid=(steps + 1,),
        in_specs=in_specs,
        out_specs=out_specs,
        out_shape=out_shape,
        scratch_shapes=[pltpu.VMEM((mloc, vp, t), jnp.float32)],
        input_output_aliases=aliases,
        compiler_params=pltpu.CompilerParams(vmem_limit_bytes=VMEM),
        cost_estimate=pl.CostEstimate(
            flops=2 * h * h, bytes_accessed=2 * h * h, transcendentals=0
        ),
        name="backward_part",
    )(*args)


def transposes_kernel(w_ref, wo_ref, wt_ref, wot_ref):
    wt_ref[...] = w_ref[...].astype(jnp.float32).T.astype(jnp.bfloat16)

    @pl.when(pl.program_id(0) == 0)
    def _():
        v, h = wo_ref.shape
        rows = jnp.concatenate(
            [wo_ref[...].astype(jnp.float32) * 0.5, jnp.zeros((wot_ref.shape[1] - v, h), jnp.float32)], 0
        )
        wot_ref[...] = rows.T.astype(jnp.bfloat16)


def transposes(w_inner, w_out, vp):
    v, h = w_out.shape
    t = TILE
    return pl.pallas_call(
        transposes_kernel,
        grid=(h // t,),
        in_specs=[
            pl.BlockSpec((t, h), lambda s: (s, 0)),
            pl.BlockSpec((v, h), lambda s: (0, 0)),
        ],
        out_specs=[
            pl.BlockSpec((h, t), lambda s: (0, s)),
            pl.BlockSpec((h, vp), lambda s: (0, 0)),
        ],
        out_shape=[pltpu.VMEM((h, h), jnp.bfloat16), pltpu.VMEM((h, vp), jnp.bfloat16)],
        compiler_params=pltpu.CompilerParams(vmem_limit_bytes=VMEM),
        cost_estimate=pl.CostEstimate(flops=2 * h, bytes_accessed=2 * h, transcendentals=0),
        name="transposes",
    )(w_inner, w_out)


def input_kernel(wt_ref, gp_ref, *refs):
    mloc, h, t = refs[-1].shape
    for k in range(0, h, SLAB):
        rows = pl.ds(k, SLAB)
        out = jnp.dot(wt_ref[rows, :], gp_ref[pl.program_id(0)], preferred_element_type=jnp.float32)
        for m in range(mloc):
            refs[-1][m, rows, :] = out[:, m * t : (m + 1) * t].astype(jnp.bfloat16)


def input_gradient(start, p, n, wt, gp, gh):
    steps, h, width = gp.shape
    t = TILE
    mloc = width // t
    off = start // t
    in_specs = [
        pl.BlockSpec((h, h), lambda s: (0, 0), pipeline_mode=pl.Buffered(1)),
        pl.BlockSpec(gp.shape, lambda s: (0, 0, 0)),
    ]
    args = [wt, gp]
    if gh is not None:
        in_specs.append(pl.BlockSpec(memory_space=pl.ANY))
        args.append(gh)
    return pl.pallas_call(
        input_kernel,
        grid=(steps,),
        in_specs=in_specs,
        out_specs=pl.BlockSpec((mloc, h, t), lambda s: (0, 0, off + s)),
        out_shape=jax.ShapeDtypeStruct((mloc, h, n), jnp.bfloat16),
        input_output_aliases={} if gh is None else {2: 0},
        compiler_params=pltpu.CompilerParams(vmem_limit_bytes=VMEM),
        cost_estimate=pl.CostEstimate(
            flops=2 * h * h, bytes_accessed=2 * h * h, transcendentals=0
        ),
        name="grad_hidden_part",
    )(*args)


def after(value, *others):
    return lax.optimization_barrier((value,) + others)[0]


def shards(hidden, target, area, var_weight, w_inner, b_inner, w_out, b_out):
    mloc, h, n = hidden.shape
    n_mem = lax.axis_size("mem")
    n_grid = lax.axis_size("grid")
    members = mloc * n_mem
    npoints = n * n_grid
    v = w_out.shape[0]
    vp = 128
    n_lo = 2
    while n_lo * n_lo * 4 <= n_grid:
        n_lo *= 2
    n_hi = n_grid // n_lo

    swap_x = [(i, (i + n_mem // 2) % n_mem) for i in range(n_mem)]
    swap_core = [(i, i ^ 1) for i in range(n_mem)]

    def shift_lo(k):
        return [(a * n_lo + b, a * n_lo + (b + k) % n_lo) for a in range(n_hi) for b in range(n_lo)]

    def shift_hi(k):
        return [(a * n_lo + b, (a + k) % n_hi * n_lo + b) for a in range(n_hi) for b in range(n_lo)]

    to_x = lambda a: lax.ppermute(a, "mem", swap_x)
    to_core = lambda a: lax.ppermute(a, "mem", swap_core)
    to_lo = lambda a, k: lax.ppermute(a, "grid", shift_lo(k))
    to_hi = lambda a, k: lax.ppermute(a, "grid", shift_hi(k))

    mem, grid = lax.axis_index("mem"), lax.axis_index("grid")
    at_zero = {("mem", bit): mem & bit == 0 for bit in (1, n_mem // 2)}
    bit = 1
    while bit < n_lo:
        at_zero["grid", bit] = grid & bit == 0
        bit *= 2
    hidden, at_zero = lax.optimization_barrier((hidden, at_zero))
    hidden, w_out, b_inner, b_out = (
        pltpu.with_memory_space_constraint(a, pltpu.HBM)
        for a in (hidden, w_out, b_inner.reshape(1, h), b_out.reshape(1, v))
    )
    unit = n // sum(EIGHTHS)
    starts = [unit * sum(EIGHTHS[:k]) for k in range(len(EIGHTHS))]
    spans = [(start, unit * size) for start, size in zip(starts, EIGHTHS)]
    parts, far = [], []
    for start, p in spans:
        w, vmem = w_inner, VMEM
        if parts:
            b_out = after(b_out, parts[-1][2])
        else:
            w = pltpu.with_memory_space_constraint(w_inner, pltpu.HBM)
            vmem += 4 * h * h
        parts.append(forward(start, p, hidden, w, b_inner, w_out, b_out, vmem))
        far.append(to_x(parts[-1][2]))
    near = [to_core(fields) for _, _, fields in parts]
    wt, wot = transposes(after(w_inner, parts[-1][2]), w_out, vp)
    vw, area = var_weight.reshape(1, v), area.reshape(1, n)
    acc = extra = gh = None
    grad_pre = []
    for k, (start, p) in enumerate(spans):
        act, slope, fields = parts[k]
        first, last = k == 0, k == len(spans) - 1
        if k:
            far[k] = after(far[k], parts[-1][2] if k == 1 else grad_pre[k - 2])
        gp, extra, acc, *accs = backward(
            start, p, first, last, (n_hi, n_lo), members,
            (fields, near[k], far[k], to_core(far[k])),
            (target, area, vw, act, slope, hidden, wot), acc, extra,
        )
        grad_pre.append(gp)
    keep_x, send_x, keep_y, send_y = accs

    def gathered(block, axis, name, bit):
        n = lax.axis_size(name)
        other = lax.ppermute(block, name, [(i, i ^ bit) for i in range(n)])
        return ordered(block, other, axis, name, bit)

    def ordered(block, other, axis, name, bit):
        return jnp.where(
            at_zero[name, bit],
            jnp.concatenate([block, other], axis),
            jnp.concatenate([other, block], axis),
        )

    def beside(k, gh, start_after, wait_for):
        gh = input_gradient(*spans[k], n, wt, after(grad_pre[k], start_after), gh)
        return lax.optimization_barrier((gh, wait_for))

    r, cx = h // (2 * n_grid), keep_x.shape[-1]
    others = range(1, n_lo)
    got_x = to_core(send_x)
    got_y = to_core(send_y)
    out_x = keep_x[1] + got_x[1]
    out_y = [keep_y[k] + got_y[k] for k in others]
    from_x = to_x(out_x)
    from_y = [to_lo(out_y[k - 1], k) for k in others]
    for k in (0, 1):
        gh, (keep_x, keep_y) = beside(k, gh, (out_x, out_y), (keep_x, keep_y))
    own_x = keep_x[0] + got_x[0] + from_x
    own_y = sum(from_y, keep_y[0] + got_y[0])
    own_x, own_y = [own_x[k] for k in range(n_lo)], [own_y[k] for k in range(2)]
    from_y = [to_lo(own_x[k], k) for k in others]
    from_x = to_x(own_y[1])
    gh, (own_x, own_y) = beside(2, gh, (own_x[1:], own_y[1]), (own_x[0], own_y[0]))
    sums = [sum(from_y, own_x), own_y + from_x]

    extra = [part[:, r:].reshape(-1, cx) for part in sums]
    pieces = [jnp.concatenate([part[k, :r] for part in sums] + extra, 0) for k in range(n_hi)]
    from_hi = [to_hi(pieces[k], k) for k in range(1, n_hi)]
    gh, own = beside(3, gh, pieces[1:], pieces[0])
    total = sum(from_hi, own)
    far = to_x(total)
    mine = total[2 * r :][None]
    beyond = lax.ppermute(mine, "grid", [(g, g ^ 1) for g in range(n_grid)])
    pairs = [(m * n_grid + g, (m + n_mem // 2) % n_mem * n_grid + (g ^ 1)) for m in range(n_mem) for g in range(n_grid)]
    across = lax.ppermute(mine, ("mem", "grid"), pairs)

    scale = 1.0 / math.sqrt(members * npoints)
    halves = [ordered(total[k : k + r], far[k : k + r], 1, "mem", n_mem // 2) for k in (0, r)]
    grad_inner = gathered(jnp.concatenate(halves, 1) * scale, 0, "mem", 1)

    sides = [ordered(mine, far[2 * r :][None], 0, "mem", n_mem // 2)]
    sides.append(ordered(beyond, across, 0, "mem", n_mem // 2))
    extra = ordered(*(side[None] for side in sides), 0, "grid", 1)
    bit = 2
    while bit < n_lo:
        extra = gathered(extra, 0, "grid", bit)
        bit *= 2
    extra = gathered(extra[None], 0, "mem", 1)
    extra = extra.reshape(2, n_lo, 2, 2, n_hi, EXTRA_ROWS, cx)
    extra = extra.transpose(0, 4, 1, 5, 3, 2, 6).reshape(2 * n_grid * EXTRA_ROWS, h)
    loss = jnp.sum(extra[v]) / npoints
    return (loss, gh, grad_inner, extra[:v] * (0.5 * scale))


def solution(mesh):
    in_specs = (P("mem", None, "grid"), P(None, "grid"), P("grid"), P(), P(), P(), P(), P())
    out_specs = (P(), P("mem", None, "grid"), P("grid", None), P())
    return jax.shard_map(shards, mesh=mesh, in_specs=in_specs, out_specs=out_specs, check_vma=False)
```

```python
import functools
import math

import jax
import jax.numpy as jnp
from jax import lax
from jax.experimental import pallas as pl
from jax.experimental.pallas import tpu as pltpu
from jax.sharding import PartitionSpec as P

EIGHTHS = (2, 2, 2, 2)
TILE = 256
EPS = 0.0004
K0 = math.sqrt(2.0 / math.pi)
K1 = K0 * 0.044715
SLAB = 256
EXTRA_ROWS = 8
VMEM = 8 * 1024 * 1024
NT = (((1,), (1,)), ((), ()))


def column(row, size):
    r = lax.broadcasted_iota(jnp.int32, (size, size), 0)
    c = lax.broadcasted_iota(jnp.int32, (size, size), 1)
    return jnp.sum(jnp.where(r == c, row, 0.0), axis=1, keepdims=True)


def field_rows(v, mloc, m, r0):
    full = v // 8 * 8
    if r0 < full:
        return pl.ds(m * full + r0, 8)
    return pl.ds(mloc * full + m * (v - full), v - full)


def forward_kernel(hid_ref, w_ref, b_ref, wo_ref, bo_ref, act_ref, slope_ref, f_ref, bias, half, *slabs):
    step = pl.program_id(0)
    mloc, h, t = hid_ref.shape
    v = half.shape[0]
    size = h // len(slabs)

    @pl.when(step == 0)
    def _():
        for k in range(h // 128):
            bias[pl.ds(k * 128, 128), :] = jnp.broadcast_to(
                column(b_ref[:, pl.ds(k * 128, 128)], 128), (128, 128)
            )
        half[...] = wo_ref[...] * jnp.bfloat16(0.5)

    hid = jnp.concatenate([hid_ref[m] for m in range(mloc)], axis=1)
    out = jnp.broadcast_to(column(bo_ref[...], v), (v, mloc * t))
    for k in range(len(slabs) + 1):
        if k < len(slabs):
            rows = pl.ds(k * size, size)
            slabs[k][...] = jnp.dot(w_ref[rows, :], hid, preferred_element_type=jnp.float32)
        if k == 0:
            continue
        slab, start = slabs[k - 1], (k - 1) * size
        for r in range(0, size, 16):
            rows = pl.ds(start + r, 16)
            b = jnp.concatenate([bias[rows, :]] * (t // 128), axis=1)
            for m in range(mloc):
                x = slab[pl.ds(r, 16), pl.ds(m * t, t)] + b
                q = x * x * K1
                th = jnp.tanh(x * (K0 + q))
                up = 1.0 + th
                act = x * up
                act_ref[step, m, rows, :] = act.astype(jnp.bfloat16)
                slope_ref[step, m, rows, :] = up + act * ((1.0 - th) * (K0 + 3.0 * q))
        rows = pl.ds(start, size)
        act = jnp.concatenate([act_ref[step, m, rows, :] for m in range(mloc)], axis=1)
        out = out + jnp.dot(half[:, rows], act, preferred_element_type=jnp.float32)
    for m in range(mloc):
        for r0 in range(0, v, 8):
            f_ref[field_rows(v, mloc, m, r0), :] = out[r0 : r0 + 8, m * t : (m + 1) * t]


def forward(start, p, hidden, w_inner, b_inner, w_out, b_out, vmem):
    mloc, h, n = hidden.shape
    v = w_out.shape[0]
    t = TILE
    tiles = p // t
    whole = lambda s: (0, 0)
    once = pl.Buffered(1)
    shape = (p // t, mloc, h, t)
    held = pl.BlockSpec(shape, lambda s: (0, 0, 0, 0))
    return pl.pallas_call(
        forward_kernel,
        grid=(tiles,),
        in_specs=[
            pl.BlockSpec((mloc, h, t), lambda s: (0, 0, start // t + s)),
            pl.BlockSpec((h, h), whole, pipeline_mode=once),
            pl.BlockSpec((1, h), whole, pipeline_mode=once),
            pl.BlockSpec((v, h), whole, pipeline_mode=once),
            pl.BlockSpec((1, v), whole, pipeline_mode=once),
        ],
        out_specs=[
            held,
            held,
            pl.BlockSpec((mloc * v, t), lambda s: (0, s)),
        ],
        out_shape=[
            pltpu.VMEM(shape, jnp.bfloat16),
            pltpu.VMEM(shape, jnp.float32),
            jax.ShapeDtypeStruct((mloc * v, p), jnp.float32),
        ],
        scratch_shapes=[
            pltpu.VMEM((h, 128), jnp.float32),
            pltpu.VMEM((v, h), jnp.bfloat16),
        ]
        + [pltpu.VMEM((SLAB, mloc * t), jnp.float32)] * (h // SLAB),
        compiler_params=pltpu.CompilerParams(vmem_limit_bytes=vmem),
        cost_estimate=pl.CostEstimate(
            flops=2 * h * h, bytes_accessed=2 * h * h, transcendentals=0
        ),
        name="forward_part",
    )(hidden, w_inner, b_inner, w_out, b_out)


def backward_kernel(
    first, last, dims, members,
    f_ref, fc_ref, fx_ref, fxc_ref, target_ref, area_ref, vw_ref, act_ref, slope_ref, hid_ref,
    wot_ref, acc_in, extra_in, gp_ref, extra_ref, *refs,
):
    acc, *refs = refs
    if last:
        keep_x, send_x, keep_y, send_y, *refs = refs
    (gf,) = refs
    step = pl.program_id(0)
    end = pl.num_programs(0) - 1
    mloc, _, t = hid_ref.shape
    v = target_ref.shape[0]
    h = wot_ref.shape[0]
    denom = members * (members - 1)

    def pair(a, b):
        d = a - b
        s = d * d + EPS
        r = lax.rsqrt(s)
        return d * r, s * r

    def scores(r0, vw, area):
        rows = pl.ds(r0, min(8, v - r0))
        places = [field_rows(v, mloc, m, r0) for m in range(mloc)]
        own = [f_ref[place, :] for place in places]
        others = [ref[place, :] for ref in (fc_ref, fx_ref, fxc_ref) for place in places]
        target = target_ref[rows, :]
        dsum = [jnp.zeros_like(target) for _ in range(mloc)]
        obs = []
        cross = inner = near = jnp.zeros_like(target)
        n_cross = n_inner = 0
        for i in range(mloc):
            sl, ph = pair(own[i], target)
            obs.append(sl)
            near = near + ph
            for b in others:
                sl, ph = pair(own[i], b)
                dsum[i] = dsum[i] + sl
                cross = cross + ph
                n_cross += 1
            for j in range(i + 1, mloc):
                sl, ph = pair(own[i], own[j])
                dsum[i] = dsum[i] + sl
                dsum[j] = dsum[j] - sl
                inner = inner + ph
                n_inner += 1
        weight = vw[r0 : r0 + 8] * area
        for m in range(mloc):
            gf[m, rows, :] = weight * (obs[m] * (1.0 / members) - dsum[m] * (1.0 / denom))
        near = (near - 0.02 * mloc) * (1.0 / members)
        pairs = (inner - 0.02 * n_inner) + 0.5 * (cross - 0.02 * n_cross)
        return jnp.sum(weight * (near - pairs * (1.0 / denom)), axis=0, keepdims=True)

    def weights(k):
        rows = pl.ds(k, SLAB)
        hid = jnp.concatenate([hid_ref[m] for m in range(mloc)], axis=1)
        acc[rows, :] += lax.dot_general(
            gp_ref[step - 1, rows, :], hid, NT, preferred_element_type=jnp.float32
        )

    def work(with_weights):
        vw, area = column(vw_ref[...], v), area_ref[...]
        starts = list(range(0, v, 8))
        slabs = list(range(0, h, SLAB)) if with_weights else [None]
        loss = jnp.zeros((1, t), jnp.float32)
        for k, slab in enumerate(slabs):
            if with_weights:
                weights(slab)
            for r0 in starts[k :: len(slabs)]:
                loss = loss + scores(r0, vw, area)
        for m in range(mloc):
            gf[m, pl.ds(v, gf.shape[1] - v), :] = jnp.zeros((gf.shape[1] - v, t), jnp.float32)
        g = jnp.concatenate([gf[m] for m in range(mloc)], axis=1).astype(jnp.bfloat16)
        for k in range(0, h, 256):
            rows = pl.ds(k, 256)
            ga = jnp.dot(wot_ref[rows, :], g, preferred_element_type=jnp.float32)
            for m in range(mloc):
                piece = ga[:, m * t : (m + 1) * t] * slope_ref[step, m, rows, :]
                gp_ref[step, rows, pl.ds(m * t, t)] = piece.astype(jnp.bfloat16)
        act = jnp.concatenate([act_ref[step, m] for m in range(mloc)], axis=1)
        extra_ref[...] += lax.dot_general(g, act, NT, preferred_element_type=jnp.float32)
        extra_ref[pl.ds(v, 1), pl.ds(0, t)] += loss

    @pl.when(step == 0)
    def _():
        if first:
            acc[...] = jnp.zeros_like(acc)
            extra_ref[...] = jnp.zeros_like(extra_ref)
        else:
            extra_ref[...] = extra_in[...]
        work(False)

    @pl.when((step > 0) & (step < end))
    def _():
        work(True)

    @pl.when(step == end)
    def _():
        for k in range(0, h, SLAB):
            weights(k)

    if last:
        n_hi, n_lo = dims

        @pl.when(step == end)
        def _():
            mem = lax.axis_index("mem")
            grid = lax.axis_index("grid")
            x, core = mem // 2, mem % 2
            hi, lo = grid // n_lo, grid % n_lo
            r = h // (2 * n_hi * n_lo)
            cx = keep_x.shape[4]
            for dlo in range(n_lo):
                for dhi in range(n_hi):
                    g = lax.rem(hi + dhi, n_hi) * n_lo + lax.rem(lo + dlo, n_lo)
                    block = dhi * n_lo + lax.rem(lo + dlo, n_lo)
                    for c, to_x, to_y in ((core, keep_x, keep_y), (1 - core, send_x, send_y)):
                        r0 = pl.multiple_of((g * 2 + c) * r, r)
                        total = acc[pl.ds(r0, r), :]
                        e0 = (c * (n_hi * n_lo) + block) * EXTRA_ROWS
                        at = pl.multiple_of(
                            jnp.minimum(e0, extra_ref.shape[0] - EXTRA_ROWS), EXTRA_ROWS
                        )
                        e = jnp.where(
                            e0 < extra_ref.shape[0], extra_ref[pl.ds(at, EXTRA_ROWS), :], 0.0
                        )
                        for values, rows in ((total, pl.ds(0, r)), (e, pl.ds(r, EXTRA_ROWS))):
                            q = [values[:, k * cx : (k + 1) * cx] for k in range(4)]
                            for d in range(2):
                                own = x == d
                                to_x[d, dlo, dhi, rows, :] = jnp.where(own, q[0], q[1])
                                to_y[dlo, d, dhi, rows, :] = jnp.where(own, q[2], q[3])


def backward(start, p, first, last, dims, members, fields, rest, acc, extra):
    target, area, vw, act, slope, hidden, wot = rest
    mloc, h, n = hidden.shape
    v = target.shape[0]
    vp = wot.shape[1]
    t = TILE
    off = start // t
    once = pl.Buffered(1)
    steps = p // t
    ahead = lambda s: jnp.minimum(s, steps - 1)
    f_spec = pl.BlockSpec((mloc * v, t), lambda s: (0, ahead(s)))
    whole = lambda s: (0, 0)
    const = lambda a: pl.BlockSpec(a.shape, whole, pipeline_mode=once)
    held = lambda a: pl.BlockSpec(a.shape, lambda s: (0,) * len(a.shape))
    in_specs = [f_spec] * 4 + [
        pl.BlockSpec((v, t), lambda s: (0, off + ahead(s))),
        pl.BlockSpec((1, t), lambda s: (0, off + ahead(s))),
        const(vw), held(act), held(slope),
        pl.BlockSpec((mloc, h, t), lambda s: (0, 0, off + jnp.maximum(s - 1, 0))),
        const(wot),
    ]
    act, slope = (pltpu.with_memory_space_constraint(a, pltpu.VMEM) for a in (act, slope))
    args = [*fields, target, area, vw, act, slope, hidden, wot]
    kernel = functools.partial(backward_kernel, first, last, dims, members)
    if first:
        kernel_fn = lambda *refs: kernel(*refs[:11], None, None, *refs[11:])
        aliases = {}
    else:
        kernel_fn = kernel
        in_specs += [held(acc), const(extra)]
        args += [acc, extra]
        aliases = {11: 2}
    out_shape = [
        pltpu.VMEM((p // t, h, mloc * t), jnp.bfloat16),
        jax.ShapeDtypeStruct((vp, h), jnp.float32),
        pltpu.VMEM((h, h), jnp.float32),
    ]
    if last:
        n_hi, n_lo = dims
        r = h // (2 * n_hi * n_lo)
        cx = h // 4
        out_shape += [pltpu.VMEM((2, n_lo, n_hi, r + EXTRA_ROWS, cx), jnp.float32)] * 2
        out_shape += [pltpu.VMEM((n_lo, 2, n_hi, r + EXTRA_ROWS, cx), jnp.float32)] * 2
    out_specs = [held(a) for a in out_shape]
    return pl.pallas_call(
        kernel_fn,
        grid=(steps + 1,),
        in_specs=in_specs,
        out_specs=out_specs,
        out_shape=out_shape,
        scratch_shapes=[pltpu.VMEM((mloc, vp, t), jnp.float32)],
        input_output_aliases=aliases,
        compiler_params=pltpu.CompilerParams(vmem_limit_bytes=VMEM),
        cost_estimate=pl.CostEstimate(
            flops=2 * h * h, bytes_accessed=2 * h * h, transcendentals=0
        ),
        name="backward_part",
    )(*args)


def transposes_kernel(w_ref, wo_ref, wt_ref, wot_ref):
    wt_ref[...] = w_ref[...].astype(jnp.float32).T.astype(jnp.bfloat16)

    @pl.when(pl.program_id(0) == 0)
    def _():
        v, h = wo_ref.shape
        rows = jnp.concatenate(
            [wo_ref[...].astype(jnp.float32) * 0.5, jnp.zeros((wot_ref.shape[1] - v, h), jnp.float32)], 0
        )
        wot_ref[...] = rows.T.astype(jnp.bfloat16)


def transposes(w_inner, w_out, vp):
    v, h = w_out.shape
    t = TILE
    return pl.pallas_call(
        transposes_kernel,
        grid=(h // t,),
        in_specs=[
            pl.BlockSpec((t, h), lambda s: (s, 0)),
            pl.BlockSpec((v, h), lambda s: (0, 0)),
        ],
        out_specs=[
            pl.BlockSpec((h, t), lambda s: (0, s)),
            pl.BlockSpec((h, vp), lambda s: (0, 0)),
        ],
        out_shape=[pltpu.VMEM((h, h), jnp.bfloat16), pltpu.VMEM((h, vp), jnp.bfloat16)],
        compiler_params=pltpu.CompilerParams(vmem_limit_bytes=VMEM),
        cost_estimate=pl.CostEstimate(flops=2 * h, bytes_accessed=2 * h, transcendentals=0),
        name="transposes",
    )(w_inner, w_out)


def input_kernel(wt_ref, gp_ref, *refs):
    mloc, h, t = refs[-1].shape
    for k in range(0, h, SLAB):
        rows = pl.ds(k, SLAB)
        out = jnp.dot(wt_ref[rows, :], gp_ref[pl.program_id(0)], preferred_element_type=jnp.float32)
        for m in range(mloc):
            refs[-1][m, rows, :] = out[:, m * t : (m + 1) * t].astype(jnp.bfloat16)


def last_kernel(n_hi, n_lo, scale, npoints, own_ref, other_ref, e_ref, f_ref, inner_ref, out_ref, loss_ref):
    core = lax.axis_index("mem") % 2
    r = own_ref.shape[0]
    inner_ref[pl.ds(pl.multiple_of(core * r, r), r), :] = own_ref[...] * scale
    inner_ref[pl.ds(pl.multiple_of((1 - core) * r, r), r), :] = other_ref[...] * scale
    v = out_ref.shape[0]
    cx = e_ref.shape[-1]
    for row in range(0, v + 1, EXTRA_ROWS):
        c, g = divmod(row // EXTRA_ROWS, n_hi * n_lo)
        hi, lo = divmod(g, n_lo)
        count = min(EXTRA_ROWS, v - row)
        total = 0.0
        for part in range(2):
            for x in range(2):
                piece = jnp.where(core == c, e_ref[lo, x, part, hi], f_ref[lo, x, part, hi])
                columns = pl.ds((2 * part + x) * cx, cx)
                out_ref[pl.ds(row, count), columns] = piece[:count] * (0.5 * scale)
                if row + EXTRA_ROWS > v:
                    total = total + jnp.sum(piece[count : count + 1], axis=1, keepdims=True)
        if row + EXTRA_ROWS > v:
            loss_ref[...] = total * (1.0 / npoints)


def finished(dims, scale, npoints, v, own, other, e_own, e_other):
    r, h = own.shape
    shapes = [(2 * r, h), (v, h), (1, 1)]
    return pl.pallas_call(
        functools.partial(last_kernel, *dims, scale, npoints),
        out_shape=[jax.ShapeDtypeStruct(shape, jnp.float32) for shape in shapes],
        compiler_params=pltpu.CompilerParams(vmem_limit_bytes=VMEM),
        name="last",
    )(own, other, e_own, e_other)


def input_gradient(start, p, n, wt, gp, gh):
    steps, h, width = gp.shape
    t = TILE
    mloc = width // t
    off = start // t
    in_specs = [
        pl.BlockSpec((h, h), lambda s: (0, 0), pipeline_mode=pl.Buffered(1)),
        pl.BlockSpec(gp.shape, lambda s: (0, 0, 0)),
    ]
    args = [wt, gp]
    if gh is not None:
        in_specs.append(pl.BlockSpec(memory_space=pl.ANY))
        args.append(gh)
    return pl.pallas_call(
        input_kernel,
        grid=(steps,),
        in_specs=in_specs,
        out_specs=pl.BlockSpec((mloc, h, t), lambda s: (0, 0, off + s)),
        out_shape=jax.ShapeDtypeStruct((mloc, h, n), jnp.bfloat16),
        input_output_aliases={} if gh is None else {2: 0},
        compiler_params=pltpu.CompilerParams(vmem_limit_bytes=VMEM),
        cost_estimate=pl.CostEstimate(
            flops=2 * h * h, bytes_accessed=2 * h * h, transcendentals=0
        ),
        name="grad_hidden_part",
    )(*args)


def after(value, *others):
    return lax.optimization_barrier((value,) + others)[0]


def shards(hidden, target, area, var_weight, w_inner, b_inner, w_out, b_out):
    mloc, h, n = hidden.shape
    n_mem = lax.axis_size("mem")
    n_grid = lax.axis_size("grid")
    members = mloc * n_mem
    npoints = n * n_grid
    v = w_out.shape[0]
    vp = 128
    n_lo = 2
    while n_lo * n_lo * 4 <= n_grid:
        n_lo *= 2
    n_hi = n_grid // n_lo

    swap_x = [(i, (i + n_mem // 2) % n_mem) for i in range(n_mem)]
    swap_core = [(i, i ^ 1) for i in range(n_mem)]

    def shift_lo(k):
        return [(a * n_lo + b, a * n_lo + (b + k) % n_lo) for a in range(n_hi) for b in range(n_lo)]

    def shift_hi(k):
        return [(a * n_lo + b, (a + k) % n_hi * n_lo + b) for a in range(n_hi) for b in range(n_lo)]

    to_x = lambda a: lax.ppermute(a, "mem", swap_x)
    to_core = lambda a: lax.ppermute(a, "mem", swap_core)
    to_lo = lambda a, k: lax.ppermute(a, "grid", shift_lo(k))
    to_hi = lambda a, k: lax.ppermute(a, "grid", shift_hi(k))

    mem, grid = lax.axis_index("mem"), lax.axis_index("grid")
    at_zero = {("mem", bit): mem & bit == 0 for bit in (1, n_mem // 2)}
    bit = 1
    while bit < n_lo:
        at_zero["grid", bit] = grid & bit == 0
        bit *= 2
    hidden, at_zero = lax.optimization_barrier((hidden, at_zero))
    hidden, w_out, b_inner, b_out = (
        pltpu.with_memory_space_constraint(a, pltpu.HBM)
        for a in (hidden, w_out, b_inner.reshape(1, h), b_out.reshape(1, v))
    )
    unit = n // sum(EIGHTHS)
    starts = [unit * sum(EIGHTHS[:k]) for k in range(len(EIGHTHS))]
    spans = [(start, unit * size) for start, size in zip(starts, EIGHTHS)]
    parts, far = [], []
    for start, p in spans:
        w, vmem = w_inner, VMEM
        if len(parts) == 2:
            wt, wot = transposes(after(w_inner, parts[1][2]), w_out, vp)
            b_out = after(b_out, wt)
        if parts:
            b_out = after(b_out, parts[-1][2])
        else:
            w = pltpu.with_memory_space_constraint(w_inner, pltpu.HBM)
            vmem += 4 * h * h
        parts.append(forward(start, p, hidden, w, b_inner, w_out, b_out, vmem))
        far.append(to_x(parts[-1][2]))
    near = [to_core(fields) for _, _, fields in parts]
    vw, area = var_weight.reshape(1, v), area.reshape(1, n)
    acc = extra = gh = None
    grad_pre = []
    for k, (start, p) in enumerate(spans):
        act, slope, fields = parts[k]
        first, last = k == 0, k == len(spans) - 1
        if k:
            far[k] = after(far[k], parts[-1][2] if k == 1 else grad_pre[k - 2])
        gp, extra, acc, *accs = backward(
            start, p, first, last, (n_hi, n_lo), members,
            (fields, near[k], far[k], to_core(far[k])),
            (target, area, vw, act, slope, hidden, wot), acc, extra,
        )
        grad_pre.append(gp)
    keep_x, send_x, keep_y, send_y = accs

    def gathered(block, axis, name, bit):
        n = lax.axis_size(name)
        other = lax.ppermute(block, name, [(i, i ^ bit) for i in range(n)])
        return ordered(block, other, axis, name, bit)

    def ordered(block, other, axis, name, bit):
        return jnp.where(
            at_zero[name, bit],
            jnp.concatenate([block, other], axis),
            jnp.concatenate([other, block], axis),
        )

    def beside(k, gh, start_after, wait_for):
        gh = input_gradient(*spans[k], n, wt, after(grad_pre[k], start_after), gh)
        return lax.optimization_barrier((gh, wait_for))

    r, cx = h // (2 * n_grid), keep_x.shape[-1]
    others = range(1, n_lo)
    got_x = to_core(send_x)
    got_y = to_core(send_y)
    out_x = keep_x[1] + got_x[1]
    out_y = [keep_y[k] + got_y[k] for k in others]
    from_x = to_x(out_x)
    from_y = [to_lo(out_y[k - 1], k) for k in others]
    for k in (0, 1):
        gh, (keep_x, keep_y) = beside(k, gh, (out_x, out_y), (keep_x, keep_y))
    own_x = keep_x[0] + got_x[0] + from_x
    own_y = sum(from_y, keep_y[0] + got_y[0])
    own_x, own_y = [own_x[k] for k in range(n_lo)], [own_y[k] for k in range(2)]
    from_y = [to_lo(own_x[k], k) for k in others]
    from_x = to_x(own_y[1])
    gh, (own_x, own_y) = beside(2, gh, (own_x[1:], own_y[1]), (own_x[0], own_y[0]))
    sums = [sum(from_y, own_x), own_y + from_x]

    extra = [part[:, r:].reshape(-1, cx) for part in sums]
    pieces = [jnp.concatenate([part[k, :r] for part in sums] + extra, 0) for k in range(n_hi)]
    from_hi = [to_hi(pieces[k], k) for k in range(1, n_hi)]
    gh, own = beside(3, gh, pieces[1:], pieces[0])
    total = sum(from_hi, own)
    far = to_x(total)
    mine = total[2 * r :][None]
    beyond = lax.ppermute(mine, "grid", [(g, g ^ 1) for g in range(n_grid)])
    pairs = [(m * n_grid + g, (m + n_mem // 2) % n_mem * n_grid + (g ^ 1)) for m in range(n_mem) for g in range(n_grid)]
    across = lax.ppermute(mine, ("mem", "grid"), pairs)

    scale = 1.0 / math.sqrt(members * npoints)
    halves = [ordered(total[k : k + r], far[k : k + r], 1, "mem", n_mem // 2) for k in (0, r)]
    own = jnp.concatenate(halves, 1)
    other = to_core(own)

    sides = [ordered(mine, far[2 * r :][None], 0, "mem", n_mem // 2)]
    sides.append(ordered(beyond, across, 0, "mem", n_mem // 2))
    extra = ordered(*(side[None] for side in sides), 0, "grid", 1)
    bit = 2
    while bit < n_lo:
        extra = gathered(extra, 0, "grid", bit)
        bit *= 2
    extra = extra.reshape(n_lo, 2, 2, n_hi, EXTRA_ROWS, cx)
    grad_inner, grad_out, loss = finished(
        (n_hi, n_lo), scale, npoints, v, own, other, extra, to_core(extra)
    )
    return (loss.reshape(()), gh, grad_inner, grad_out)


def solution(mesh):
    in_specs = (P("mem", None, "grid"), P(None, "grid"), P("grid"), P(), P(), P(), P(), P())
    out_specs = (P(), P("mem", None, "grid"), P("grid", None), P())
    return jax.shard_map(shards, mesh=mesh, in_specs=in_specs, out_specs=out_specs, check_vma=False)
```

```python
import functools
import math

import jax
import jax.numpy as jnp
from jax import lax
from jax.experimental import pallas as pl
from jax.experimental.pallas import tpu as pltpu
from jax.sharding import PartitionSpec as P

EIGHTHS = (2, 2, 2, 2)
TILE = 256
EPS = 0.0004
K0 = math.sqrt(2.0 / math.pi)
K1 = K0 * 0.044715
SLAB = 256
EXTRA_ROWS = 8
VMEM = 8 * 1024 * 1024
NT = (((1,), (1,)), ((), ()))


def column(row, size):
    r = lax.broadcasted_iota(jnp.int32, (size, size), 0)
    c = lax.broadcasted_iota(jnp.int32, (size, size), 1)
    return jnp.sum(jnp.where(r == c, row, 0.0), axis=1, keepdims=True)


def field_rows(v, mloc, m, r0):
    full = v // 8 * 8
    if r0 < full:
        return pl.ds(m * full + r0, 8)
    return pl.ds(mloc * full + m * (v - full), v - full)


def forward_kernel(hid_ref, w_ref, b_ref, wo_ref, bo_ref, act_ref, slope_ref, f_ref, bias, half, *slabs):
    step = pl.program_id(0)
    mloc, h, t = hid_ref.shape
    v = half.shape[0]
    size = h // len(slabs)

    @pl.when(step == 0)
    def _():
        for k in range(h // 128):
            bias[pl.ds(k * 128, 128), :] = jnp.broadcast_to(
                column(b_ref[:, pl.ds(k * 128, 128)], 128), (128, 128)
            )
        half[...] = wo_ref[...] * jnp.bfloat16(0.5)

    hid = jnp.concatenate([hid_ref[m] for m in range(mloc)], axis=1)
    out = jnp.broadcast_to(column(bo_ref[...], v), (v, mloc * t))
    for k in range(len(slabs) + 1):
        if k < len(slabs):
            rows = pl.ds(k * size, size)
            slabs[k][...] = jnp.dot(w_ref[rows, :], hid, preferred_element_type=jnp.float32)
        if k == 0:
            continue
        slab, start = slabs[k - 1], (k - 1) * size
        for r in range(0, size, 16):
            rows = pl.ds(start + r, 16)
            b = jnp.concatenate([bias[rows, :]] * (t // 128), axis=1)
            for m in range(mloc):
                x = slab[pl.ds(r, 16), pl.ds(m * t, t)] + b
                q = x * x * K1
                th = jnp.tanh(x * (K0 + q))
                up = 1.0 + th
                act = x * up
                act_ref[step, m, rows, :] = act.astype(jnp.bfloat16)
                slope_ref[step, m, rows, :] = up + act * ((1.0 - th) * (K0 + 3.0 * q))
        rows = pl.ds(start, size)
        act = jnp.concatenate([act_ref[step, m, rows, :] for m in range(mloc)], axis=1)
        out = out + jnp.dot(half[:, rows], act, preferred_element_type=jnp.float32)
    for m in range(mloc):
        for r0 in range(0, v, 8):
            f_ref[field_rows(v, mloc, m, r0), :] = out[r0 : r0 + 8, m * t : (m + 1) * t]


def forward(start, p, hidden, w_inner, b_inner, w_out, b_out, vmem):
    mloc, h, n = hidden.shape
    v = w_out.shape[0]
    t = TILE
    tiles = p // t
    whole = lambda s: (0, 0)
    once = pl.Buffered(1)
    shape = (p // t, mloc, h, t)
    held = pl.BlockSpec(shape, lambda s: (0, 0, 0, 0))
    return pl.pallas_call(
        forward_kernel,
        grid=(tiles,),
        in_specs=[
            pl.BlockSpec((mloc, h, t), lambda s: (0, 0, start // t + s)),
            pl.BlockSpec((h, h), whole, pipeline_mode=once),
            pl.BlockSpec((1, h), whole, pipeline_mode=once),
            pl.BlockSpec((v, h), whole, pipeline_mode=once),
            pl.BlockSpec((1, v), whole, pipeline_mode=once),
        ],
        out_specs=[
            held,
            held,
            pl.BlockSpec((mloc * v, t), lambda s: (0, s)),
        ],
        out_shape=[
            pltpu.VMEM(shape, jnp.bfloat16),
            pltpu.VMEM(shape, jnp.float32),
            jax.ShapeDtypeStruct((mloc * v, p), jnp.float32),
        ],
        scratch_shapes=[
            pltpu.VMEM((h, 128), jnp.float32),
            pltpu.VMEM((v, h), jnp.bfloat16),
        ]
        + [pltpu.VMEM((SLAB, mloc * t), jnp.float32)] * (h // SLAB),
        compiler_params=pltpu.CompilerParams(vmem_limit_bytes=vmem),
        cost_estimate=pl.CostEstimate(
            flops=2 * h * h, bytes_accessed=2 * h * h, transcendentals=0
        ),
        name="forward_part",
    )(hidden, w_inner, b_inner, w_out, b_out)


def backward_kernel(
    first, last, dims, members,
    f_ref, fc_ref, fx_ref, fxc_ref, target_ref, area_ref, vw_ref, act_ref, slope_ref, hid_ref,
    wot_ref, acc_in, extra_in, gp_ref, extra_ref, *refs,
):
    acc, *refs = refs
    if last:
        keep_x, send_x, keep_y, send_y, *refs = refs
    (gf,) = refs
    step = pl.program_id(0)
    end = pl.num_programs(0) - 1
    mloc, _, t = hid_ref.shape
    v = target_ref.shape[0]
    h = wot_ref.shape[0]
    denom = members * (members - 1)

    def pair(a, b):
        d = a - b
        s = d * d + EPS
        r = lax.rsqrt(s)
        return d * r, s * r

    def scores(r0, vw, area):
        rows = pl.ds(r0, min(8, v - r0))
        places = [field_rows(v, mloc, m, r0) for m in range(mloc)]
        own = [f_ref[place, :] for place in places]
        others = [ref[place, :] for ref in (fc_ref, fx_ref, fxc_ref) for place in places]
        target = target_ref[rows, :]
        dsum = [jnp.zeros_like(target) for _ in range(mloc)]
        obs = []
        cross = inner = near = jnp.zeros_like(target)
        n_cross = n_inner = 0
        for i in range(mloc):
            sl, ph = pair(own[i], target)
            obs.append(sl)
            near = near + ph
            for k, b in enumerate(others):
                sl, ph = pair(own[i], b)
                dsum[i] = dsum[i] + sl
                if k % mloc == i:
                    cross = cross + ph
                    n_cross += 1
                elif k % mloc > i:
                    inner = inner + ph
                    n_inner += 1
            for j in range(i + 1, mloc):
                sl, ph = pair(own[i], own[j])
                dsum[i] = dsum[i] + sl
                dsum[j] = dsum[j] - sl
                inner = inner + ph
                n_inner += 1
        weight = vw[r0 : r0 + 8] * area
        for m in range(mloc):
            gf[m, rows, :] = weight * (obs[m] * (1.0 / members) - dsum[m] * (1.0 / denom))
        near = (near - 0.02 * mloc) * (1.0 / members)
        pairs = (inner - 0.02 * n_inner) + 0.5 * (cross - 0.02 * n_cross)
        return jnp.sum(weight * (near - pairs * (1.0 / denom)), axis=0, keepdims=True)

    def weights(k):
        rows = pl.ds(k, SLAB)
        hid = jnp.concatenate([hid_ref[m] for m in range(mloc)], axis=1)
        acc[rows, :] += lax.dot_general(
            gp_ref[step - 1, rows, :], hid, NT, preferred_element_type=jnp.float32
        )

    def work(with_weights):
        vw, area = column(vw_ref[...], v), area_ref[...]
        starts = list(range(0, v, 8))
        slabs = list(range(0, h, SLAB)) if with_weights else [None]
        loss = jnp.zeros((1, t), jnp.float32)
        for k, slab in enumerate(slabs):
            if with_weights:
                weights(slab)
            for r0 in starts[k :: len(slabs)]:
                loss = loss + scores(r0, vw, area)
        for m in range(mloc):
            gf[m, pl.ds(v, gf.shape[1] - v), :] = jnp.zeros((gf.shape[1] - v, t), jnp.float32)
        g = jnp.concatenate([gf[m] for m in range(mloc)], axis=1).astype(jnp.bfloat16)
        for k in range(0, h, 256):
            rows = pl.ds(k, 256)
            ga = jnp.dot(wot_ref[rows, :], g, preferred_element_type=jnp.float32)
            for m in range(mloc):
                piece = ga[:, m * t : (m + 1) * t] * slope_ref[step, m, rows, :]
                gp_ref[step, rows, pl.ds(m * t, t)] = piece.astype(jnp.bfloat16)
        act = jnp.concatenate([act_ref[step, m] for m in range(mloc)], axis=1)
        extra_ref[...] += lax.dot_general(g, act, NT, preferred_element_type=jnp.float32)
        extra_ref[pl.ds(v, 1), pl.ds(0, t)] += loss

    @pl.when(step == 0)
    def _():
        if first:
            acc[...] = jnp.zeros_like(acc)
            extra_ref[...] = jnp.zeros_like(extra_ref)
        work(False)

    @pl.when((step > 0) & (step < end))
    def _():
        work(True)

    @pl.when(step == end)
    def _():
        for k in range(0, h, SLAB):
            weights(k)

    if last:
        n_hi, n_lo = dims

        @pl.when(step == end)
        def _():
            mem = lax.axis_index("mem")
            grid = lax.axis_index("grid")
            x, core = mem // 2, mem % 2
            hi, lo = grid // n_lo, grid % n_lo
            r = h // (2 * n_hi * n_lo)
            cx = keep_x.shape[4]
            for dlo in range(n_lo):
                for dhi in range(n_hi):
                    g = lax.rem(hi + dhi, n_hi) * n_lo + lax.rem(lo + dlo, n_lo)
                    block = dhi * n_lo + lax.rem(lo + dlo, n_lo)
                    for c, to_x, to_y in ((core, keep_x, keep_y), (1 - core, send_x, send_y)):
                        r0 = pl.multiple_of((g * 2 + c) * r, r)
                        total = acc[pl.ds(r0, r), :]
                        e0 = (c * (n_hi * n_lo) + block) * EXTRA_ROWS
                        at = pl.multiple_of(
                            jnp.minimum(e0, extra_ref.shape[0] - EXTRA_ROWS), EXTRA_ROWS
                        )
                        e = jnp.where(
                            e0 < extra_ref.shape[0], extra_ref[pl.ds(at, EXTRA_ROWS), :], 0.0
                        )
                        for values, rows in ((total, pl.ds(0, r)), (e, pl.ds(r, EXTRA_ROWS))):
                            q = [values[:, k * cx : (k + 1) * cx] for k in range(4)]
                            for d in range(2):
                                own = x == d
                                to_x[d, dlo, dhi, rows, :] = jnp.where(own, q[0], q[1])
                                to_y[dlo, d, dhi, rows, :] = jnp.where(own, q[2], q[3])


def backward(start, p, first, last, dims, members, fields, rest, acc, extra):
    target, area, vw, act, slope, hidden, wot = rest
    mloc, h, n = hidden.shape
    v = target.shape[0]
    vp = wot.shape[1]
    t = TILE
    off = start // t
    once = pl.Buffered(1)
    steps = p // t
    ahead = lambda s: jnp.minimum(s, steps - 1)
    f_spec = pl.BlockSpec((mloc * v, t), lambda s: (0, ahead(s)))
    whole = lambda s: (0, 0)
    const = lambda a: pl.BlockSpec(a.shape, whole, pipeline_mode=once)
    held = lambda a: pl.BlockSpec(a.shape, lambda s: (0,) * len(a.shape))
    in_specs = [f_spec] * 4 + [
        pl.BlockSpec((v, t), lambda s: (0, off + ahead(s))),
        pl.BlockSpec((1, t), lambda s: (0, off + ahead(s))),
        const(vw), held(act), held(slope),
        pl.BlockSpec((mloc, h, t), lambda s: (0, 0, off + jnp.maximum(s - 1, 0))),
        const(wot),
    ]
    act, slope = (pltpu.with_memory_space_constraint(a, pltpu.VMEM) for a in (act, slope))
    args = [*fields, target, area, vw, act, slope, hidden, wot]
    kernel = functools.partial(backward_kernel, first, last, dims, members)
    if first:
        kernel_fn = lambda *refs: kernel(*refs[:11], None, None, *refs[11:])
        aliases = {}
    else:
        kernel_fn = kernel
        in_specs += [held(acc), held(extra)]
        args += [acc, extra]
        aliases = {11: 2, 12: 1}
    out_shape = [
        pltpu.VMEM((p // t, h, mloc * t), jnp.bfloat16),
        pltpu.VMEM((vp, h), jnp.float32),
        pltpu.VMEM((h, h), jnp.float32),
    ]
    if last:
        n_hi, n_lo = dims
        r = h // (2 * n_hi * n_lo)
        cx = h // 4
        out_shape += [pltpu.VMEM((2, n_lo, n_hi, r + EXTRA_ROWS, cx), jnp.float32)] * 2
        out_shape += [pltpu.VMEM((n_lo, 2, n_hi, r + EXTRA_ROWS, cx), jnp.float32)] * 2
    out_specs = [held(a) for a in out_shape]
    return pl.pallas_call(
        kernel_fn,
        grid=(steps + 1,),
        in_specs=in_specs,
        out_specs=out_specs,
        out_shape=out_shape,
        scratch_shapes=[pltpu.VMEM((mloc, vp, t), jnp.float32)],
        input_output_aliases=aliases,
        compiler_params=pltpu.CompilerParams(vmem_limit_bytes=VMEM),
        cost_estimate=pl.CostEstimate(
            flops=2 * h * h, bytes_accessed=2 * h * h, transcendentals=0
        ),
        name="backward_part",
    )(*args)


def transposes_kernel(w_ref, wo_ref, wt_ref, wot_ref):
    wt_ref[...] = w_ref[...].astype(jnp.float32).T.astype(jnp.bfloat16)

    @pl.when(pl.program_id(0) == 0)
    def _():
        v, h = wo_ref.shape
        rows = jnp.concatenate(
            [wo_ref[...].astype(jnp.float32) * 0.5, jnp.zeros((wot_ref.shape[1] - v, h), jnp.float32)], 0
        )
        wot_ref[...] = rows.T.astype(jnp.bfloat16)


def transposes(w_inner, w_out, vp):
    v, h = w_out.shape
    t = TILE
    return pl.pallas_call(
        transposes_kernel,
        grid=(h // t,),
        in_specs=[
            pl.BlockSpec((t, h), lambda s: (s, 0)),
            pl.BlockSpec((v, h), lambda s: (0, 0)),
        ],
        out_specs=[
            pl.BlockSpec((h, t), lambda s: (0, s)),
            pl.BlockSpec((h, vp), lambda s: (0, 0)),
        ],
        out_shape=[pltpu.VMEM((h, h), jnp.bfloat16), pltpu.VMEM((h, vp), jnp.bfloat16)],
        compiler_params=pltpu.CompilerParams(vmem_limit_bytes=VMEM),
        cost_estimate=pl.CostEstimate(flops=2 * h, bytes_accessed=2 * h, transcendentals=0),
        name="transposes",
    )(w_inner, w_out)


def input_kernel(wt_ref, gp_ref, *refs):
    mloc, h, t = refs[-1].shape
    for k in range(0, h, SLAB):
        rows = pl.ds(k, SLAB)
        out = jnp.dot(wt_ref[rows, :], gp_ref[pl.program_id(0)], preferred_element_type=jnp.float32)
        for m in range(mloc):
            refs[-1][m, rows, :] = out[:, m * t : (m + 1) * t].astype(jnp.bfloat16)


def last_kernel(n_hi, n_lo, scale, npoints, own_ref, other_ref, e_ref, f_ref, inner_ref, out_ref, loss_ref):
    core = lax.axis_index("mem") % 2
    r = own_ref.shape[0]
    inner_ref[pl.ds(pl.multiple_of(core * r, r), r), :] = own_ref[...] * scale
    inner_ref[pl.ds(pl.multiple_of((1 - core) * r, r), r), :] = other_ref[...] * scale
    v = out_ref.shape[0]
    cx = e_ref.shape[-1]
    for row in range(0, v + 1, EXTRA_ROWS):
        c, g = divmod(row // EXTRA_ROWS, n_hi * n_lo)
        hi, lo = divmod(g, n_lo)
        count = min(EXTRA_ROWS, v - row)
        total = 0.0
        for part in range(2):
            for x in range(2):
                piece = jnp.where(core == c, e_ref[lo, x, part, hi], f_ref[lo, x, part, hi])
                columns = pl.ds((2 * part + x) * cx, cx)
                out_ref[pl.ds(row, count), columns] = piece[:count] * (0.5 * scale)
                if row + EXTRA_ROWS > v:
                    total = total + jnp.sum(piece[count : count + 1], axis=1, keepdims=True)
        if row + EXTRA_ROWS > v:
            loss_ref[...] = total * (1.0 / npoints)


def finished(dims, scale, npoints, v, own, other, e_own, e_other):
    r, h = own.shape
    shapes = [(2 * r, h), (v, h), (1, 1)]
    return pl.pallas_call(
        functools.partial(last_kernel, *dims, scale, npoints),
        out_shape=[jax.ShapeDtypeStruct(shape, jnp.float32) for shape in shapes],
        compiler_params=pltpu.CompilerParams(vmem_limit_bytes=VMEM),
        name="last",
    )(own, other, e_own, e_other)


def input_gradient(start, p, n, wt, gp, gh):
    steps, h, width = gp.shape
    t = TILE
    mloc = width // t
    off = start // t
    in_specs = [
        pl.BlockSpec((h, h), lambda s: (0, 0), pipeline_mode=pl.Buffered(1)),
        pl.BlockSpec(gp.shape, lambda s: (0, 0, 0)),
    ]
    args = [wt, gp]
    if gh is not None:
        in_specs.append(pl.BlockSpec(memory_space=pl.ANY))
        args.append(gh)
    return pl.pallas_call(
        input_kernel,
        grid=(steps,),
        in_specs=in_specs,
        out_specs=pl.BlockSpec((mloc, h, t), lambda s: (0, 0, off + s)),
        out_shape=jax.ShapeDtypeStruct((mloc, h, n), jnp.bfloat16),
        input_output_aliases={} if gh is None else {2: 0},
        compiler_params=pltpu.CompilerParams(vmem_limit_bytes=VMEM),
        cost_estimate=pl.CostEstimate(
            flops=2 * h * h, bytes_accessed=2 * h * h, transcendentals=0
        ),
        name="grad_hidden_part",
    )(*args)


def after(value, *others):
    return lax.optimization_barrier((value,) + others)[0]


def shards(hidden, target, area, var_weight, w_inner, b_inner, w_out, b_out):
    mloc, h, n = hidden.shape
    n_mem = lax.axis_size("mem")
    n_grid = lax.axis_size("grid")
    members = mloc * n_mem
    npoints = n * n_grid
    v = w_out.shape[0]
    vp = 128
    n_lo = 2
    while n_lo * n_lo * 4 <= n_grid:
        n_lo *= 2
    n_hi = n_grid // n_lo

    swap_x = [(i, (i + n_mem // 2) % n_mem) for i in range(n_mem)]
    swap_core = [(i, i ^ 1) for i in range(n_mem)]

    def shift_lo(k):
        return [(a * n_lo + b, a * n_lo + (b + k) % n_lo) for a in range(n_hi) for b in range(n_lo)]

    def shift_hi(k):
        return [(a * n_lo + b, (a + k) % n_hi * n_lo + b) for a in range(n_hi) for b in range(n_lo)]

    to_x = lambda a: lax.ppermute(a, "mem", swap_x)
    to_core = lambda a: lax.ppermute(a, "mem", swap_core)
    to_lo = lambda a, k: lax.ppermute(a, "grid", shift_lo(k))
    to_hi = lambda a, k: lax.ppermute(a, "grid", shift_hi(k))

    mem, grid = lax.axis_index("mem"), lax.axis_index("grid")
    at_zero = {("mem", bit): mem & bit == 0 for bit in (1, n_mem // 2)}
    bit = 1
    while bit < n_lo:
        at_zero["grid", bit] = grid & bit == 0
        bit *= 2
    hidden, at_zero = lax.optimization_barrier((hidden, at_zero))
    hidden, w_out, b_inner, b_out = (
        pltpu.with_memory_space_constraint(a, pltpu.HBM)
        for a in (hidden, w_out, b_inner.reshape(1, h), b_out.reshape(1, v))
    )
    unit = n // sum(EIGHTHS)
    starts = [unit * sum(EIGHTHS[:k]) for k in range(len(EIGHTHS))]
    spans = [(start, unit * size) for start, size in zip(starts, EIGHTHS)]
    parts, far = [], []
    for start, p in spans:
        w, vmem = w_inner, VMEM
        if len(parts) == 2:
            wt, wot = transposes(after(w_inner, parts[1][2]), w_out, vp)
            b_out = after(b_out, wt)
        if parts:
            b_out = after(b_out, parts[-1][2])
        else:
            w = pltpu.with_memory_space_constraint(w_inner, pltpu.HBM)
            vmem += 4 * h * h
        parts.append(forward(start, p, hidden, w, b_inner, w_out, b_out, vmem))
        far.append(to_x(parts[-1][2]))
    near = [to_core(fields) for _, _, fields in parts]
    vw, area = var_weight.reshape(1, v), area.reshape(1, n)
    acc = extra = gh = None
    grad_pre = []
    for k, (start, p) in enumerate(spans):
        act, slope, fields = parts[k]
        first, last = k == 0, k == len(spans) - 1
        if k:
            far[k] = after(far[k], parts[-1][2] if k == 1 else grad_pre[k - 2])
        gp, extra, acc, *accs = backward(
            start, p, first, last, (n_hi, n_lo), members,
            (fields, near[k], far[k], to_core(far[k])),
            (target, area, vw, act, slope, hidden, wot), acc, extra,
        )
        grad_pre.append(gp)
    keep_x, send_x, keep_y, send_y = accs

    def gathered(block, axis, name, bit):
        n = lax.axis_size(name)
        other = lax.ppermute(block, name, [(i, i ^ bit) for i in range(n)])
        return ordered(block, other, axis, name, bit)

    def ordered(block, other, axis, name, bit):
        return jnp.where(
            at_zero[name, bit],
            jnp.concatenate([block, other], axis),
            jnp.concatenate([other, block], axis),
        )

    def beside(k, gh, start_after, wait_for):
        gh = input_gradient(*spans[k], n, wt, after(grad_pre[k], start_after), gh)
        return lax.optimization_barrier((gh, wait_for))

    r, cx = h // (2 * n_grid), keep_x.shape[-1]
    others = range(1, n_lo)
    got_x = to_core(send_x)
    got_y = to_core(send_y)
    out_x = keep_x[1] + got_x[1]
    out_y = [keep_y[k] + got_y[k] for k in others]
    from_x = to_x(out_x)
    from_y = [to_lo(out_y[k - 1], k) for k in others]
    for k in (0, 1):
        gh, (keep_x, keep_y) = beside(k, gh, (out_x, out_y), (keep_x, keep_y))
    own_x = keep_x[0] + got_x[0] + from_x
    own_y = sum(from_y, keep_y[0] + got_y[0])
    own_x, own_y = [own_x[k] for k in range(n_lo)], [own_y[k] for k in range(2)]
    from_y = [to_lo(own_x[k], k) for k in others]
    from_x = to_x(own_y[1])
    gh, (own_x, own_y) = beside(2, gh, (own_x[1:], own_y[1]), (own_x[0], own_y[0]))
    sums = [sum(from_y, own_x), own_y + from_x]

    extra = [part[:, r:].reshape(-1, cx) for part in sums]
    pieces = [jnp.concatenate([part[k, :r] for part in sums] + extra, 0) for k in range(n_hi)]
    from_hi = [to_hi(pieces[k], k) for k in range(1, n_hi)]
    gh, own = beside(3, gh, pieces[1:], pieces[0])
    total = sum(from_hi, own)
    far = to_x(total)
    mine = total[2 * r :][None]
    beyond = lax.ppermute(mine, "grid", [(g, g ^ 1) for g in range(n_grid)])
    pairs = [(m * n_grid + g, (m + n_mem // 2) % n_mem * n_grid + (g ^ 1)) for m in range(n_mem) for g in range(n_grid)]
    across = lax.ppermute(mine, ("mem", "grid"), pairs)

    scale = 1.0 / math.sqrt(members * npoints)
    halves = [ordered(total[k : k + r], far[k : k + r], 1, "mem", n_mem // 2) for k in (0, r)]
    own = jnp.concatenate(halves, 1)
    other = to_core(own)

    sides = [ordered(mine, far[2 * r :][None], 0, "mem", n_mem // 2)]
    sides.append(ordered(beyond, across, 0, "mem", n_mem // 2))
    extra = ordered(*(side[None] for side in sides), 0, "grid", 1)
    bit = 2
    while bit < n_lo:
        extra = gathered(extra, 0, "grid", bit)
        bit *= 2
    extra = extra.reshape(n_lo, 2, 2, n_hi, EXTRA_ROWS, cx)
    grad_inner, grad_out, loss = finished(
        (n_hi, n_lo), scale, npoints, v, own, other, extra, to_core(extra)
    )
    return (loss.reshape(()), gh, grad_inner, grad_out)


def solution(mesh):
    in_specs = (P("mem", None, "grid"), P(None, "grid"), P("grid"), P(), P(), P(), P(), P())
    out_specs = (P(), P("mem", None, "grid"), P("grid", None), P())
    return jax.shard_map(shards, mesh=mesh, in_specs=in_specs, out_specs=out_specs, check_vma=False)
```

```python
import functools
import math

import jax
import jax.numpy as jnp
from jax import lax
from jax.experimental import pallas as pl
from jax.experimental.pallas import tpu as pltpu
from jax.sharding import PartitionSpec as P

EIGHTHS = (2, 2, 2, 2)
TILE = 256
EPS = 0.0004
K0 = math.sqrt(2.0 / math.pi)
K1 = K0 * 0.044715
SLAB = 256
EXTRA_ROWS = 8
VMEM = 8 * 1024 * 1024
NT = (((1,), (1,)), ((), ()))


def column(row, size):
    r = lax.broadcasted_iota(jnp.int32, (size, size), 0)
    c = lax.broadcasted_iota(jnp.int32, (size, size), 1)
    return jnp.sum(jnp.where(r == c, row, 0.0), axis=1, keepdims=True)


def field_rows(v, mloc, m, r0):
    full = v // 8 * 8
    if r0 < full:
        return pl.ds(m * full + r0, 8)
    return pl.ds(mloc * full + m * (v - full), v - full)


def forward_kernel(hid_ref, w_ref, b_ref, wo_ref, bo_ref, act_ref, slope_ref, f_ref, bias, half, *slabs):
    step = pl.program_id(0)
    mloc, h, t = hid_ref.shape
    v = half.shape[0]
    size = h // len(slabs)

    @pl.when(step == 0)
    def _():
        for k in range(h // 128):
            bias[pl.ds(k * 128, 128), :] = jnp.broadcast_to(
                column(b_ref[:, pl.ds(k * 128, 128)], 128), (128, 128)
            )
        half[...] = wo_ref[...] * jnp.bfloat16(0.5)

    cols = pl.ds(pl.multiple_of(step * t, t), t)
    hid = jnp.concatenate([hid_ref[m] for m in range(mloc)], axis=1)
    out = jnp.broadcast_to(column(bo_ref[...], v), (v, mloc * t))
    for k in range(len(slabs) + 1):
        if k < len(slabs):
            rows = pl.ds(k * size, size)
            slabs[k][...] = jnp.dot(w_ref[rows, :], hid, preferred_element_type=jnp.float32)
        if k == 0:
            continue
        slab, start = slabs[k - 1], (k - 1) * size
        for r in range(0, size, 16):
            rows = pl.ds(start + r, 16)
            b = jnp.concatenate([bias[rows, :]] * (t // 128), axis=1)
            for m in range(mloc):
                x = slab[pl.ds(r, 16), pl.ds(m * t, t)] + b
                q = x * x * K1
                th = jnp.tanh(x * (K0 + q))
                up = 1.0 + th
                act = x * up
                act_ref[step, m, rows, :] = act.astype(jnp.bfloat16)
                slope_ref[step, m, rows, :] = up + act * ((1.0 - th) * (K0 + 3.0 * q))
        rows = pl.ds(start, size)
        act = jnp.concatenate([act_ref[step, m, rows, :] for m in range(mloc)], axis=1)
        out = out + jnp.dot(half[:, rows], act, preferred_element_type=jnp.float32)
    for m in range(mloc):
        for r0 in range(0, v, 8):
            f_ref[field_rows(v, mloc, m, r0), cols] = out[r0 : r0 + 8, m * t : (m + 1) * t]


def forward(start, p, hidden, w_inner, b_inner, w_out, b_out, vmem):
    mloc, h, n = hidden.shape
    v = w_out.shape[0]
    t = TILE
    tiles = p // t
    whole = lambda s: (0, 0)
    once = pl.Buffered(1)
    shape = (p // t, mloc, h, t)
    held = pl.BlockSpec(shape, lambda s: (0, 0, 0, 0))
    return pl.pallas_call(
        forward_kernel,
        grid=(tiles,),
        in_specs=[
            pl.BlockSpec((mloc, h, t), lambda s: (0, 0, start // t + s)),
            pl.BlockSpec((h, h), whole, pipeline_mode=once),
            pl.BlockSpec((1, h), whole, pipeline_mode=once),
            pl.BlockSpec((v, h), whole, pipeline_mode=once),
            pl.BlockSpec((1, v), whole, pipeline_mode=once),
        ],
        out_specs=[
            held,
            held,
            pl.BlockSpec((mloc * v, p), whole),
        ],
        out_shape=[
            pltpu.VMEM(shape, jnp.bfloat16),
            pltpu.VMEM(shape, jnp.float32),
            pltpu.VMEM((mloc * v, p), jnp.float32),
        ],
        scratch_shapes=[
            pltpu.VMEM((h, 128), jnp.float32),
            pltpu.VMEM((v, h), jnp.bfloat16),
        ]
        + [pltpu.VMEM((SLAB, mloc * t), jnp.float32)] * (h // SLAB),
        compiler_params=pltpu.CompilerParams(vmem_limit_bytes=vmem),
        cost_estimate=pl.CostEstimate(
            flops=2 * h * h, bytes_accessed=2 * h * h, transcendentals=0
        ),
        name="forward_part",
    )(hidden, w_inner, b_inner, w_out, b_out)


def backward_kernel(
    first, last, dims, members,
    f_ref, fc_ref, fx_ref, fxc_ref, target_ref, area_ref, vw_ref, act_ref, slope_ref, hid_ref,
    wot_ref, acc_in, extra_in, gp_ref, extra_ref, *refs,
):
    acc, *refs = refs
    if last:
        keep_x, send_x, keep_y, send_y, *refs = refs
    (gf,) = refs
    step = pl.program_id(0)
    end = pl.num_programs(0) - 1
    mloc, _, t = hid_ref.shape
    v = target_ref.shape[0]
    h = wot_ref.shape[0]
    denom = members * (members - 1)

    def pair(a, b):
        d = a - b
        s = d * d + EPS
        r = lax.rsqrt(s)
        return d * r, s * r

    def scores(r0, vw, area):
        rows = pl.ds(r0, min(8, v - r0))
        places = [field_rows(v, mloc, m, r0) for m in range(mloc)]
        cols = pl.ds(pl.multiple_of(step * t, t), t)
        own = [f_ref[place, cols] for place in places]
        others = [ref[place, cols] for ref in (fc_ref, fx_ref, fxc_ref) for place in places]
        target = target_ref[rows, :]
        dsum = [jnp.zeros_like(target) for _ in range(mloc)]
        obs = []
        cross = inner = near = jnp.zeros_like(target)
        n_cross = n_inner = 0
        for i in range(mloc):
            sl, ph = pair(own[i], target)
            obs.append(sl)
            near = near + ph
            for k, b in enumerate(others):
                sl, ph = pair(own[i], b)
                dsum[i] = dsum[i] + sl
                if k % mloc == i:
                    cross = cross + ph
                    n_cross += 1
                elif k % mloc > i:
                    inner = inner + ph
                    n_inner += 1
            for j in range(i + 1, mloc):
                sl, ph = pair(own[i], own[j])
                dsum[i] = dsum[i] + sl
                dsum[j] = dsum[j] - sl
                inner = inner + ph
                n_inner += 1
        weight = vw[r0 : r0 + 8] * area
        for m in range(mloc):
            gf[m, rows, :] = weight * (obs[m] * (1.0 / members) - dsum[m] * (1.0 / denom))
        near = (near - 0.02 * mloc) * (1.0 / members)
        pairs = (inner - 0.02 * n_inner) + 0.5 * (cross - 0.02 * n_cross)
        return jnp.sum(weight * (near - pairs * (1.0 / denom)), axis=0, keepdims=True)

    def weights(k):
        rows = pl.ds(k, SLAB)
        hid = jnp.concatenate([hid_ref[m] for m in range(mloc)], axis=1)
        acc[rows, :] += lax.dot_general(
            gp_ref[step - 1, rows, :], hid, NT, preferred_element_type=jnp.float32
        )

    def work(with_weights):
        vw, area = column(vw_ref[...], v), area_ref[...]
        starts = list(range(0, v, 8))
        slabs = list(range(0, h, SLAB)) if with_weights else [None]
        loss = jnp.zeros((1, t), jnp.float32)
        for k, slab in enumerate(slabs):
            if with_weights:
                weights(slab)
            for r0 in starts[k :: len(slabs)]:
                loss = loss + scores(r0, vw, area)
        for m in range(mloc):
            gf[m, pl.ds(v, gf.shape[1] - v), :] = jnp.zeros((gf.shape[1] - v, t), jnp.float32)
        g = jnp.concatenate([gf[m] for m in range(mloc)], axis=1).astype(jnp.bfloat16)
        for k in range(0, h, 256):
            rows = pl.ds(k, 256)
            ga = jnp.dot(wot_ref[rows, :], g, preferred_element_type=jnp.float32)
            for m in range(mloc):
                piece = ga[:, m * t : (m + 1) * t] * slope_ref[step, m, rows, :]
                gp_ref[step, rows, pl.ds(m * t, t)] = piece.astype(jnp.bfloat16)
        act = jnp.concatenate([act_ref[step, m] for m in range(mloc)], axis=1)
        extra_ref[...] += lax.dot_general(g, act, NT, preferred_element_type=jnp.float32)
        extra_ref[pl.ds(v, 1), pl.ds(0, t)] += loss

    @pl.when(step == 0)
    def _():
        if first:
            acc[...] = jnp.zeros_like(acc)
            extra_ref[...] = jnp.zeros_like(extra_ref)
        work(False)

    @pl.when((step > 0) & (step < end))
    def _():
        work(True)

    @pl.when(step == end)
    def _():
        for k in range(0, h, SLAB):
            weights(k)

    if last:
        n_hi, n_lo = dims

        @pl.when(step == end)
        def _():
            mem = lax.axis_index("mem")
            grid = lax.axis_index("grid")
            x, core = mem // 2, mem % 2
            hi, lo = grid // n_lo, grid % n_lo
            r = h // (2 * n_hi * n_lo)
            cx = keep_x.shape[4]
            for dlo in range(n_lo):
                for dhi in range(n_hi):
                    g = lax.rem(hi + dhi, n_hi) * n_lo + lax.rem(lo + dlo, n_lo)
                    block = dhi * n_lo + lax.rem(lo + dlo, n_lo)
                    for c, to_x, to_y in ((core, keep_x, keep_y), (1 - core, send_x, send_y)):
                        r0 = pl.multiple_of((g * 2 + c) * r, r)
                        total = acc[pl.ds(r0, r), :]
                        e0 = (c * (n_hi * n_lo) + block) * EXTRA_ROWS
                        at = pl.multiple_of(
                            jnp.minimum(e0, extra_ref.shape[0] - EXTRA_ROWS), EXTRA_ROWS
                        )
                        e = jnp.where(
                            e0 < extra_ref.shape[0], extra_ref[pl.ds(at, EXTRA_ROWS), :], 0.0
                        )
                        for values, rows in ((total, pl.ds(0, r)), (e, pl.ds(r, EXTRA_ROWS))):
                            q = [values[:, k * cx : (k + 1) * cx] for k in range(4)]
                            for d in range(2):
                                own = x == d
                                to_x[d, dlo, dhi, rows, :] = jnp.where(own, q[0], q[1])
                                to_y[dlo, d, dhi, rows, :] = jnp.where(own, q[2], q[3])


def backward(start, p, first, last, dims, members, fields, rest, acc, extra):
    target, area, vw, act, slope, hidden, wot = rest
    mloc, h, n = hidden.shape
    v = target.shape[0]
    vp = wot.shape[1]
    t = TILE
    off = start // t
    once = pl.Buffered(1)
    steps = p // t
    ahead = lambda s: jnp.minimum(s, steps - 1)
    whole = lambda s: (0, 0)
    f_spec = pl.BlockSpec((mloc * v, p), whole)
    const = lambda a: pl.BlockSpec(a.shape, whole, pipeline_mode=once)
    held = lambda a: pl.BlockSpec(a.shape, lambda s: (0,) * len(a.shape))
    in_specs = [f_spec] * 4 + [
        pl.BlockSpec((v, t), lambda s: (0, off + ahead(s))),
        pl.BlockSpec((1, t), lambda s: (0, off + ahead(s))),
        const(vw), held(act), held(slope),
        pl.BlockSpec((mloc, h, t), lambda s: (0, 0, off + jnp.maximum(s - 1, 0))),
        const(wot),
    ]
    act, slope = (pltpu.with_memory_space_constraint(a, pltpu.VMEM) for a in (act, slope))
    args = [*fields, target, area, vw, act, slope, hidden, wot]
    kernel = functools.partial(backward_kernel, first, last, dims, members)
    if first:
        kernel_fn = lambda *refs: kernel(*refs[:11], None, None, *refs[11:])
        aliases = {}
    else:
        kernel_fn = kernel
        in_specs += [held(acc), held(extra)]
        args += [acc, extra]
        aliases = {11: 2, 12: 1}
    out_shape = [
        pltpu.VMEM((p // t, h, mloc * t), jnp.bfloat16),
        pltpu.VMEM((vp, h), jnp.float32),
        pltpu.VMEM((h, h), jnp.float32),
    ]
    if last:
        n_hi, n_lo = dims
        r = h // (2 * n_hi * n_lo)
        cx = h // 4
        out_shape += [pltpu.VMEM((2, n_lo, n_hi, r + EXTRA_ROWS, cx), jnp.float32)] * 2
        out_shape += [pltpu.VMEM((n_lo, 2, n_hi, r + EXTRA_ROWS, cx), jnp.float32)] * 2
    out_specs = [held(a) for a in out_shape]
    return pl.pallas_call(
        kernel_fn,
        grid=(steps + 1,),
        in_specs=in_specs,
        out_specs=out_specs,
        out_shape=out_shape,
        scratch_shapes=[pltpu.VMEM((mloc, vp, t), jnp.float32)],
        input_output_aliases=aliases,
        compiler_params=pltpu.CompilerParams(vmem_limit_bytes=VMEM),
        cost_estimate=pl.CostEstimate(
            flops=2 * h * h, bytes_accessed=2 * h * h, transcendentals=0
        ),
        name="backward_part",
    )(*args)


def transposes_kernel(w_ref, wo_ref, wt_ref, wot_ref):
    wt_ref[...] = w_ref[...].astype(jnp.float32).T.astype(jnp.bfloat16)

    @pl.when(pl.program_id(0) == 0)
    def _():
        v, h = wo_ref.shape
        rows = jnp.concatenate(
            [wo_ref[...].astype(jnp.float32) * 0.5, jnp.zeros((wot_ref.shape[1] - v, h), jnp.float32)], 0
        )
        wot_ref[...] = rows.T.astype(jnp.bfloat16)


def transposes(w_inner, w_out, vp):
    v, h = w_out.shape
    t = TILE
    return pl.pallas_call(
        transposes_kernel,
        grid=(h // t,),
        in_specs=[
            pl.BlockSpec((t, h), lambda s: (s, 0)),
            pl.BlockSpec((v, h), lambda s: (0, 0)),
        ],
        out_specs=[
            pl.BlockSpec((h, t), lambda s: (0, s)),
            pl.BlockSpec((h, vp), lambda s: (0, 0)),
        ],
        out_shape=[pltpu.VMEM((h, h), jnp.bfloat16), pltpu.VMEM((h, vp), jnp.bfloat16)],
        compiler_params=pltpu.CompilerParams(vmem_limit_bytes=VMEM),
        cost_estimate=pl.CostEstimate(flops=2 * h, bytes_accessed=2 * h, transcendentals=0),
        name="transposes",
    )(w_inner, w_out)


def input_kernel(wt_ref, gp_ref, *refs):
    mloc, h, t = refs[-1].shape
    for k in range(0, h, SLAB):
        rows = pl.ds(k, SLAB)
        out = jnp.dot(wt_ref[rows, :], gp_ref[pl.program_id(0)], preferred_element_type=jnp.float32)
        for m in range(mloc):
            refs[-1][m, rows, :] = out[:, m * t : (m + 1) * t].astype(jnp.bfloat16)


def last_kernel(n_hi, n_lo, scale, npoints, own_ref, other_ref, e_ref, f_ref, inner_ref, out_ref, loss_ref):
    core = lax.axis_index("mem") % 2
    r = own_ref.shape[0]
    inner_ref[pl.ds(pl.multiple_of(core * r, r), r), :] = own_ref[...] * scale
    inner_ref[pl.ds(pl.multiple_of((1 - core) * r, r), r), :] = other_ref[...] * scale
    v = out_ref.shape[0]
    cx = e_ref.shape[-1]
    for row in range(0, v + 1, EXTRA_ROWS):
        c, g = divmod(row // EXTRA_ROWS, n_hi * n_lo)
        hi, lo = divmod(g, n_lo)
        count = min(EXTRA_ROWS, v - row)
        total = 0.0
        for part in range(2):
            for x in range(2):
                piece = jnp.where(core == c, e_ref[lo, x, part, hi], f_ref[lo, x, part, hi])
                columns = pl.ds((2 * part + x) * cx, cx)
                out_ref[pl.ds(row, count), columns] = piece[:count] * (0.5 * scale)
                if row + EXTRA_ROWS > v:
                    total = total + jnp.sum(piece[count : count + 1], axis=1, keepdims=True)
        if row + EXTRA_ROWS > v:
            loss_ref[...] = total * (1.0 / npoints)


def finished(dims, scale, npoints, v, own, other, e_own, e_other):
    r, h = own.shape
    shapes = [(2 * r, h), (v, h), (1, 1)]
    return pl.pallas_call(
        functools.partial(last_kernel, *dims, scale, npoints),
        out_shape=[jax.ShapeDtypeStruct(shape, jnp.float32) for shape in shapes],
        compiler_params=pltpu.CompilerParams(vmem_limit_bytes=VMEM),
        name="last",
    )(own, other, e_own, e_other)


def input_gradient(start, p, n, wt, gp, gh):
    steps, h, width = gp.shape
    t = TILE
    mloc = width // t
    off = start // t
    in_specs = [
        pl.BlockSpec((h, h), lambda s: (0, 0), pipeline_mode=pl.Buffered(1)),
        pl.BlockSpec(gp.shape, lambda s: (0, 0, 0)),
    ]
    args = [wt, gp]
    if gh is not None:
        in_specs.append(pl.BlockSpec(memory_space=pl.ANY))
        args.append(gh)
    return pl.pallas_call(
        input_kernel,
        grid=(steps,),
        in_specs=in_specs,
        out_specs=pl.BlockSpec((mloc, h, t), lambda s: (0, 0, off + s)),
        out_shape=jax.ShapeDtypeStruct((mloc, h, n), jnp.bfloat16),
        input_output_aliases={} if gh is None else {2: 0},
        compiler_params=pltpu.CompilerParams(vmem_limit_bytes=VMEM),
        cost_estimate=pl.CostEstimate(
            flops=2 * h * h, bytes_accessed=2 * h * h, transcendentals=0
        ),
        name="grad_hidden_part",
    )(*args)


def after(value, *others):
    return lax.optimization_barrier((value,) + others)[0]


def shards(hidden, target, area, var_weight, w_inner, b_inner, w_out, b_out):
    mloc, h, n = hidden.shape
    n_mem = lax.axis_size("mem")
    n_grid = lax.axis_size("grid")
    members = mloc * n_mem
    npoints = n * n_grid
    v = w_out.shape[0]
    vp = 128
    n_lo = 2
    while n_lo * n_lo * 4 <= n_grid:
        n_lo *= 2
    n_hi = n_grid // n_lo

    swap_x = [(i, (i + n_mem // 2) % n_mem) for i in range(n_mem)]
    swap_core = [(i, i ^ 1) for i in range(n_mem)]

    def shift_lo(k):
        return [(a * n_lo + b, a * n_lo + (b + k) % n_lo) for a in range(n_hi) for b in range(n_lo)]

    def shift_hi(k):
        return [(a * n_lo + b, (a + k) % n_hi * n_lo + b) for a in range(n_hi) for b in range(n_lo)]

    to_x = lambda a: lax.ppermute(a, "mem", swap_x)
    to_core = lambda a: lax.ppermute(a, "mem", swap_core)
    to_lo = lambda a, k: lax.ppermute(a, "grid", shift_lo(k))
    to_hi = lambda a, k: lax.ppermute(a, "grid", shift_hi(k))

    mem, grid = lax.axis_index("mem"), lax.axis_index("grid")
    at_zero = {("mem", bit): mem & bit == 0 for bit in (1, n_mem // 2)}
    bit = 1
    while bit < n_lo:
        at_zero["grid", bit] = grid & bit == 0
        bit *= 2
    hidden, at_zero = lax.optimization_barrier((hidden, at_zero))
    hidden, w_out, b_inner, b_out = (
        pltpu.with_memory_space_constraint(a, pltpu.HBM)
        for a in (hidden, w_out, b_inner.reshape(1, h), b_out.reshape(1, v))
    )
    unit = n // sum(EIGHTHS)
    starts = [unit * sum(EIGHTHS[:k]) for k in range(len(EIGHTHS))]
    spans = [(start, unit * size) for start, size in zip(starts, EIGHTHS)]
    parts, far = [], []
    for start, p in spans:
        w, vmem = w_inner, VMEM
        if len(parts) == 2:
            wt, wot = transposes(after(w_inner, parts[1][2]), w_out, vp)
            b_out = after(b_out, wt)
        if parts:
            b_out = after(b_out, parts[-1][2])
        else:
            w = pltpu.with_memory_space_constraint(w_inner, pltpu.HBM)
            vmem += 4 * h * h
        parts.append(forward(start, p, hidden, w, b_inner, w_out, b_out, vmem))
        far.append(to_x(parts[-1][2]))
    near = [to_core(fields) for _, _, fields in parts]
    vw, area = var_weight.reshape(1, v), area.reshape(1, n)
    acc = extra = gh = None
    grad_pre = []
    for k, (start, p) in enumerate(spans):
        act, slope, fields = parts[k]
        first, last = k == 0, k == len(spans) - 1
        if k:
            far[k] = after(far[k], parts[-1][2] if k == 1 else grad_pre[k - 2])
        gp, extra, acc, *accs = backward(
            start, p, first, last, (n_hi, n_lo), members,
            (fields, near[k], far[k], to_core(far[k])),
            (target, area, vw, act, slope, hidden, wot), acc, extra,
        )
        grad_pre.append(gp)
    keep_x, send_x, keep_y, send_y = accs

    def gathered(block, axis, name, bit):
        n = lax.axis_size(name)
        other = lax.ppermute(block, name, [(i, i ^ bit) for i in range(n)])
        return ordered(block, other, axis, name, bit)

    def ordered(block, other, axis, name, bit):
        return jnp.where(
            at_zero[name, bit],
            jnp.concatenate([block, other], axis),
            jnp.concatenate([other, block], axis),
        )

    def beside(k, gh, start_after, wait_for):
        gh = input_gradient(*spans[k], n, wt, after(grad_pre[k], start_after), gh)
        return lax.optimization_barrier((gh, wait_for))

    r, cx = h // (2 * n_grid), keep_x.shape[-1]
    others = range(1, n_lo)
    got_x = to_core(send_x)
    got_y = to_core(send_y)
    out_x = keep_x[1] + got_x[1]
    out_y = [keep_y[k] + got_y[k] for k in others]
    from_x = to_x(out_x)
    from_y = [to_lo(out_y[k - 1], k) for k in others]
    for k in (0, 1):
        gh, (keep_x, keep_y) = beside(k, gh, (out_x, out_y), (keep_x, keep_y))
    own_x = keep_x[0] + got_x[0] + from_x
    own_y = sum(from_y, keep_y[0] + got_y[0])
    own_x, own_y = [own_x[k] for k in range(n_lo)], [own_y[k] for k in range(2)]
    from_y = [to_lo(own_x[k], k) for k in others]
    from_x = to_x(own_y[1])
    gh, (own_x, own_y) = beside(2, gh, (own_x[1:], own_y[1]), (own_x[0], own_y[0]))
    sums = [sum(from_y, own_x), own_y + from_x]

    extra = [part[:, r:].reshape(-1, cx) for part in sums]
    pieces = [jnp.concatenate([part[k, :r] for part in sums] + extra, 0) for k in range(n_hi)]
    from_hi = [to_hi(pieces[k], k) for k in range(1, n_hi)]
    gh, own = beside(3, gh, pieces[1:], pieces[0])
    total = sum(from_hi, own)
    far = to_x(total)
    mine = total[2 * r :][None]
    beyond = lax.ppermute(mine, "grid", [(g, g ^ 1) for g in range(n_grid)])
    pairs = [(m * n_grid + g, (m + n_mem // 2) % n_mem * n_grid + (g ^ 1)) for m in range(n_mem) for g in range(n_grid)]
    across = lax.ppermute(mine, ("mem", "grid"), pairs)

    scale = 1.0 / math.sqrt(members * npoints)
    halves = [ordered(total[k : k + r], far[k : k + r], 1, "mem", n_mem // 2) for k in (0, r)]
    own = jnp.concatenate(halves, 1)
    other = to_core(own)

    sides = [ordered(mine, far[2 * r :][None], 0, "mem", n_mem // 2)]
    sides.append(ordered(beyond, across, 0, "mem", n_mem // 2))
    extra = ordered(*(side[None] for side in sides), 0, "grid", 1)
    bit = 2
    while bit < n_lo:
        extra = gathered(extra, 0, "grid", bit)
        bit *= 2
    extra = extra.reshape(n_lo, 2, 2, n_hi, EXTRA_ROWS, cx)
    grad_inner, grad_out, loss = finished(
        (n_hi, n_lo), scale, npoints, v, own, other, extra, to_core(extra)
    )
    return (loss.reshape(()), gh, grad_inner, grad_out)


def solution(mesh):
    in_specs = (P("mem", None, "grid"), P(None, "grid"), P("grid"), P(), P(), P(), P(), P())
    out_specs = (P(), P("mem", None, "grid"), P("grid", None), P())
    return jax.shard_map(shards, mesh=mesh, in_specs=in_specs, out_specs=out_specs, check_vma=False)
```

```python
import functools
import math

import jax
import jax.numpy as jnp
from jax import lax
from jax.experimental import pallas as pl
from jax.experimental.pallas import tpu as pltpu
from jax.sharding import PartitionSpec as P

EIGHTHS = (2, 2, 2, 2)
TILE = 256
EPS = 0.0004
K0 = math.sqrt(2.0 / math.pi)
K1 = K0 * 0.044715
SLAB = 256
EXTRA_ROWS = 8
VMEM = 8 * 1024 * 1024
NT = (((1,), (1,)), ((), ()))


def column(row, size):
    r = lax.broadcasted_iota(jnp.int32, (size, size), 0)
    c = lax.broadcasted_iota(jnp.int32, (size, size), 1)
    return jnp.sum(jnp.where(r == c, row, 0.0), axis=1, keepdims=True)


def field_rows(v, mloc, m, r0):
    full = v // 8 * 8
    if r0 < full:
        return pl.ds(m * full + r0, 8)
    return pl.ds(mloc * full + m * (v - full), v - full)


def forward_kernel(first, hid_ref, w_ref, b_ref, wo_ref, bo_ref, act_ref, slope_ref, f_ref, bias, half, *slabs):
    step = pl.program_id(0)
    mloc, h, t = hid_ref.shape
    v = half.shape[0]
    size = h // len(slabs)

    if first:

        @pl.when(step == 0)
        def _():
            for k in range(h // 128):
                bias[pl.ds(k * 128, 128), :] = jnp.broadcast_to(
                    column(b_ref[:, pl.ds(k * 128, 128)], 128), (128, 128)
                )
            half[...] = wo_ref[...] * jnp.bfloat16(0.5)

    cols = pl.ds(pl.multiple_of(step * t, t), t)
    hid = jnp.concatenate([hid_ref[m] for m in range(mloc)], axis=1)
    out = jnp.broadcast_to(column(bo_ref[...], v), (v, mloc * t))
    for k in range(len(slabs) + 1):
        if k < len(slabs):
            rows = pl.ds(k * size, size)
            slabs[k][...] = jnp.dot(w_ref[rows, :], hid, preferred_element_type=jnp.float32)
        if k == 0:
            continue
        slab, start = slabs[k - 1], (k - 1) * size
        for r in range(0, size, 16):
            rows = pl.ds(start + r, 16)
            b = jnp.concatenate([bias[rows, :]] * (t // 128), axis=1)
            for m in range(mloc):
                x = slab[pl.ds(r, 16), pl.ds(m * t, t)] + b
                q = x * x * K1
                th = jnp.tanh(x * (K0 + q))
                up = 1.0 + th
                act = x * up
                act_ref[step, m, rows, :] = act.astype(jnp.bfloat16)
                slope_ref[step, m, rows, :] = up + act * ((1.0 - th) * (K0 + 3.0 * q))
        rows = pl.ds(start, size)
        act = jnp.concatenate([act_ref[step, m, rows, :] for m in range(mloc)], axis=1)
        out = out + jnp.dot(half[:, rows], act, preferred_element_type=jnp.float32)
    for m in range(mloc):
        for r0 in range(0, v, 8):
            f_ref[field_rows(v, mloc, m, r0), cols] = out[r0 : r0 + 8, m * t : (m + 1) * t]


def forward(start, p, hidden, w_inner, b_inner, w_out, b_out, vmem, first):
    mloc, h, n = hidden.shape
    v = w_out.shape[0]
    t = TILE
    tiles = p // t
    whole = lambda s: (0, 0)
    once = pl.Buffered(1)
    shape = (p // t, mloc, h, t)
    held = pl.BlockSpec(shape, lambda s: (0, 0, 0, 0))
    made = []
    if first:
        made = [pltpu.VMEM((h, 128), jnp.float32), pltpu.VMEM((v, h), jnp.bfloat16)]
        kernel = functools.partial(forward_kernel, True)
    else:

        def kernel(hid, w, bias, half, bo, act, slope, fields, *slabs):
            forward_kernel(False, hid, w, None, None, bo, act, slope, fields, bias, half, *slabs)

    return pl.pallas_call(
        kernel,
        grid=(tiles,),
        in_specs=[
            pl.BlockSpec((mloc, h, t), lambda s: (0, 0, start // t + s)),
            pl.BlockSpec((h, h), whole, pipeline_mode=once),
            pl.BlockSpec(b_inner.shape, whole, pipeline_mode=once),
            pl.BlockSpec((v, h), whole, pipeline_mode=once),
            pl.BlockSpec((1, v), whole, pipeline_mode=once),
        ],
        out_specs=[
            held,
            held,
            pl.BlockSpec((mloc * v, p), whole),
        ]
        + [pl.BlockSpec(a.shape, whole) for a in made],
        out_shape=[
            pltpu.VMEM(shape, jnp.bfloat16),
            pltpu.VMEM(shape, jnp.float32),
            pltpu.VMEM((mloc * v, p), jnp.float32),
        ]
        + made,
        scratch_shapes=[pltpu.VMEM((SLAB, mloc * t), jnp.float32)] * (h // SLAB),
        compiler_params=pltpu.CompilerParams(vmem_limit_bytes=vmem),
        cost_estimate=pl.CostEstimate(
            flops=2 * h * h, bytes_accessed=2 * h * h, transcendentals=0
        ),
        name="forward_part",
    )(hidden, w_inner, b_inner, w_out, b_out)


def backward_kernel(
    first, last, dims, members,
    f_ref, fc_ref, fx_ref, fxc_ref, target_ref, area_ref, vw_ref, act_ref, slope_ref, hid_ref,
    wot_ref, acc_in, extra_in, gp_ref, extra_ref, *refs,
):
    acc, *refs = refs
    if last:
        keep_x, send_x, keep_y, send_y, *refs = refs
    (gf,) = refs
    step = pl.program_id(0)
    end = pl.num_programs(0) - 1
    mloc, _, t = hid_ref.shape
    v = target_ref.shape[0]
    h = wot_ref.shape[0]
    denom = members * (members - 1)

    def pair(a, b):
        d = a - b
        s = d * d + EPS
        r = lax.rsqrt(s)
        return d * r, s * r

    def scores(r0, vw, area):
        rows = pl.ds(r0, min(8, v - r0))
        places = [field_rows(v, mloc, m, r0) for m in range(mloc)]
        cols = pl.ds(pl.multiple_of(step * t, t), t)
        own = [f_ref[place, cols] for place in places]
        others = [ref[place, cols] for ref in (fc_ref, fx_ref, fxc_ref) for place in places]
        target = target_ref[rows, :]
        dsum = [jnp.zeros_like(target) for _ in range(mloc)]
        obs = []
        cross = inner = near = jnp.zeros_like(target)
        n_cross = n_inner = 0
        for i in range(mloc):
            sl, ph = pair(own[i], target)
            obs.append(sl)
            near = near + ph
            for k, b in enumerate(others):
                sl, ph = pair(own[i], b)
                dsum[i] = dsum[i] + sl
                if k % mloc == i:
                    cross = cross + ph
                    n_cross += 1
                elif k % mloc > i:
                    inner = inner + ph
                    n_inner += 1
            for j in range(i + 1, mloc):
                sl, ph = pair(own[i], own[j])
                dsum[i] = dsum[i] + sl
                dsum[j] = dsum[j] - sl
                inner = inner + ph
                n_inner += 1
        weight = vw[r0 : r0 + 8] * area
        for m in range(mloc):
            gf[m, rows, :] = weight * (obs[m] * (1.0 / members) - dsum[m] * (1.0 / denom))
        near = (near - 0.02 * mloc) * (1.0 / members)
        pairs = (inner - 0.02 * n_inner) + 0.5 * (cross - 0.02 * n_cross)
        return jnp.sum(weight * (near - pairs * (1.0 / denom)), axis=0, keepdims=True)

    def weights(k):
        rows = pl.ds(k, SLAB)
        hid = jnp.concatenate([hid_ref[m] for m in range(mloc)], axis=1)
        acc[rows, :] += lax.dot_general(
            gp_ref[step - 1, rows, :], hid, NT, preferred_element_type=jnp.float32
        )

    def work(with_weights):
        vw, area = column(vw_ref[...], v), area_ref[...]
        starts = list(range(0, v, 8))
        slabs = list(range(0, h, SLAB)) if with_weights else [None]
        loss = jnp.zeros((1, t), jnp.float32)
        for k, slab in enumerate(slabs):
            if with_weights:
                weights(slab)
            for r0 in starts[k :: len(slabs)]:
                loss = loss + scores(r0, vw, area)
        for m in range(mloc):
            gf[m, pl.ds(v, gf.shape[1] - v), :] = jnp.zeros((gf.shape[1] - v, t), jnp.float32)
        g = jnp.concatenate([gf[m] for m in range(mloc)], axis=1).astype(jnp.bfloat16)
        for k in range(0, h, 256):
            rows = pl.ds(k, 256)
            ga = jnp.dot(wot_ref[rows, :], g, preferred_element_type=jnp.float32)
            for m in range(mloc):
                piece = ga[:, m * t : (m + 1) * t] * slope_ref[step, m, rows, :]
                gp_ref[step, rows, pl.ds(m * t, t)] = piece.astype(jnp.bfloat16)
        act = jnp.concatenate([act_ref[step, m] for m in range(mloc)], axis=1)
        extra_ref[...] += lax.dot_general(g, act, NT, preferred_element_type=jnp.float32)
        extra_ref[pl.ds(v, 1), pl.ds(0, t)] += loss

    @pl.when(step == 0)
    def _():
        if first:
            acc[...] = jnp.zeros_like(acc)
            extra_ref[...] = jnp.zeros_like(extra_ref)
        work(False)

    @pl.when((step > 0) & (step < end))
    def _():
        work(True)

    @pl.when(step == end)
    def _():
        for k in range(0, h, SLAB):
            weights(k)

    if last:
        n_hi, n_lo = dims

        @pl.when(step == end)
        def _():
            mem = lax.axis_index("mem")
            grid = lax.axis_index("grid")
            x, core = mem // 2, mem % 2
            hi, lo = grid // n_lo, grid % n_lo
            r = h // (2 * n_hi * n_lo)
            cx = keep_x.shape[4]
            for dlo in range(n_lo):
                for dhi in range(n_hi):
                    g = lax.rem(hi + dhi, n_hi) * n_lo + lax.rem(lo + dlo, n_lo)
                    block = dhi * n_lo + lax.rem(lo + dlo, n_lo)
                    for c, to_x, to_y in ((core, keep_x, keep_y), (1 - core, send_x, send_y)):
                        r0 = pl.multiple_of((g * 2 + c) * r, r)
                        total = acc[pl.ds(r0, r), :]
                        e0 = (c * (n_hi * n_lo) + block) * EXTRA_ROWS
                        at = pl.multiple_of(
                            jnp.minimum(e0, extra_ref.shape[0] - EXTRA_ROWS), EXTRA_ROWS
                        )
                        e = jnp.where(
                            e0 < extra_ref.shape[0], extra_ref[pl.ds(at, EXTRA_ROWS), :], 0.0
                        )
                        for values, rows in ((total, pl.ds(0, r)), (e, pl.ds(r, EXTRA_ROWS))):
                            q = [values[:, k * cx : (k + 1) * cx] for k in range(4)]
                            for d in range(2):
                                own = x == d
                                to_x[d, dlo, dhi, rows, :] = jnp.where(own, q[0], q[1])
                                to_y[dlo, d, dhi, rows, :] = jnp.where(own, q[2], q[3])


def backward(start, p, first, last, dims, members, fields, rest, acc, extra):
    target, area, vw, act, slope, hidden, wot = rest
    mloc, h, n = hidden.shape
    v = target.shape[0]
    vp = wot.shape[1]
    t = TILE
    off = start // t
    once = pl.Buffered(1)
    steps = p // t
    ahead = lambda s: jnp.minimum(s, steps - 1)
    whole = lambda s: (0, 0)
    f_spec = pl.BlockSpec((mloc * v, p), whole)
    const = lambda a: pl.BlockSpec(a.shape, whole, pipeline_mode=once)
    held = lambda a: pl.BlockSpec(a.shape, lambda s: (0,) * len(a.shape))
    in_specs = [f_spec] * 4 + [
        pl.BlockSpec((v, t), lambda s: (0, off + ahead(s))),
        pl.BlockSpec((1, t), lambda s: (0, off + ahead(s))),
        const(vw), held(act), held(slope),
        pl.BlockSpec((mloc, h, t), lambda s: (0, 0, off + jnp.maximum(s - 1, 0))),
        const(wot),
    ]
    act, slope = (pltpu.with_memory_space_constraint(a, pltpu.VMEM) for a in (act, slope))
    args = [*fields, target, area, vw, act, slope, hidden, wot]
    kernel = functools.partial(backward_kernel, first, last, dims, members)
    if first:
        kernel_fn = lambda *refs: kernel(*refs[:11], None, None, *refs[11:])
        aliases = {}
    else:
        kernel_fn = kernel
        in_specs += [held(acc), held(extra)]
        args += [acc, extra]
        aliases = {11: 2, 12: 1}
    out_shape = [
        pltpu.VMEM((p // t, h, mloc * t), jnp.bfloat16),
        pltpu.VMEM((vp, h), jnp.float32),
        pltpu.VMEM((h, h), jnp.float32),
    ]
    if last:
        n_hi, n_lo = dims
        r = h // (2 * n_hi * n_lo)
        cx = h // 4
        out_shape += [pltpu.VMEM((2, n_lo, n_hi, r + EXTRA_ROWS, cx), jnp.float32)] * 2
        out_shape += [pltpu.VMEM((n_lo, 2, n_hi, r + EXTRA_ROWS, cx), jnp.float32)] * 2
    out_specs = [held(a) for a in out_shape]
    return pl.pallas_call(
        kernel_fn,
        grid=(steps + 1,),
        in_specs=in_specs,
        out_specs=out_specs,
        out_shape=out_shape,
        scratch_shapes=[pltpu.VMEM((mloc, vp, t), jnp.float32)],
        input_output_aliases=aliases,
        compiler_params=pltpu.CompilerParams(vmem_limit_bytes=VMEM),
        cost_estimate=pl.CostEstimate(
            flops=2 * h * h, bytes_accessed=2 * h * h, transcendentals=0
        ),
        name="backward_part",
    )(*args)


def transposes_kernel(w_ref, wo_ref, wt_ref, wot_ref):
    wt_ref[...] = w_ref[...].astype(jnp.float32).T.astype(jnp.bfloat16)

    @pl.when(pl.program_id(0) == 0)
    def _():
        v, h = wo_ref.shape
        rows = jnp.concatenate(
            [wo_ref[...].astype(jnp.float32) * 0.5, jnp.zeros((wot_ref.shape[1] - v, h), jnp.float32)], 0
        )
        wot_ref[...] = rows.T.astype(jnp.bfloat16)


def transposes(w_inner, w_out, vp):
    v, h = w_out.shape
    t = TILE
    return pl.pallas_call(
        transposes_kernel,
        grid=(h // t,),
        in_specs=[
            pl.BlockSpec((t, h), lambda s: (s, 0)),
            pl.BlockSpec((v, h), lambda s: (0, 0)),
        ],
        out_specs=[
            pl.BlockSpec((h, t), lambda s: (0, s)),
            pl.BlockSpec((h, vp), lambda s: (0, 0)),
        ],
        out_shape=[pltpu.VMEM((h, h), jnp.bfloat16), pltpu.VMEM((h, vp), jnp.bfloat16)],
        compiler_params=pltpu.CompilerParams(vmem_limit_bytes=VMEM),
        cost_estimate=pl.CostEstimate(flops=2 * h, bytes_accessed=2 * h, transcendentals=0),
        name="transposes",
    )(w_inner, w_out)


def input_kernel(wt_ref, gp_ref, *refs):
    mloc, h, t = refs[-1].shape
    for k in range(0, h, SLAB):
        rows = pl.ds(k, SLAB)
        out = jnp.dot(wt_ref[rows, :], gp_ref[pl.program_id(0)], preferred_element_type=jnp.float32)
        for m in range(mloc):
            refs[-1][m, rows, :] = out[:, m * t : (m + 1) * t].astype(jnp.bfloat16)


def last_kernel(n_hi, n_lo, scale, npoints, own_ref, other_ref, e_ref, f_ref, inner_ref, out_ref, loss_ref):
    core = lax.axis_index("mem") % 2
    r = own_ref.shape[0]
    inner_ref[pl.ds(pl.multiple_of(core * r, r), r), :] = own_ref[...] * scale
    inner_ref[pl.ds(pl.multiple_of((1 - core) * r, r), r), :] = other_ref[...] * scale
    v = out_ref.shape[0]
    cx = e_ref.shape[-1]
    for row in range(0, v + 1, EXTRA_ROWS):
        c, g = divmod(row // EXTRA_ROWS, n_hi * n_lo)
        hi, lo = divmod(g, n_lo)
        count = min(EXTRA_ROWS, v - row)
        total = 0.0
        for part in range(2):
            for x in range(2):
                piece = jnp.where(core == c, e_ref[lo, x, part, hi], f_ref[lo, x, part, hi])
                columns = pl.ds((2 * part + x) * cx, cx)
                out_ref[pl.ds(row, count), columns] = piece[:count] * (0.5 * scale)
                if row + EXTRA_ROWS > v:
                    total = total + jnp.sum(piece[count : count + 1], axis=1, keepdims=True)
        if row + EXTRA_ROWS > v:
            loss_ref[...] = total * (1.0 / npoints)


def finished(dims, scale, npoints, v, own, other, e_own, e_other):
    r, h = own.shape
    shapes = [(2 * r, h), (v, h), (1, 1)]
    return pl.pallas_call(
        functools.partial(last_kernel, *dims, scale, npoints),
        out_shape=[jax.ShapeDtypeStruct(shape, jnp.float32) for shape in shapes],
        compiler_params=pltpu.CompilerParams(vmem_limit_bytes=VMEM),
        name="last",
    )(own, other, e_own, e_other)


def input_gradient(start, p, n, wt, gp, gh):
    steps, h, width = gp.shape
    t = TILE
    mloc = width // t
    off = start // t
    in_specs = [
        pl.BlockSpec((h, h), lambda s: (0, 0), pipeline_mode=pl.Buffered(1)),
        pl.BlockSpec(gp.shape, lambda s: (0, 0, 0)),
    ]
    args = [wt, gp]
    if gh is not None:
        in_specs.append(pl.BlockSpec(memory_space=pl.ANY))
        args.append(gh)
    return pl.pallas_call(
        input_kernel,
        grid=(steps,),
        in_specs=in_specs,
        out_specs=pl.BlockSpec((mloc, h, t), lambda s: (0, 0, off + s)),
        out_shape=jax.ShapeDtypeStruct((mloc, h, n), jnp.bfloat16),
        input_output_aliases={} if gh is None else {2: 0},
        compiler_params=pltpu.CompilerParams(vmem_limit_bytes=VMEM),
        cost_estimate=pl.CostEstimate(
            flops=2 * h * h, bytes_accessed=2 * h * h, transcendentals=0
        ),
        name="grad_hidden_part",
    )(*args)


def after(value, *others):
    return lax.optimization_barrier((value,) + others)[0]


def shards(hidden, target, area, var_weight, w_inner, b_inner, w_out, b_out):
    mloc, h, n = hidden.shape
    n_mem = lax.axis_size("mem")
    n_grid = lax.axis_size("grid")
    members = mloc * n_mem
    npoints = n * n_grid
    v = w_out.shape[0]
    vp = 128
    n_lo = 2
    while n_lo * n_lo * 4 <= n_grid:
        n_lo *= 2
    n_hi = n_grid // n_lo

    swap_x = [(i, (i + n_mem // 2) % n_mem) for i in range(n_mem)]
    swap_core = [(i, i ^ 1) for i in range(n_mem)]

    def shift_lo(k):
        return [(a * n_lo + b, a * n_lo + (b + k) % n_lo) for a in range(n_hi) for b in range(n_lo)]

    def shift_hi(k):
        return [(a * n_lo + b, (a + k) % n_hi * n_lo + b) for a in range(n_hi) for b in range(n_lo)]

    to_x = lambda a: lax.ppermute(a, "mem", swap_x)
    to_core = lambda a: lax.ppermute(a, "mem", swap_core)
    to_lo = lambda a, k: lax.ppermute(a, "grid", shift_lo(k))
    to_hi = lambda a, k: lax.ppermute(a, "grid", shift_hi(k))

    mem, grid = lax.axis_index("mem"), lax.axis_index("grid")
    at_zero = {("mem", bit): mem & bit == 0 for bit in (1, n_mem // 2)}
    bit = 1
    while bit < n_lo:
        at_zero["grid", bit] = grid & bit == 0
        bit *= 2
    hidden, at_zero = lax.optimization_barrier((hidden, at_zero))
    hidden, w_out, b_inner, b_out = (
        pltpu.with_memory_space_constraint(a, pltpu.HBM)
        for a in (hidden, w_out, b_inner.reshape(1, h), b_out.reshape(1, v))
    )
    unit = n // sum(EIGHTHS)
    starts = [unit * sum(EIGHTHS[:k]) for k in range(len(EIGHTHS))]
    spans = [(start, unit * size) for start, size in zip(starts, EIGHTHS)]
    parts, far, made = [], [], []
    for start, p in spans:
        w, vmem = w_inner, VMEM
        if len(parts) == 2:
            wt, wot = transposes(after(w_inner, parts[1][2]), w_out, vp)
            b_out = after(b_out, wt)
        if parts:
            b_out = after(b_out, parts[-1][2])
        else:
            w = pltpu.with_memory_space_constraint(w_inner, pltpu.HBM)
            vmem += 4 * h * h
        spread = made or (b_inner, w_out)
        *part, = forward(start, p, hidden, w, *spread, b_out, vmem, not parts)
        made = made or part[3:]
        parts.append(part[:3])
        far.append(to_x(parts[-1][2]))
    near = [to_core(fields) for _, _, fields in parts]
    vw, area = var_weight.reshape(1, v), area.reshape(1, n)
    acc = extra = gh = None
    grad_pre = []
    for k, (start, p) in enumerate(spans):
        act, slope, fields = parts[k]
        first, last = k == 0, k == len(spans) - 1
        if k:
            far[k] = after(far[k], parts[-1][2] if k == 1 else grad_pre[k - 2])
        gp, extra, acc, *accs = backward(
            start, p, first, last, (n_hi, n_lo), members,
            (fields, near[k], far[k], to_core(far[k])),
            (target, area, vw, act, slope, hidden, wot), acc, extra,
        )
        grad_pre.append(gp)
    keep_x, send_x, keep_y, send_y = accs

    def gathered(block, axis, name, bit):
        n = lax.axis_size(name)
        other = lax.ppermute(block, name, [(i, i ^ bit) for i in range(n)])
        return ordered(block, other, axis, name, bit)

    def ordered(block, other, axis, name, bit):
        return jnp.where(
            at_zero[name, bit],
            jnp.concatenate([block, other], axis),
            jnp.concatenate([other, block], axis),
        )

    def beside(k, gh, start_after, wait_for):
        gh = input_gradient(*spans[k], n, wt, after(grad_pre[k], start_after), gh)
        return lax.optimization_barrier((gh, wait_for))

    r, cx = h // (2 * n_grid), keep_x.shape[-1]
    others = range(1, n_lo)
    got_x = to_core(send_x)
    got_y = to_core(send_y)
    out_x = keep_x[1] + got_x[1]
    out_y = [keep_y[k] + got_y[k] for k in others]
    from_x = to_x(out_x)
    from_y = [to_lo(out_y[k - 1], k) for k in others]
    for k in (0, 1):
        gh, (keep_x, keep_y) = beside(k, gh, (out_x, out_y), (keep_x, keep_y))
    own_x = keep_x[0] + got_x[0] + from_x
    own_y = sum(from_y, keep_y[0] + got_y[0])
    own_x, own_y = [own_x[k] for k in range(n_lo)], [own_y[k] for k in range(2)]
    from_y = [to_lo(own_x[k], k) for k in others]
    from_x = to_x(own_y[1])
    gh, (own_x, own_y) = beside(2, gh, (own_x[1:], own_y[1]), (own_x[0], own_y[0]))
    sums = [sum(from_y, own_x), own_y + from_x]

    extra = [part[:, r:].reshape(-1, cx) for part in sums]
    pieces = [jnp.concatenate([part[k, :r] for part in sums] + extra, 0) for k in range(n_hi)]
    from_hi = [to_hi(pieces[k], k) for k in range(1, n_hi)]
    gh, own = beside(3, gh, pieces[1:], pieces[0])
    total = sum(from_hi, own)
    far = to_x(total)
    mine = total[2 * r :][None]
    beyond = lax.ppermute(mine, "grid", [(g, g ^ 1) for g in range(n_grid)])
    pairs = [(m * n_grid + g, (m + n_mem // 2) % n_mem * n_grid + (g ^ 1)) for m in range(n_mem) for g in range(n_grid)]
    across = lax.ppermute(mine, ("mem", "grid"), pairs)

    scale = 1.0 / math.sqrt(members * npoints)
    halves = [ordered(total[k : k + r], far[k : k + r], 1, "mem", n_mem // 2) for k in (0, r)]
    own = jnp.concatenate(halves, 1)
    other = to_core(own)

    sides = [ordered(mine, far[2 * r :][None], 0, "mem", n_mem // 2)]
    sides.append(ordered(beyond, across, 0, "mem", n_mem // 2))
    extra = ordered(*(side[None] for side in sides), 0, "grid", 1)
    bit = 2
    while bit < n_lo:
        extra = gathered(extra, 0, "grid", bit)
        bit *= 2
    extra = extra.reshape(n_lo, 2, 2, n_hi, EXTRA_ROWS, cx)
    grad_inner, grad_out, loss = finished(
        (n_hi, n_lo), scale, npoints, v, own, other, extra, to_core(extra)
    )
    return (loss.reshape(()), gh, grad_inner, grad_out)


def solution(mesh):
    in_specs = (P("mem", None, "grid"), P(None, "grid"), P("grid"), P(), P(), P(), P(), P())
    out_specs = (P(), P("mem", None, "grid"), P("grid", None), P())
    return jax.shard_map(shards, mesh=mesh, in_specs=in_specs, out_specs=out_specs, check_vma=False)
```
